32 devices in a mesh: wide: 8 (over y, x, core), narrow: 4 (over z).
Axes of the slice: x: 2, y: 2, z: 4, core: 2. Of those that a mesh axis runs over, the one named last changes fastest.
Arguments:
- prior_states: bfloat16 [8, 2, 83, 8192], P('wide', None, None, 'narrow'), may hold values from -6 to 6
- target: bfloat16 [8, 83, 8192], P('wide', None, 'narrow'), may hold values from -6 to 6
- noise_draw: bfloat16 [8, 83, 8192], P('wide', None, 'narrow'), may hold values from -6 to 6
- level_index: int32 [8], P('wide'), may hold values from 0 to 7
- g2m_edges: int32 [8, 4096, 4], P('wide', 'narrow'), may hold values from 0 to 8191
- neighbours: int32 [8, 4096, 32], P('wide', 'narrow'), may hold values from 0 to 4095
- m2g_edges: int32 [8, 8192, 3], P('wide', 'narrow'), may hold values from 0 to 4095
- valid_mask: int32 [8, 8192], P('wide', 'narrow'), may hold values from 0 to 1, as said below
- channel_weights: float32 [83], replicated, may hold values from 0.25 to 2
- w_embed: float32 [249, 512], replicated, may hold values from -0.375 to 0.375
- w_cond: float32 [32, 2048], replicated, may hold values from -0.75 to 0.75
- w_attn: float32 [512, 2048], P(None, 'narrow'), may hold values from -0.375 to 0.375
- w_up: float32 [512, 2048], P(None, 'narrow'), may hold values from -0.25 to 0.25
- w_down: float32 [2048, 512], P('narrow'), may hold values from -0.125 to 0.125
- w_dec: float32 [512, 83], replicated, may hold values from -0.25 to 0.25
- biases: float32 [2643], replicated, may hold values from -0.75 to 0.75
- mom_attn: float32 [512, 2048], P(None, 'narrow'), may hold values from -0.00015258789 to 0.00015258789
- mom_up: float32 [512, 2048], P(None, 'narrow'), may hold values from -0.00015258789 to 0.00015258789
- mom_down: float32 [2048, 512], P('narrow'), may hold values from -0.00015258789 to 0.00015258789
- m_embed: float32 [249, 512], replicated, may hold values from -1.9073486e-05 to 1.9073486e-05
- v_embed: float32 [249, 512], replicated, may hold values from 5.910356e-12 to 4.7282848e-11
- m_cond: float32 [32, 2048], replicated, may hold values from -1.9073486e-05 to 1.9073486e-05
- v_cond: float32 [32, 2048], replicated, may hold values from 5.910356e-12 to 4.7282848e-11
- m_dec: float32 [512, 83], replicated, may hold values from -1.9073486e-05 to 1.9073486e-05
- v_dec: float32 [512, 83], replicated, may hold values from 5.910356e-12 to 4.7282848e-11
- m_bias: float32 [2643], replicated, may hold values from -5.340576e-05 to 5.340576e-05
- v_bias: float32 [2643], replicated, may hold values from 5.9103555e-11 to 4.7282844e-10
- ema_embed: float32 [249, 512], replicated, may hold values from -0.375 to 0.375
- ema_cond: float32 [32, 2048], replicated, may hold values from -0.75 to 0.75
- ema_attn: float32 [512, 2048], P(None, 'narrow'), may hold values from -0.375 to 0.375
- ema_up: float32 [512, 2048], P(None, 'narrow'), may hold values from -0.25 to 0.25
- ema_down: float32 [2048, 512], P('narrow'), may hold values from -0.125 to 0.125
- ema_dec: float32 [512, 83], replicated, may hold values from -0.25 to 0.25
- ema_bias: float32 [2643], replicated, may hold values from -0.75 to 0.75
Outputs:
- new_attn: float32 [512, 2048], P(None, 'narrow')
- new_up: float32 [512, 2048], P(None, 'narrow')
- new_down: float32 [2048, 512], P('narrow')
- moment_attn: float32 [512, 2048], P(None, 'narrow')
- moment_up: float32 [512, 2048], P(None, 'narrow')
- moment_down: float32 [2048, 512], P('narrow')
- new_embed: float32 [249, 512], replicated
- new_cond: float32 [32, 2048], replicated
- new_dec: float32 [512, 83], replicated
- new_bias: float32 [2643], replicated
- first_embed: float32 [249, 512], replicated
- second_embed: float32 [249, 512], replicated
- first_cond: float32 [32, 2048], replicated
- second_cond: float32 [32, 2048], replicated
- first_dec: float32 [512, 83], replicated
- second_dec: float32 [512, 83], replicated
- first_bias: float32 [2643], replicated
- second_bias: float32 [2643], replicated
- average_embed: float32 [249, 512], replicated
- average_cond: float32 [32, 2048], replicated
- average_attn: float32 [512, 2048], P(None, 'narrow')
- average_up: float32 [512, 2048], P(None, 'narrow')
- average_down: float32 [2048, 512], P('narrow')
- average_dec: float32 [512, 83], replicated
- average_bias: float32 [2643], replicated
- loss_sum: float32 [], replicated
- weight_total: float32 [], replicated
- grad_norm: float32 [], replicated
The draws below stay inside these ranges and needn't reach their ends.
Inputs may be any that keep to these rules, and one draw needn't show every extreme that they name: `g2m_edges`: pixel numbers within the date. `neighbours`: node numbers within the date. `m2g_edges`: node numbers within the date. `valid_mask`: 1 where a pixel counts in the loss.
All inputs are finite; a program needn't handle non-finite values.
Results may differ from the reference program's by a relative error of at most 0.0062.
Values may be sent and summed in bfloat16 or wider, within the bound.
No kernel may reach another device: no remote copies, remote signals or barrier semaphores. Data moves between devices by JAX's collectives and lax.ppermute only.
A program may use at most 384 MiB of HBM per device.

```python
import math
import jax
import jax.numpy as jnp
from jax import lax

LATENT_WIDTH = 512
HEADS = 4
HEAD_WIDTH = 128
FF = 2048
C = 83
COND = 32
NBR = 32
G2M_K = 4
M2G_K = 3
NS_ITERS = 5
SIGMA_LEVELS = 8
STEP_NUMBER = 10
PIXELS = 8192
NODES = 4096
DATES = 8
NPARAM = 3383891


def draw_valid_mask(key, part):
    key = jax.random.fold_in(key, 11)
    date_rows = lax.broadcasted_iota(jnp.int32, (DATES, PIXELS), 0)
    pixel_cols = lax.broadcasted_iota(jnp.int32, (DATES, PIXELS), 1)
    chance = 300 + 350 * date_rows // max(DATES - 1, 1) + 350 * pixel_cols // max(PIXELS - 1, 1)
    draw_ranks = jax.random.randint(key, (DATES, PIXELS), 0, 1000)
    return (draw_ranks < chance).astype(jnp.int32)


def touch_ends(result, own_key, least, high):
    longest = result.shape.index(max(result.shape))
    spots = []
    for shift in (0, 1):
        where = [jax.random.randint(jax.random.fold_in(own_key, axis), (), 0, length) for axis, length in enumerate(result.shape)]
        where[longest] = (where[longest] + shift) % result.shape[longest]
        spots.append(tuple(where))
    return result.at[spots[0]].set(least).at[spots[1]].set(high)


def block_scale(stream_key, dims, pieces, low, top_value):
    def one(dim, shards_of):
        heights = jax.random.uniform(jax.random.fold_in(jax.random.fold_in(stream_key, 6), dim), (shards_of,), jnp.float32, low / len(pieces), top_value / len(pieces))
        return jnp.repeat(jnp.exp(heights), dims[dim] // shards_of).reshape((-1,) + (1,) * (len(dims) - dim - 1))

    loudness = one(*pieces[0])
    for cut in pieces[1:]:
        loudness = loudness * one(*cut)
    return loudness


def bell_draw(key, shape, spread, most, split=(), held_as=jnp.bfloat16):
    values = jax.random.normal(key, shape, jnp.float32) * spread
    if len(split) > 0:
        values = block_scale(key, shape, split, -0.22, 0.18) * values
    return jnp.clip(values, min=-most, max=most).astype(held_as)


def setup_inputs(seed: int = 0) -> dict:
    key_of = jax.random.split(jax.random.key(seed), 35)
    prior_states = bell_draw(key_of[0], (DATES, 2, C, PIXELS), 1.0, 6.0, ((0, 8), (3, 4)))
    target = bell_draw(key_of[1], (DATES, C, PIXELS), 1.0, 6.0, ((0, 8), (2, 4)))
    noise_draw = bell_draw(key_of[2], (DATES, C, PIXELS), 1.0, 6.0, ((0, 8), (2, 4)))
    level_index = touch_ends(jax.random.randint(key_of[3], (DATES,), 0, SIGMA_LEVELS), jax.random.fold_in(key_of[3], 1), 0, SIGMA_LEVELS - 1).astype(jnp.int32)
    g2m_edges = touch_ends(jax.random.randint(key_of[4], (DATES, NODES, G2M_K), 0, PIXELS), jax.random.fold_in(key_of[4], 1), 0, PIXELS - 1).astype(jnp.int32)
    neighbours = touch_ends(jax.random.randint(key_of[5], (DATES, NODES, NBR), 0, NODES), jax.random.fold_in(key_of[5], 1), 0, NODES - 1).astype(jnp.int32)
    m2g_edges = touch_ends(jax.random.randint(key_of[6], (DATES, PIXELS, M2G_K), 0, NODES), jax.random.fold_in(key_of[6], 1), 0, NODES - 1).astype(jnp.int32)
    valid_mask = draw_valid_mask(jax.random.fold_in(key_of[34], 71), 0)
    channel_weights = jnp.clip(jnp.exp(jax.random.uniform(key_of[8], (C,), jnp.float32, math.log(0.25), math.log(2.0))), 0.25, 2.0)
    w_embed = bell_draw(key_of[9], (3 * C, LATENT_WIDTH), (3 * C) ** -0.5, 0.375, (), jnp.float32)
    w_cond = bell_draw(key_of[10], (COND, 4 * LATENT_WIDTH), (0.3 * COND ** -0.5), 0.75, (), jnp.float32)
    w_attn = bell_draw(key_of[11], (LATENT_WIDTH, 4 * LATENT_WIDTH), (LATENT_WIDTH // 2) ** -0.5, 0.375, ((1, 4),), jnp.float32)
    w_up = bell_draw(key_of[12], (LATENT_WIDTH, FF), LATENT_WIDTH ** -0.5, 0.25, ((1, 4),), jnp.float32)
    w_down = bell_draw(key_of[13], (FF, LATENT_WIDTH), FF ** -0.5, 0.125, ((0, 4),), jnp.float32)
    w_dec = bell_draw(key_of[14], (LATENT_WIDTH, C), LATENT_WIDTH ** -0.5, 0.25, (), jnp.float32)
    biases = bell_draw(key_of[15], (LATENT_WIDTH + FF + C,), 0.05, 0.75, (), jnp.float32)
    mom_attn = bell_draw(key_of[16], (LATENT_WIDTH, 4 * LATENT_WIDTH), (0.02 * NPARAM ** -0.5), 0.00015258789, ((1, 4),), jnp.float32)
    mom_up = bell_draw(key_of[17], (LATENT_WIDTH, FF), (0.02 * NPARAM ** -0.5), 0.00015258789, ((1, 4),), jnp.float32)
    mom_down = bell_draw(key_of[18], (FF, LATENT_WIDTH), (0.02 * NPARAM ** -0.5), 0.00015258789, ((0, 4),), jnp.float32)
    m_embed = bell_draw(key_of[19], (3 * C, LATENT_WIDTH), (0.0022 * NPARAM ** -0.5), 1.9073486328125e-05, (), jnp.float32)
    v_embed = jnp.clip(jnp.exp(jax.random.uniform(key_of[20], (3 * C, LATENT_WIDTH), jnp.float32, math.log(5.910355971999737e-12), math.log(4.7282847775997894e-11))), 5.910355971999737e-12, 4.7282847775997894e-11)
    m_cond = bell_draw(key_of[21], (COND, 4 * LATENT_WIDTH), (0.0022 * NPARAM ** -0.5), 1.9073486328125e-05, (), jnp.float32)
    v_cond = jnp.clip(jnp.exp(jax.random.uniform(key_of[22], (COND, 4 * LATENT_WIDTH), jnp.float32, math.log(5.910355971999737e-12), math.log(4.7282847775997894e-11))), 5.910355971999737e-12, 4.7282847775997894e-11)
    m_dec = bell_draw(key_of[23], (LATENT_WIDTH, C), (0.0022 * NPARAM ** -0.5), 1.9073486328125e-05, (), jnp.float32)
    v_dec = jnp.clip(jnp.exp(jax.random.uniform(key_of[24], (LATENT_WIDTH, C), jnp.float32, math.log(5.910355971999737e-12), math.log(4.7282847775997894e-11))), 5.910355971999737e-12, 4.7282847775997894e-11)
    m_bias = bell_draw(key_of[25], (LATENT_WIDTH + FF + C,), (0.007 * NPARAM ** -0.5), 5.340576171875e-05, (), jnp.float32)
    v_bias = jnp.clip(jnp.exp(jax.random.uniform(key_of[26], (LATENT_WIDTH + FF + C,), jnp.float32, math.log(5.910355538318868e-11), math.log(4.728284430655094e-10))), 5.910355538318868e-11, 4.728284430655094e-10)
    ema_embed = bell_draw(key_of[27], (3 * C, LATENT_WIDTH), (3 * C) ** -0.5, 0.375, (), jnp.float32)
    ema_cond = bell_draw(key_of[28], (COND, 4 * LATENT_WIDTH), (0.3 * COND ** -0.5), 0.75, (), jnp.float32)
    ema_attn = bell_draw(key_of[29], (LATENT_WIDTH, 4 * LATENT_WIDTH), (LATENT_WIDTH // 2) ** -0.5, 0.375, ((1, 4),), jnp.float32)
    ema_up = bell_draw(key_of[30], (LATENT_WIDTH, FF), LATENT_WIDTH ** -0.5, 0.25, ((1, 4),), jnp.float32)
    ema_down = bell_draw(key_of[31], (FF, LATENT_WIDTH), FF ** -0.5, 0.125, ((0, 4),), jnp.float32)
    ema_dec = bell_draw(key_of[32], (LATENT_WIDTH, C), LATENT_WIDTH ** -0.5, 0.25, (), jnp.float32)
    ema_bias = bell_draw(key_of[33], (LATENT_WIDTH + FF + C,), 0.05, 0.75, (), jnp.float32)
    return {"prior_states": prior_states, "target": target, "noise_draw": noise_draw, "level_index": level_index, "g2m_edges": g2m_edges, "neighbours": neighbours, "m2g_edges": m2g_edges, "valid_mask": valid_mask, "channel_weights": channel_weights, "w_embed": w_embed, "w_cond": w_cond, "w_attn": w_attn, "w_up": w_up, "w_down": w_down, "w_dec": w_dec, "biases": biases, "mom_attn": mom_attn, "mom_up": mom_up, "mom_down": mom_down, "m_embed": m_embed, "v_embed": v_embed, "m_cond": m_cond, "v_cond": v_cond, "m_dec": m_dec, "v_dec": v_dec, "m_bias": m_bias, "v_bias": v_bias, "ema_embed": ema_embed, "ema_cond": ema_cond, "ema_attn": ema_attn, "ema_up": ema_up, "ema_down": ema_down, "ema_dec": ema_dec, "ema_bias": ema_bias}


@jax.custom_vjp
def low(v):
    return lax.optimization_barrier(v.astype(jnp.bfloat16)).astype(jnp.float32)

@jax.custom_vjp
def lowered_backward(v):
    return v

def low_keep(v):
    return (low(v), None)

def low_pass(kept, grad):
    return (grad,)

def back_keep(v):
    return (v, None)

def back_low(kept, grad):
    return (low(grad),)
low.defvjp(low_keep, low_pass)
lowered_backward.defvjp(back_keep, back_low)
highest_precision = lax.Precision.HIGHEST
sigma_low = 0.25
sigma_high = 4.0
clip_bound = 0.02
muon_rate = 0.5
muon_decay = 0.95
adam_rate = 0.03
beta_one = 0.9
beta_two = 0.95
adam_eps = 1e-08
decay_rate = 0.01
ema_keep = 0.9
coef_a = 3.4445
coef_b = -4.775
coef_c = 2.0315

def sigma_terms(level):
    fraction = level.astype(jnp.float32) / (SIGMA_LEVELS - 1)
    noise_level = sigma_low * (sigma_high / sigma_low) ** fraction
    square = noise_level * noise_level + 1.0
    scale_in = lax.rsqrt(square)
    return (noise_level, scale_in, 1.0 / square, noise_level * scale_in, square / (noise_level * noise_level))

def cond_features(noise_level):
    frequencies = 1.0 + jnp.arange(COND // 2).astype(jnp.float32)
    phases = jnp.log(noise_level) * frequencies
    return jnp.concatenate([jnp.sin(phases), jnp.cos(phases)])

def lat_weights(first_row, row_count, pixel_total):
    row_ids = (first_row + jnp.arange(row_count)).astype(jnp.float32)
    return jnp.cos(math.pi * ((row_ids + 0.5) / pixel_total - 0.5))

def layer_norm(values):
    centred = values - lax.optimization_barrier(jnp.mean(values, axis=-1, keepdims=True))
    return centred * lax.rsqrt(lax.optimization_barrier(jnp.mean(centred * centred, axis=-1, keepdims=True)) + 1e-05)

def forward(weights, date_data, channel_weights, lat_weight):
    w_embed, w_cond, w_attn, w_up, w_down, w_dec, biases = weights
    bias_embed = biases[:LATENT_WIDTH]
    bias_up = biases[LATENT_WIDTH:LATENT_WIDTH + FF]
    bias_out = biases[LATENT_WIDTH + FF:]

    def one_date(date_item):
        prior_pair, target, noise_draw, level, g2m_rows, near_ids, m2g_rows, valid_rows = date_item
        noise_level, scale_in, skip_scale, out_scale, loss_scale = sigma_terms(level)
        noisy = target + noise_level * noise_draw
        features = jnp.concatenate([prior_pair[0], prior_pair[1], low(scale_in * noisy)], axis=0)
        embed_pre = lowered_backward(lax.dot_general(features, w_embed, (((0,), (0,)), ((), ())), precision=highest_precision) + bias_embed)
        embedded = low(jax.nn.silu(embed_pre))
        node_in = lax.optimization_barrier(jnp.mean(embedded[g2m_rows], axis=1))
        modulation = jnp.dot(cond_features(noise_level), w_cond, precision=highest_precision)
        attn_in = layer_norm(node_in) * (1.0 + modulation[:LATENT_WIDTH]) + modulation[LATENT_WIDTH:2 * LATENT_WIDTH]
        qkv_rows = low(lowered_backward(jnp.dot(low(attn_in), w_attn[:, :3 * LATENT_WIDTH], precision=highest_precision)))
        mesh_node_count = qkv_rows.shape[0]
        query_rows = qkv_rows[:, :LATENT_WIDTH].reshape(mesh_node_count, HEADS, HEAD_WIDTH)
        neighbour_key_rows = qkv_rows[:, LATENT_WIDTH:2 * LATENT_WIDTH][near_ids].reshape(mesh_node_count, NBR, HEADS, HEAD_WIDTH)
        neighbour_value_rows = qkv_rows[:, 2 * LATENT_WIDTH:][near_ids].reshape(mesh_node_count, NBR, HEADS, HEAD_WIDTH)
        attention_scores = lowered_backward(jnp.einsum('tzp,tvzp->tzv', query_rows, neighbour_key_rows, precision=highest_precision) / math.sqrt(HEAD_WIDTH))
        softmax_weights = low(jax.nn.softmax(attention_scores, axis=-1))
        attended_rows = jnp.einsum('ika,iakv->ikv', softmax_weights, neighbour_value_rows, precision=highest_precision).reshape(mesh_node_count, LATENT_WIDTH)
        attended_rows = low(lowered_backward(attended_rows))
        node_mid = node_in + lowered_backward(jnp.dot(attended_rows, w_attn[:, 3 * LATENT_WIDTH:], precision=highest_precision))
        mlp_in = layer_norm(node_mid) * (1.0 + modulation[2 * LATENT_WIDTH:3 * LATENT_WIDTH]) + modulation[3 * LATENT_WIDTH:]
        up_pre = lowered_backward(jnp.dot(low(mlp_in), w_up, precision=highest_precision) + bias_up)
        node_out = node_mid + lowered_backward(jnp.dot(low(jax.nn.silu(up_pre)), w_down, precision=highest_precision))
        decoded = low(lax.optimization_barrier(jnp.mean(low(node_out)[m2g_rows], axis=1)))
        raw_output = lax.dot_general(w_dec, decoded, (((0,), (1,)), ((), ())), precision=highest_precision)
        raw_output = lowered_backward(raw_output + bias_out[:, None])
        errors = skip_scale * noisy + out_scale * raw_output - target
        weighted = channel_weights[:, None] * (lat_weight * valid_rows)[None, :]
        return loss_scale * jnp.sum(weighted * errors * errors)
    return jnp.sum(lax.map(jax.checkpoint(one_date), date_data))

def orthogonalize(weight_matrix):
    gram_product = jnp.dot(weight_matrix, weight_matrix.T, precision=highest_precision)
    scale_factor = 1.0 / (jnp.sqrt(jnp.trace(gram_product)) + 1e-07)
    weight_matrix = weight_matrix * scale_factor
    gram_product = gram_product * (scale_factor * scale_factor)
    for iteration in range(NS_ITERS):
        if iteration > 0:
            gram_product = jnp.dot(weight_matrix, weight_matrix.T, precision=highest_precision)
        polynomial = coef_b * gram_product + coef_c * jnp.dot(gram_product, gram_product, precision=highest_precision)
        weight_matrix = coef_a * weight_matrix + jnp.dot(polynomial, weight_matrix, precision=highest_precision)
    return weight_matrix

def muon_update(weight, momentum, grad, is_tall):
    momentum_new = muon_decay * momentum + grad
    ratio = math.sqrt(max(1.0, weight.shape[0] / weight.shape[1]))
    if is_tall:
        direction = orthogonalize(momentum_new.T).T
    else:
        direction = orthogonalize(momentum_new)
    return (weight - muon_rate * ratio * direction, momentum_new)

def adam_update(weight, grad, first, second):
    first_new = beta_one * first + (1.0 - beta_one) * grad
    second_new = beta_two * second + (1.0 - beta_two) * grad * grad
    first_hat = first_new / (1.0 - beta_one ** STEP_NUMBER)
    second_hat = second_new / (1.0 - beta_two ** STEP_NUMBER)
    weight_new = weight - adam_rate * (first_hat / (jnp.sqrt(second_hat) + adam_eps) + decay_rate * weight)
    return (weight_new, first_new, second_new)

def reference(prior_states, target, noise_draw, level_index, g2m_edges, neighbours, m2g_edges, valid_mask, channel_weights, w_embed, w_cond, w_attn, w_up, w_down, w_dec, biases, mom_attn, mom_up, mom_down, m_embed, v_embed, m_cond, v_cond, m_dec, v_dec, m_bias, v_bias, ema_embed, ema_cond, ema_attn, ema_up, ema_down, ema_dec, ema_bias):
    valid_float = valid_mask.astype(jnp.float32)
    date_data = (prior_states.astype(jnp.float32), target.astype(jnp.float32), noise_draw.astype(jnp.float32), level_index, g2m_edges, neighbours, m2g_edges, valid_float)
    lat_weight = lat_weights(0, PIXELS, PIXELS)
    weight_total = jnp.sum(lat_weight[None, :] * valid_float)
    weights = (w_embed, w_cond, w_attn, w_up, w_down, w_dec, biases)

    def objective(params):
        p_embed, p_cond, p_attn, p_up, p_down, p_dec, p_bias = params
        rounded = (low(p_embed), p_cond, low(p_attn), low(p_up), low(p_down), low(p_dec), p_bias)
        loss_total = forward(rounded, date_data, channel_weights, lat_weight)
        return (loss_total / weight_total, loss_total)
    loss_value, pullback, loss_sum = jax.vjp(objective, weights, has_aux=True)
    gradients, = pullback(jnp.ones_like(loss_value))
    square_sum = jnp.sum(jnp.stack([jnp.sum(grad * grad) for grad in gradients]))
    grad_norm = jnp.sqrt(square_sum)
    factor = jnp.minimum(1.0, clip_bound / (grad_norm + 1e-06))
    g_embed, g_cond, g_attn, g_up, g_down, g_dec, g_bias = [grad * factor for grad in gradients]
    new_attn, moment_attn = muon_update(w_attn, mom_attn, g_attn, False)
    new_up, moment_up = muon_update(w_up, mom_up, g_up, False)
    new_down, moment_down = muon_update(w_down, mom_down, g_down, True)
    new_embed, first_embed, second_embed = adam_update(w_embed, g_embed, m_embed, v_embed)
    new_cond, first_cond, second_cond = adam_update(w_cond, g_cond, m_cond, v_cond)
    new_dec, first_dec, second_dec = adam_update(w_dec, g_dec, m_dec, v_dec)
    new_bias, first_bias, second_bias = adam_update(biases, g_bias, m_bias, v_bias)
    keep_rest = 1.0 - ema_keep
    return (new_attn, new_up, new_down, moment_attn, moment_up, moment_down, new_embed, new_cond, new_dec, new_bias, first_embed, second_embed, first_cond, second_cond, first_dec, second_dec, first_bias, second_bias, ema_keep * ema_embed + keep_rest * new_embed, ema_keep * ema_cond + keep_rest * new_cond, ema_keep * ema_attn + keep_rest * new_attn, ema_keep * ema_up + keep_rest * new_up, ema_keep * ema_down + keep_rest * new_down, ema_keep * ema_dec + keep_rest * new_dec, ema_keep * ema_bias + keep_rest * new_bias, loss_sum, weight_total, grad_norm)
```

```python
import math

import jax
import jax.numpy as jnp
from jax import lax
from jax.sharding import PartitionSpec as P

LATENT_WIDTH = 512
HEADS = 4
HEAD_WIDTH = 128
FF = 2048
COND = 32
NBR = 32
G2M_K = 4
M2G_K = 3
NS_ITERS = 5
SIGMA_LEVELS = 8
STEP_NUMBER = 10


highest_precision = lax.Precision.HIGHEST
sigma_low = 0.25
sigma_high = 4.0
clip_bound = 0.02
muon_rate = 0.5
muon_decay = 0.95
adam_rate = 0.03
beta_one = 0.9
beta_two = 0.95
adam_eps = 1e-08
decay_rate = 0.01
ema_keep = 0.9
coef_a = 3.4445
coef_b = -4.775
coef_c = 2.0315


def sigma_terms(level):
    fraction = level.astype(jnp.float32) / (SIGMA_LEVELS - 1)
    noise_level = sigma_low * (sigma_high / sigma_low) ** fraction
    square = noise_level * noise_level + 1.0
    scale_in = lax.rsqrt(square)
    return (
        noise_level,
        scale_in,
        1.0 / square,
        noise_level * scale_in,
        square / (noise_level * noise_level),
    )


def cond_features(noise_level):
    frequencies = 1.0 + jnp.arange(COND // 2).astype(jnp.float32)
    phases = jnp.log(noise_level) * frequencies
    return jnp.concatenate([jnp.sin(phases), jnp.cos(phases)])


def lat_weights(first_row, row_count, pixel_total):
    row_ids = (first_row + jnp.arange(row_count, dtype=jnp.int32)).astype(jnp.float32)
    return jnp.cos(math.pi * ((row_ids + 0.5) / pixel_total - 0.5))


def norm_stats(values):
    centred = values - jnp.mean(values, axis=-1, keepdims=True)
    inverse = lax.rsqrt(jnp.mean(centred * centred, axis=-1, keepdims=True) + 1e-05)
    return (centred * inverse, inverse)


def norm_back(grad_normed, normed, inverse):
    first_mean = jnp.mean(grad_normed, axis=-1, keepdims=True)
    second_mean = jnp.mean(grad_normed * normed, axis=-1, keepdims=True)
    return inverse * (grad_normed - first_mean - normed * second_mean)


def silu_slope(values):
    sigmoid_values = jax.nn.sigmoid(values)
    return sigmoid_values * (1.0 + values * (1.0 - sigmoid_values))


def contract_rows(left, right):
    return lax.dot_general(
        left, right, (((0,), (0,)), ((), ())), preferred_element_type=jnp.float32
    )


def contract_last(left, right):
    return lax.dot_general(
        left, right, (((1,), (1,)), ((), ())), preferred_element_type=jnp.float32
    )


def bit_swap(values, axis_name, bit):
    size = lax.axis_size(axis_name)
    return lax.ppermute(values, axis_name, [(i, i ^ (1 << bit)) for i in range(size)])


def axis_bits(axis_name):
    bits = []
    reach = 1
    while reach < lax.axis_size(axis_name):
        bits.append((axis_name, len(bits)))
        reach *= 2
    return bits


def small_sum(values):
    for axis_name, bit in axis_bits("wide") + axis_bits("narrow"):
        values = values + bit_swap(values, axis_name, bit)
    return values


def large_sum(values, sent_type):
    steps = axis_bits("wide") + axis_bits("narrow")
    for axis_name, bit in steps:
        half = values.shape[0] // 2
        mine = (lax.axis_index(axis_name) >> bit) & 1
        kept = lax.dynamic_slice_in_dim(values, mine * half, half, 0)
        sent = lax.dynamic_slice_in_dim(values, (1 - mine) * half, half, 0)
        values = kept + bit_swap(sent.astype(sent_type), axis_name, bit).astype(jnp.float32)
    values = values.astype(sent_type)
    for axis_name, bit in steps[::-1]:
        mine = (lax.axis_index(axis_name) >> bit) & 1
        other = bit_swap(values, axis_name, bit)
        is_high = mine == 1
        values = jnp.concatenate(
            [jnp.where(is_high, other, values), jnp.where(is_high, values, other)], axis=0
        )
    return values.astype(jnp.float32)


def ring_slots(values):
    size = lax.axis_size("narrow")
    slots = [values]
    for shift in range(1, size):
        slots.append(
            lax.ppermute(values, "narrow", [((i + shift) % size, i) for i in range(size)])
        )
    return slots


def line_slots(values):
    size = lax.axis_size("narrow")
    pos = lax.axis_index("narrow")
    up = [(i, i + 1) for i in range(size - 1)]
    down = [(i + 1, i) for i in range(size - 1)]
    from_low, from_high = values, values
    low_list, high_list = [], []
    for _ in range(size - 1):
        from_low = lax.ppermute(from_low, "narrow", up)
        from_high = lax.ppermute(from_high, "narrow", down)
        low_list.append(from_low)
        high_list.append(from_high)
    slots = [values]
    for shift in range(1, size):
        slots.append(
            jnp.where(pos + shift < size, high_list[shift - 1], low_list[size - shift - 1])
        )
    return slots


def ring_sum(parts):
    size = lax.axis_size("narrow")
    total = parts[0]
    for shift in range(1, size):
        arrived = lax.ppermute(
            parts[shift].astype(jnp.bfloat16),
            "narrow",
            [(i, (i + shift) % size) for i in range(size)],
        )
        total = total + arrived.astype(jnp.float32)
    return total


def count_matrix(index_rows, first, column_count):
    columns = first + jnp.arange(column_count, dtype=jnp.int32)[None, :]
    total = jnp.zeros((index_rows.shape[0], column_count), jnp.float32)
    for slot in range(index_rows.shape[1]):
        total = total + (index_rows[:, slot : slot + 1] == columns).astype(jnp.float32)
    return total.astype(jnp.bfloat16)


def wide_gather(block, axis):
    rows = block.shape[0] // lax.axis_size("wide")
    own = lax.dynamic_slice_in_dim(block, lax.axis_index("wide") * rows, rows, 0)
    if axis == 1:
        across = lax.all_gather(own, "narrow", axis=1, tiled=True)
        return lax.all_gather(across, "wide", axis=0, tiled=True)
    across = lax.all_gather(own, "narrow", axis=0)
    whole = lax.all_gather(across, "wide", axis=1)
    return whole.reshape(-1, block.shape[1])


def high_dot(left, right):
    return jnp.dot(left, right, precision=highest_precision)


def orthogonal_map(gram):
    scale = 1.0 / (jnp.sqrt(jnp.trace(gram)) + 1e-07)
    gram = gram * (scale * scale)
    eye = jnp.eye(gram.shape[0], dtype=jnp.float32)
    mapped = None
    for iteration in range(NS_ITERS):
        poly = coef_a * eye + coef_b * gram + coef_c * high_dot(gram, gram)
        if iteration < NS_ITERS - 1:
            gram = high_dot(poly, high_dot(poly, gram))
        mapped = poly * scale if mapped is None else high_dot(poly, mapped)
    return mapped


def adam_update(weight, grad, first, second):
    first_new = beta_one * first + (1.0 - beta_one) * grad
    second_new = beta_two * second + (1.0 - beta_two) * grad * grad
    first_hat = first_new / (1.0 - beta_one**STEP_NUMBER)
    second_hat = second_new / (1.0 - beta_two**STEP_NUMBER)
    weight_new = weight - adam_rate * (
        first_hat / (jnp.sqrt(second_hat) + adam_eps) + decay_rate * weight
    )
    return (weight_new, first_new, second_new)


def on_device(
    prior_states,
    target,
    noise_draw,
    level_index,
    g2m_edges,
    neighbours,
    m2g_edges,
    valid_mask,
    channel_weights,
    w_embed,
    w_cond,
    w_attn,
    w_up,
    w_down,
    w_dec,
    biases,
    mom_attn,
    mom_up,
    mom_down,
    m_embed,
    v_embed,
    m_cond,
    v_cond,
    m_dec,
    v_dec,
    m_bias,
    v_bias,
    ema_embed,
    ema_cond,
    ema_attn,
    ema_up,
    ema_down,
    ema_dec,
    ema_bias,
):
    narrow_pos = lax.axis_index("narrow")
    narrow_count = lax.axis_size("narrow")
    pixel_local = valid_mask.shape[1]
    node_local = neighbours.shape[1]
    pixel_total = pixel_local * narrow_count
    node_total = node_local * narrow_count
    embed_low = w_embed.astype(jnp.bfloat16)
    dec_low = w_dec.astype(jnp.bfloat16)
    bias_embed = biases[:LATENT_WIDTH]
    bias_up = biases[LATENT_WIDTH : LATENT_WIDTH + FF]
    bias_out = biases[LATENT_WIDTH + FF :]
    noise_level, scale_in, skip_scale, out_scale, loss_scale = sigma_terms(level_index[0])
    target_rows = target[0].astype(jnp.float32)
    noisy = target_rows + noise_level * noise_draw[0].astype(jnp.float32)
    features = jnp.concatenate(
        [prior_states[0, 0], prior_states[0, 1], (scale_in * noisy).astype(jnp.bfloat16)], axis=0
    )
    feature_slots = line_slots(features)
    g2m_slots = ring_slots(g2m_edges[0].T)
    attn_full = wide_gather(w_attn.astype(jnp.bfloat16), 1)
    up_full = wide_gather(w_up.astype(jnp.bfloat16), 1)
    down_full = wide_gather(w_down.astype(jnp.bfloat16), 0)
    mom_attn_full = wide_gather(mom_attn, 1)
    mom_up_full = wide_gather(mom_up, 1)
    mom_down_full = wide_gather(mom_down, 0)
    lat_weight = lat_weights(narrow_pos * pixel_local, pixel_local, pixel_total)
    pixel_weight = lat_weight * valid_mask[0].astype(jnp.float32)
    weight_total = small_sum(jnp.sum(pixel_weight).reshape(1, 1))[0, 0]

    g2m_ids = (jnp.concatenate(g2m_slots, axis=1) - narrow_pos * pixel_local) % pixel_total
    g2m_ids = g2m_ids.T
    near_ids = (neighbours[0] - narrow_pos * node_local) % node_total
    m2g_ids = (m2g_edges[0] - narrow_pos * node_local) % node_total
    g2m_counts = [
        count_matrix(g2m_ids, slot * pixel_local, pixel_local) for slot in range(narrow_count)
    ]
    near_counts = count_matrix(near_ids, 0, node_total)
    m2g_counts = count_matrix(m2g_ids, 0, node_total)

    embed_pres = []
    node_in = None
    for slot in range(narrow_count):
        embed_pre = contract_rows(feature_slots[slot], embed_low) + bias_embed
        embedded = jax.nn.silu(embed_pre).astype(jnp.bfloat16)
        part = jnp.dot(g2m_counts[slot], embedded, preferred_element_type=jnp.float32)
        node_in = part if node_in is None else node_in + part
        embed_pres.append(embed_pre)
    node_in = node_in / G2M_K
    conditioning = cond_features(noise_level)
    modulation = jnp.dot(conditioning, w_cond, precision=highest_precision)
    gain_one = 1.0 + modulation[:LATENT_WIDTH]
    gain_two = 1.0 + modulation[2 * LATENT_WIDTH : 3 * LATENT_WIDTH]
    normed_one, inverse_one = norm_stats(node_in)
    attn_in = (normed_one * gain_one + modulation[LATENT_WIDTH : 2 * LATENT_WIDTH]).astype(
        jnp.bfloat16
    )
    attn_own = attn_in[:node_local]
    query_map = attn_full[:, :LATENT_WIDTH]
    pair_map = attn_full[:, LATENT_WIDTH : 3 * LATENT_WIDTH]
    proj_map = attn_full[:, 3 * LATENT_WIDTH :]
    query_rows = jnp.dot(attn_own, query_map, preferred_element_type=jnp.float32).astype(
        jnp.bfloat16
    )
    pair_rows = jnp.dot(attn_in, pair_map, preferred_element_type=jnp.float32).astype(
        jnp.bfloat16
    )
    key_rows = pair_rows[:, :LATENT_WIDTH]
    value_rows = pair_rows[:, LATENT_WIDTH:]

    counts = near_counts.astype(jnp.float32)
    attended_heads = []
    prob_heads = []
    for head in range(HEADS):
        part = slice(head * HEAD_WIDTH, (head + 1) * HEAD_WIDTH)
        scores = contract_last(query_rows[:, part], key_rows[:, part]) / math.sqrt(HEAD_WIDTH)
        scores = jnp.where(counts > 0, scores, -jnp.inf)
        raised = jnp.exp(scores - jnp.max(scores, axis=1, keepdims=True))
        prob = raised / jnp.sum(raised * counts, axis=1, keepdims=True)
        lowered = (prob.astype(jnp.bfloat16).astype(jnp.float32) * counts).astype(jnp.bfloat16)
        prob_heads.append((prob, lowered))
        attended_heads.append(
            jnp.dot(lowered, value_rows[:, part], preferred_element_type=jnp.float32)
        )
    attended_rows = jnp.concatenate(attended_heads, axis=1).astype(jnp.bfloat16)
    node_mid = node_in[:node_local] + jnp.dot(
        attended_rows, proj_map, preferred_element_type=jnp.float32
    )
    normed_two, inverse_two = norm_stats(node_mid)
    mlp_in = (normed_two * gain_two + modulation[3 * LATENT_WIDTH :]).astype(jnp.bfloat16)
    up_pre = jnp.dot(mlp_in, up_full, preferred_element_type=jnp.float32) + bias_up
    hidden = jax.nn.silu(up_pre).astype(jnp.bfloat16)
    node_out = node_mid + jnp.dot(hidden, down_full, preferred_element_type=jnp.float32)
    node_low = node_out.astype(jnp.bfloat16)
    node_raw = lax.dot_general(
        dec_low, node_low, (((0,), (1,)), ((), ())), preferred_element_type=jnp.float32
    ).astype(jnp.bfloat16)
    all_raw = jnp.concatenate(ring_slots(node_raw), axis=1)
    raw_output = contract_last(all_raw, m2g_counts) / M2G_K + bias_out[:, None]
    errors = skip_scale * noisy + out_scale * raw_output - target_rows
    weighted = channel_weights[:, None] * pixel_weight[None, :]
    loss_local = loss_scale * jnp.sum(weighted * errors * errors)
    grad_raw = (2.0 * loss_scale * out_scale / weight_total * weighted * errors).astype(
        jnp.bfloat16
    )
    grad_out_bias = jnp.sum(grad_raw.astype(jnp.float32), axis=1)
    raw_spread = jnp.dot(grad_raw, m2g_counts, preferred_element_type=jnp.float32)
    grad_node_raw = (
        ring_sum(
            [
                raw_spread[:, slot * node_local : (slot + 1) * node_local]
                for slot in range(narrow_count)
            ]
        )
        / M2G_K
    )
    grad_dec = lax.dot_general(
        node_low.astype(jnp.float32),
        grad_node_raw,
        (((0,), (1,)), ((), ())),
        precision=highest_precision,
    )
    grad_node_out = lax.dot_general(
        grad_node_raw,
        dec_low.astype(jnp.float32),
        (((0,), (1,)), ((), ())),
        precision=highest_precision,
    )
    grad_mlp = grad_node_out.astype(jnp.bfloat16)
    grad_down = contract_rows(hidden, grad_mlp)
    grad_hidden = contract_last(grad_mlp, down_full)
    grad_up_pre = (grad_hidden * silu_slope(up_pre)).astype(jnp.bfloat16)
    grad_up_bias = jnp.sum(grad_up_pre.astype(jnp.float32), axis=0)
    grad_up = contract_rows(mlp_in, grad_up_pre)
    grad_mlp_in = contract_last(grad_up_pre, up_full)
    grad_node_mid = grad_node_out + norm_back(grad_mlp_in * gain_two, normed_two, inverse_two)
    grad_proj_out = grad_node_mid.astype(jnp.bfloat16)
    grad_proj = contract_rows(attended_rows, grad_proj_out)
    sum_down = large_sum(grad_down, jnp.bfloat16)
    sum_up = large_sum(grad_up, jnp.bfloat16)
    sum_proj = large_sum(grad_proj, jnp.bfloat16)
    gradient_attended = contract_last(grad_proj_out, proj_map).astype(jnp.bfloat16)

    query_grads, key_grads, value_grads = [], [], []
    for head in range(HEADS):
        part = slice(head * HEAD_WIDTH, (head + 1) * HEAD_WIDTH)
        prob, lowered = prob_heads[head]
        grad_head = gradient_attended[:, part]
        grad_prob = contract_last(grad_head, value_rows[:, part])
        weighted_prob = prob * counts
        inner = jnp.sum(weighted_prob * grad_prob, axis=1, keepdims=True)
        grad_scores = (
            (prob * (grad_prob - inner)).astype(jnp.bfloat16).astype(jnp.float32) * counts
        ).astype(jnp.bfloat16)
        query_grads.append(
            jnp.dot(grad_scores, key_rows[:, part], preferred_element_type=jnp.float32)
        )
        key_grads.append(contract_rows(grad_scores, query_rows[:, part]))
        value_grads.append(contract_rows(lowered, grad_head))
    grad_query_rows = (jnp.concatenate(query_grads, axis=1) / math.sqrt(HEAD_WIDTH)).astype(
        jnp.bfloat16
    )
    grad_pair_rows = jnp.concatenate(
        [jnp.concatenate(key_grads, axis=1) / math.sqrt(HEAD_WIDTH)] + value_grads, axis=1
    ).astype(jnp.bfloat16)

    grad_qkv = jnp.concatenate(
        [contract_rows(attn_own, grad_query_rows), contract_rows(attn_in, grad_pair_rows)], axis=1
    )
    sum_qkv = large_sum(grad_qkv, jnp.bfloat16)
    grad_attn_in = contract_last(grad_pair_rows, pair_map)
    grad_attn_in = grad_attn_in.at[:node_local].add(contract_last(grad_query_rows, query_map))
    grad_node_in = norm_back(grad_attn_in * gain_one, normed_one, inverse_one)
    grad_node_in = grad_node_in.at[:node_local].add(grad_node_mid)
    grad_modulation = jnp.concatenate(
        [
            jnp.sum(grad_attn_in * normed_one, axis=0),
            jnp.sum(grad_attn_in, axis=0),
            jnp.sum(grad_mlp_in * normed_two, axis=0),
            jnp.sum(grad_mlp_in, axis=0),
        ]
    )
    grad_cond = conditioning[:, None] * grad_modulation[None, :]
    node_grads = (grad_node_in / G2M_K).astype(jnp.bfloat16)
    grad_embed = None
    grad_embed_bias = None
    for slot in range(narrow_count):
        grad_embedded = contract_rows(g2m_counts[slot], node_grads)
        grad_pre = (grad_embedded * silu_slope(embed_pres[slot])).astype(jnp.bfloat16)
        bias_part = jnp.sum(grad_pre.astype(jnp.float32), axis=0)
        embed_part = jnp.dot(feature_slots[slot], grad_pre, preferred_element_type=jnp.float32)
        grad_embed = embed_part if grad_embed is None else grad_embed + embed_part
        grad_embed_bias = bias_part if grad_embed_bias is None else grad_embed_bias + bias_part

    grad_bias = jnp.concatenate([grad_embed_bias, grad_up_bias, grad_out_bias])
    pieces = [grad_embed, grad_cond, grad_dec, grad_bias, loss_local]
    flat = jnp.concatenate([piece.reshape(-1) for piece in pieces])
    row_total = -(-flat.shape[0] // (LATENT_WIDTH * 256)) * 256
    flat = jnp.pad(flat, (0, row_total * LATENT_WIDTH - flat.shape[0]))
    flat = large_sum(flat.reshape(row_total, LATENT_WIDTH), jnp.float32).reshape(-1)
    sums = []
    place = 0
    for piece in pieces:
        sums.append(flat[place : place + piece.size].reshape(piece.shape))
        place += piece.size
    sum_embed, sum_cond, sum_dec, sum_bias, loss_sum = sums
    sum_attn = jnp.concatenate([sum_qkv, sum_proj], axis=1)
    square_sum = (
        jnp.sum(sum_embed * sum_embed)
        + jnp.sum(sum_cond * sum_cond)
        + jnp.sum(sum_attn * sum_attn)
        + jnp.sum(sum_up * sum_up)
        + jnp.sum(sum_down * sum_down)
        + jnp.sum(sum_dec * sum_dec)
        + jnp.sum(sum_bias * sum_bias)
    )
    grad_norm = jnp.sqrt(square_sum)
    factor = jnp.minimum(1.0, clip_bound / (grad_norm + 1e-06))
    attn_cols = w_attn.shape[1]
    up_cols = w_up.shape[1]
    down_rows = w_down.shape[0]
    all_attn = muon_decay * mom_attn_full + factor * sum_attn
    all_up = muon_decay * mom_up_full + factor * sum_up
    all_down = muon_decay * mom_down_full + factor * sum_down
    moment_attn = lax.dynamic_slice_in_dim(all_attn, narrow_pos * attn_cols, attn_cols, 1)
    moment_up = lax.dynamic_slice_in_dim(all_up, narrow_pos * up_cols, up_cols, 1)
    moment_down = lax.dynamic_slice_in_dim(all_down, narrow_pos * down_rows, down_rows, 0)
    map_attn = orthogonal_map(high_dot(all_attn, all_attn.T))
    map_up = orthogonal_map(high_dot(all_up, all_up.T))
    map_down = orthogonal_map(
        lax.dot_general(
            all_down, all_down, (((0,), (0,)), ((), ())), precision=highest_precision
        )
    )
    attn_orth = high_dot(map_attn, moment_attn)
    up_orth = high_dot(map_up, moment_up)
    down_orth = lax.dot_general(
        moment_down, map_down, (((1,), (1,)), ((), ())), precision=highest_precision
    )
    new_attn = (
        w_attn - muon_rate * math.sqrt(max(1.0, LATENT_WIDTH / (4 * LATENT_WIDTH))) * attn_orth
    )
    new_up = w_up - muon_rate * math.sqrt(max(1.0, LATENT_WIDTH / FF)) * up_orth
    new_down = w_down - muon_rate * math.sqrt(max(1.0, FF / LATENT_WIDTH)) * down_orth
    new_embed, first_embed, second_embed = adam_update(
        w_embed, factor * sum_embed, m_embed, v_embed
    )
    new_cond, first_cond, second_cond = adam_update(w_cond, factor * sum_cond, m_cond, v_cond)
    new_dec, first_dec, second_dec = adam_update(w_dec, factor * sum_dec, m_dec, v_dec)
    new_bias, first_bias, second_bias = adam_update(biases, factor * sum_bias, m_bias, v_bias)
    keep_rest = 1.0 - ema_keep
    return (
        new_attn,
        new_up,
        new_down,
        moment_attn,
        moment_up,
        moment_down,
        new_embed,
        new_cond,
        new_dec,
        new_bias,
        first_embed,
        second_embed,
        first_cond,
        second_cond,
        first_dec,
        second_dec,
        first_bias,
        second_bias,
        ema_keep * ema_embed + keep_rest * new_embed,
        ema_keep * ema_cond + keep_rest * new_cond,
        ema_keep * ema_attn + keep_rest * new_attn,
        ema_keep * ema_up + keep_rest * new_up,
        ema_keep * ema_down + keep_rest * new_down,
        ema_keep * ema_dec + keep_rest * new_dec,
        ema_keep * ema_bias + keep_rest * new_bias,
        loss_sum,
        weight_total,
        grad_norm,
    )


def solution(mesh):
    in_specs = (
        P("wide", None, None, "narrow"),
        P("wide", None, "narrow"),
        P("wide", None, "narrow"),
        P("wide"),
        P("wide", "narrow", None),
        P("wide", "narrow", None),
        P("wide", "narrow", None),
        P("wide", "narrow"),
        P(),
        P(),
        P(),
        P(None, "narrow"),
        P(None, "narrow"),
        P("narrow", None),
        P(),
        P(),
        P(None, "narrow"),
        P(None, "narrow"),
        P("narrow", None),
        P(),
        P(),
        P(),
        P(),
        P(),
        P(),
        P(),
        P(),
        P(),
        P(),
        P(None, "narrow"),
        P(None, "narrow"),
        P("narrow", None),
        P(),
        P(),
    )
    out_specs = (
        P(None, "narrow"),
        P(None, "narrow"),
        P("narrow", None),
        P(None, "narrow"),
        P(None, "narrow"),
        P("narrow", None),
        P(),
        P(),
        P(),
        P(),
        P(),
        P(),
        P(),
        P(),
        P(),
        P(),
        P(),
        P(),
        P(),
        P(),
        P(None, "narrow"),
        P(None, "narrow"),
        P("narrow", None),
        P(),
        P(),
        P(),
        P(),
        P(),
    )
    return jax.shard_map(
        on_device, mesh=mesh, in_specs=in_specs, out_specs=out_specs, check_vma=False
    )
```

```python
import functools
import math

import jax
import jax.numpy as jnp
from jax import lax
from jax.experimental import pallas as pl
from jax.experimental.pallas import tpu as pltpu
from jax.sharding import PartitionSpec as P

LATENT_WIDTH = 512
HEADS = 4
HEAD_WIDTH = 128
FF = 2048
COND = 32
NBR = 32
G2M_K = 4
M2G_K = 3
NS_ITERS = 5
SIGMA_LEVELS = 8
STEP_NUMBER = 10


highest_precision = lax.Precision.HIGHEST
sigma_low = 0.25
sigma_high = 4.0
clip_bound = 0.02
muon_rate = 0.5
muon_decay = 0.95
adam_rate = 0.03
beta_one = 0.9
beta_two = 0.95
adam_eps = 1e-08
decay_rate = 0.01
ema_keep = 0.9
coef_a = 3.4445
coef_b = -4.775
coef_c = 2.0315


def sigma_terms(level):
    fraction = level.astype(jnp.float32) / (SIGMA_LEVELS - 1)
    noise_level = sigma_low * (sigma_high / sigma_low) ** fraction
    square = noise_level * noise_level + 1.0
    scale_in = lax.rsqrt(square)
    return (
        noise_level,
        scale_in,
        1.0 / square,
        noise_level * scale_in,
        square / (noise_level * noise_level),
    )


def cond_features(noise_level):
    frequencies = 1.0 + jnp.arange(COND // 2).astype(jnp.float32)
    phases = jnp.log(noise_level) * frequencies
    return jnp.concatenate([jnp.sin(phases), jnp.cos(phases)])


def lat_weights(first_row, row_count, pixel_total):
    row_ids = (first_row + jnp.arange(row_count, dtype=jnp.int32)).astype(jnp.float32)
    return jnp.cos(math.pi * ((row_ids + 0.5) / pixel_total - 0.5))


def norm_stats(values):
    centred = values - jnp.mean(values, axis=-1, keepdims=True)
    inverse = lax.rsqrt(jnp.mean(centred * centred, axis=-1, keepdims=True) + 1e-05)
    return (centred * inverse, inverse)


def norm_back(grad_normed, normed, inverse):
    first_mean = jnp.mean(grad_normed, axis=-1, keepdims=True)
    second_mean = jnp.mean(grad_normed * normed, axis=-1, keepdims=True)
    return inverse * (grad_normed - first_mean - normed * second_mean)


def silu_slope(values):
    sigmoid_values = jax.nn.sigmoid(values)
    return sigmoid_values * (1.0 + values * (1.0 - sigmoid_values))


def contract_rows(left, right):
    return lax.dot_general(
        left, right, (((0,), (0,)), ((), ())), preferred_element_type=jnp.float32
    )


def contract_last(left, right):
    return lax.dot_general(
        left, right, (((1,), (1,)), ((), ())), preferred_element_type=jnp.float32
    )


def bit_swap(values, axis_name, bit):
    size = lax.axis_size(axis_name)
    return lax.ppermute(values, axis_name, [(i, i ^ (1 << bit)) for i in range(size)])


def axis_bits(axis_name):
    bits = []
    reach = 1
    while reach < lax.axis_size(axis_name):
        bits.append((axis_name, len(bits)))
        reach *= 2
    return bits


def small_sum(values):
    for axis_name, bit in axis_bits("wide") + axis_bits("narrow"):
        values = values + bit_swap(values, axis_name, bit)
    return values


def sum_stages():
    wide_bits = len(axis_bits("wide"))
    stages = [("wide", 0, 1)]
    first = 1
    while first < wide_bits:
        stages.append(("wide", first, min(2, wide_bits - first)))
        first += 2
    stages.append(("narrow", 0, len(axis_bits("narrow"))))
    return stages


def partner_swap(values, axis_name, distance):
    size = lax.axis_size(axis_name)
    return lax.ppermute(values, axis_name, [(i, i ^ distance) for i in range(size)])


def large_sum(values, sent_type):
    stages = sum_stages()
    for axis_name, first, width in stages:
        members = 1 << width
        block = values.shape[0] // members
        mine = (lax.axis_index(axis_name) >> first) & (members - 1)
        arrived = [
            partner_swap(
                lax.dynamic_slice_in_dim(values, (mine ^ far) * block, block, 0).astype(sent_type),
                axis_name,
                far << first,
            )
            for far in range(1, members)
        ]
        values = lax.dynamic_slice_in_dim(values, mine * block, block, 0)
        for piece in arrived:
            values = values + piece.astype(jnp.float32)
    values = values.astype(sent_type)
    for axis_name, first, width in stages[::-1]:
        members = 1 << width
        block = values.shape[0]
        mine = (lax.axis_index(axis_name) >> first) & (members - 1)
        pieces = [values] + [
            partner_swap(values, axis_name, far << first) for far in range(1, members)
        ]
        for bit in range(width):
            is_high = ((mine >> bit) & 1) == 1
            step = 1 << bit
            pieces = [
                jnp.where(is_high, pieces[place ^ step], pieces[place])
                for place in range(members)
            ]
        values = jnp.concatenate(pieces, axis=0)
    return values


def ring_slots(values):
    size = lax.axis_size("narrow")
    slots = [values]
    for shift in range(1, size):
        slots.append(
            lax.ppermute(values, "narrow", [((i + shift) % size, i) for i in range(size)])
        )
    return slots


def line_slots(values):
    size = lax.axis_size("narrow")
    pos = lax.axis_index("narrow")
    from_low, from_high = values, values
    low_list, high_list = [], []
    for step in range(size - 1):
        from_low = lax.ppermute(from_low, "narrow", [(i, i + 1) for i in range(step, size - 1)])
        from_high = lax.ppermute(
            from_high, "narrow", [(i, i - 1) for i in range(1, size - step)]
        )
        low_list.append(from_low)
        high_list.append(from_high)
    slots = [values]
    for shift in range(1, size):
        slots.append(
            jnp.where(pos + shift < size, high_list[shift - 1], low_list[size - shift - 1])
        )
    return slots


def ring_sum(parts):
    size = lax.axis_size("narrow")
    total = parts[0]
    for shift in range(1, size):
        arrived = lax.ppermute(
            parts[shift].astype(jnp.bfloat16),
            "narrow",
            [(i, (i + shift) % size) for i in range(size)],
        )
        total = total + arrived.astype(jnp.float32)
    return total


def wide_gather(blocks):
    wide_count = lax.axis_size("wide")
    own = []
    for block in blocks:
        rows = block.shape[0] // wide_count
        own.append(lax.dynamic_slice_in_dim(block, lax.axis_index("wide") * rows, rows, 0))
    own = jnp.stack(own)
    across = lax.all_gather(own, "narrow", axis=0)
    whole = lax.all_gather(across, "wide", axis=0)
    side = whole[:, :, :-1].transpose(2, 0, 3, 1, 4)
    side = side.reshape(side.shape[0], blocks[0].shape[0], -1)
    last = whole[:, :, -1].transpose(1, 0, 2, 3).reshape(-1, blocks[-1].shape[1])
    return [side[place] for place in range(side.shape[0])] + [last]


VMEM_LIMIT = 60 * 1024 * 1024
SCORE_SCALE = math.log2(math.e) / math.sqrt(HEAD_WIDTH)
MASKED = -1e30


def kernel_params():
    return pltpu.CompilerParams(vmem_limit_bytes=VMEM_LIMIT)


def count_kernel(ids_ref, out_ref):
    first = pl.program_id(0) * out_ref.shape[1]
    columns = lax.broadcasted_iota(jnp.int32, out_ref.shape, 1).astype(jnp.int16)
    ids = (ids_ref[...] - first).astype(jnp.int16)
    one = jnp.ones(out_ref.shape, jnp.bfloat16)
    zero = jnp.zeros(out_ref.shape, jnp.bfloat16)
    total = zero
    for slot in range(ids.shape[1]):
        total = total + jnp.where(ids[:, slot : slot + 1] == columns, one, zero)
    out_ref[...] = total


def count_matrix(ids, column_count, rows=1024, columns=2048):
    row_count, slots = ids.shape
    rows = min(rows, row_count)
    columns = min(columns, column_count)
    return pl.pallas_call(
        count_kernel,
        grid=(column_count // columns, row_count // rows),
        in_specs=[pl.BlockSpec((rows, slots), lambda j, i: (i, 0))],
        out_specs=pl.BlockSpec((rows, columns), lambda j, i: (i, j)),
        out_shape=jax.ShapeDtypeStruct((row_count, column_count), jnp.bfloat16),
        cost_estimate=pl.CostEstimate(
            flops=4 * slots * row_count * column_count,
            bytes_accessed=2 * row_count * column_count,
            transcendentals=0,
        ),
        compiler_params=kernel_params(),
    )(ids)


def bias_kernel(row_ref, lane_ref, out_ref):
    groups, width = row_ref.shape
    blocks = out_ref.shape[1] // 128
    row_iota = lax.broadcasted_iota(jnp.int32, (8 * blocks, width), 0)
    lane_iota = lax.broadcasted_iota(jnp.int32, (128, width), 0)
    for group in range(groups):
        left = jnp.where(row_iota == row_ref[group : group + 1, :], 1.0, 0.0)
        right = jnp.where(lane_iota == lane_ref[group : group + 1, :], 1.0, 0.0)
        counts = contract_last(left.astype(jnp.bfloat16), right.astype(jnp.bfloat16))
        bias = jnp.where(counts > 0.5, jnp.log2(counts), MASKED)
        for block in range(blocks):
            out_ref[group * 8 : (group + 1) * 8, block * 128 : (block + 1) * 128] = bias[
                block * 8 : (block + 1) * 8, :
            ]


def count_bias(ids, total, per_step=32):
    row_count, slots = ids.shape
    groups = row_count // 8
    member = (jnp.arange(row_count, dtype=jnp.int32) % 8)[:, None]
    row_keys = ((ids // 128) * 8 + member).reshape(groups, 8 * slots)
    lane_keys = (ids % 128).reshape(groups, 8 * slots)
    spec = pl.BlockSpec((per_step, 8 * slots), lambda i: (i, 0))
    return pl.pallas_call(
        bias_kernel,
        grid=(groups // per_step,),
        in_specs=[spec, spec],
        out_specs=pl.BlockSpec((8 * per_step, total), lambda i: (i, 0)),
        out_shape=jax.ShapeDtypeStruct((row_count, total), jnp.float32),
        cost_estimate=pl.CostEstimate(
            flops=16 * row_count * total, bytes_accessed=4 * row_count * total, transcendentals=0
        ),
        compiler_params=kernel_params(),
    )(row_keys, lane_keys)


def attend_kernel(chunk, q_ref, k_ref, v_ref, bias_ref, att_ref, mass_ref, score_ref):
    q = q_ref[...]
    total = k_ref.shape[0]
    top = None
    for start in range(0, total, chunk):
        part = pl.ds(start, chunk)
        scores = contract_last(q, k_ref[part, :]) * SCORE_SCALE + bias_ref[:, part]
        score_ref[:, part] = scores
        highest = jnp.max(scores, axis=1, keepdims=True)
        top = highest if top is None else jnp.maximum(top, highest)
    mass = jnp.zeros((q.shape[0], 1), jnp.float32)
    attended = jnp.zeros(att_ref.shape, jnp.float32)
    for start in range(0, total, chunk):
        part = pl.ds(start, chunk)
        raised = jnp.exp2(score_ref[:, part] - top)
        mass = mass + jnp.sum(raised, axis=1, keepdims=True)
        attended = attended + jnp.dot(
            raised.astype(jnp.bfloat16), v_ref[part, :], preferred_element_type=jnp.float32
        )
    att_ref[...] = attended / mass
    mass_ref[...] = jnp.broadcast_to(top + jnp.log2(mass), mass_ref.shape)


def attend(queries, pairs, bias, rows=256, chunk=512):
    row_count = queries.shape[0]
    total = pairs.shape[0]
    block = pl.BlockSpec((rows, HEAD_WIDTH), lambda h, r: (r, h))
    return pl.pallas_call(
        functools.partial(attend_kernel, chunk),
        grid=(HEADS, row_count // rows),
        in_specs=[
            block,
            pl.BlockSpec((total, HEAD_WIDTH), lambda h, r: (0, h)),
            pl.BlockSpec((total, HEAD_WIDTH), lambda h, r: (0, HEADS + h)),
            pl.BlockSpec((rows, total), lambda h, r: (r, 0)),
        ],
        out_specs=[block, block],
        out_shape=[jax.ShapeDtypeStruct(queries.shape, jnp.float32)] * 2,
        scratch_shapes=[pltpu.VMEM((rows, total), jnp.float32)],
        cost_estimate=pl.CostEstimate(
            flops=16 * row_count * total * HEAD_WIDTH * HEADS,
            bytes_accessed=16 * row_count * total,
            transcendentals=HEADS * row_count * total,
        ),
        compiler_params=kernel_params(),
    )(queries, pairs, pairs, bias)


def attend_back_kernel(
    chunk, q_ref, k_ref, v_ref, bias_ref, mass_ref, att_ref, g_ref, dq_ref, dk_ref, dv_ref, dk_sum, dv_sum
):
    step = pl.program_id(1)
    q = q_ref[...]
    g = g_ref[...]
    total = k_ref.shape[0]
    mass = mass_ref[:, :1]
    inner = jnp.sum(att_ref[...] * g.astype(jnp.float32), axis=1, keepdims=True)

    @pl.when(step == 0)
    def _():
        dk_sum[...] = jnp.zeros_like(dk_sum)
        dv_sum[...] = jnp.zeros_like(dv_sum)

    dq = jnp.zeros(q.shape, jnp.float32)
    for start in range(0, total, chunk):
        part = pl.ds(start, chunk)
        k = k_ref[part, :]
        v = v_ref[part, :]
        prob = jnp.exp2(contract_last(q, k) * SCORE_SCALE + (bias_ref[:, part] - mass))
        grad_scores = (prob * (contract_last(g, v) - inner)).astype(jnp.bfloat16)
        dq = dq + jnp.dot(grad_scores, k, preferred_element_type=jnp.float32)
        dk_sum[part, :] += contract_rows(grad_scores, q)
        dv_sum[part, :] += contract_rows(prob.astype(jnp.bfloat16), g)
    shrink = 1.0 / math.sqrt(HEAD_WIDTH)
    dq_ref[...] = (dq * shrink).astype(jnp.bfloat16)

    @pl.when(step == pl.num_programs(1) - 1)
    def _():
        dk_ref[...] = (dk_sum[...] * shrink).astype(jnp.bfloat16)
        dv_ref[...] = dv_sum[...].astype(jnp.bfloat16)


def attend_back(queries, pairs, bias, mass, attended, grads, rows=1024, chunk=256):
    row_count = queries.shape[0]
    total = pairs.shape[0]
    rows = min(rows, row_count)
    block = pl.BlockSpec((rows, HEAD_WIDTH), lambda h, r: (r, h))
    column = pl.BlockSpec((total, HEAD_WIDTH), lambda h, r: (0, h))
    key_shape = jax.ShapeDtypeStruct((total, LATENT_WIDTH), jnp.bfloat16)
    return pl.pallas_call(
        functools.partial(attend_back_kernel, chunk),
        grid=(HEADS, row_count // rows),
        in_specs=[
            block,
            column,
            pl.BlockSpec((total, HEAD_WIDTH), lambda h, r: (0, HEADS + h)),
            pl.BlockSpec((rows, total), lambda h, r: (r, 0)),
            block,
            block,
            block,
        ],
        out_specs=[block, column, column],
        out_shape=[jax.ShapeDtypeStruct(queries.shape, jnp.bfloat16), key_shape, key_shape],
        scratch_shapes=[pltpu.VMEM((total, HEAD_WIDTH), jnp.float32)] * 2,
        cost_estimate=pl.CostEstimate(
            flops=24 * row_count * total * HEAD_WIDTH * HEADS,
            bytes_accessed=16 * row_count * total,
            transcendentals=HEADS * row_count * total,
        ),
        compiler_params=kernel_params(),
    )(queries, pairs, pairs, bias, mass, attended, grads)


def high_dot(left, right):
    return jnp.dot(left, right, precision=highest_precision)


def orthogonal_map(gram):
    scale = 1.0 / (jnp.sqrt(jnp.trace(gram)) + 1e-07)
    gram = gram * (scale * scale)
    eye = jnp.eye(gram.shape[0], dtype=jnp.float32)
    mapped = None
    for iteration in range(NS_ITERS):
        poly = coef_a * eye + coef_b * gram + coef_c * high_dot(gram, gram)
        if iteration < NS_ITERS - 1:
            gram = high_dot(poly, high_dot(poly, gram))
        mapped = poly * scale if mapped is None else high_dot(poly, mapped)
    return mapped


def adam_update(weight, grad, first, second):
    first_new = beta_one * first + (1.0 - beta_one) * grad
    second_new = beta_two * second + (1.0 - beta_two) * grad * grad
    first_hat = first_new / (1.0 - beta_one**STEP_NUMBER)
    second_hat = second_new / (1.0 - beta_two**STEP_NUMBER)
    weight_new = weight - adam_rate * (
        first_hat / (jnp.sqrt(second_hat) + adam_eps) + decay_rate * weight
    )
    return (weight_new, first_new, second_new)


def on_device(
    prior_states,
    target,
    noise_draw,
    level_index,
    g2m_edges,
    neighbours,
    m2g_edges,
    valid_mask,
    channel_weights,
    w_embed,
    w_cond,
    w_attn,
    w_up,
    w_down,
    w_dec,
    biases,
    mom_attn,
    mom_up,
    mom_down,
    m_embed,
    v_embed,
    m_cond,
    v_cond,
    m_dec,
    v_dec,
    m_bias,
    v_bias,
    ema_embed,
    ema_cond,
    ema_attn,
    ema_up,
    ema_down,
    ema_dec,
    ema_bias,
):
    narrow_pos = lax.axis_index("narrow")
    narrow_count = lax.axis_size("narrow")
    pixel_local = valid_mask.shape[1]
    node_local = neighbours.shape[1]
    pixel_total = pixel_local * narrow_count
    node_total = node_local * narrow_count
    embed_low = w_embed.astype(jnp.bfloat16)
    dec_low = w_dec.astype(jnp.bfloat16)
    bias_embed = biases[:LATENT_WIDTH]
    bias_up = biases[LATENT_WIDTH : LATENT_WIDTH + FF]
    bias_out = biases[LATENT_WIDTH + FF :]
    noise_level, scale_in, skip_scale, out_scale, loss_scale = sigma_terms(level_index[0])
    target_rows = target[0].astype(jnp.float32)
    noisy = target_rows + noise_level * noise_draw[0].astype(jnp.float32)
    features = jnp.concatenate(
        [prior_states[0, 0], prior_states[0, 1], (scale_in * noisy).astype(jnp.bfloat16)], axis=0
    )
    g2m_slots = ring_slots(g2m_edges[0].T)
    feature_slots = line_slots(features)
    attn_full, up_full, down_full = wide_gather(
        [w_attn.astype(jnp.bfloat16), w_up.astype(jnp.bfloat16), w_down.astype(jnp.bfloat16)]
    )
    lat_weight = lat_weights(narrow_pos * pixel_local, pixel_local, pixel_total)
    pixel_weight = lat_weight * valid_mask[0].astype(jnp.float32)
    weight_total = small_sum(jnp.sum(pixel_weight).reshape(1, 1))[0, 0]

    g2m_ids = (jnp.concatenate(g2m_slots, axis=1) - narrow_pos * pixel_local) % pixel_total
    g2m_ids = g2m_ids.T
    near_ids = (neighbours[0] - narrow_pos * node_local) % node_total
    m2g_ids = (m2g_edges[0] - narrow_pos * node_local) % node_total
    near_bias = count_bias(near_ids, node_total)
    m2g_counts = count_matrix(m2g_ids, node_total)
    g2m_counts = [
        count_matrix(g2m_ids - slot * pixel_local, pixel_local) for slot in range(narrow_count)
    ]

    embed_pres = []
    node_in = None
    for slot in range(narrow_count):
        embed_pre = contract_rows(feature_slots[slot], embed_low) + bias_embed
        embedded = jax.nn.silu(embed_pre).astype(jnp.bfloat16)
        part = jnp.dot(g2m_counts[slot], embedded, preferred_element_type=jnp.float32)
        node_in = part if node_in is None else node_in + part
        embed_pres.append(embed_pre)
    node_in = node_in / G2M_K
    conditioning = cond_features(noise_level)
    modulation = jnp.dot(conditioning, w_cond, precision=highest_precision)
    gain_one = 1.0 + modulation[:LATENT_WIDTH]
    gain_two = 1.0 + modulation[2 * LATENT_WIDTH : 3 * LATENT_WIDTH]
    normed_one, inverse_one = norm_stats(node_in)
    attn_in = (normed_one * gain_one + modulation[LATENT_WIDTH : 2 * LATENT_WIDTH]).astype(
        jnp.bfloat16
    )
    attn_own = attn_in[:node_local]
    query_map = attn_full[:, :LATENT_WIDTH]
    pair_map = attn_full[:, LATENT_WIDTH : 3 * LATENT_WIDTH]
    proj_map = attn_full[:, 3 * LATENT_WIDTH :]
    query_rows = jnp.dot(attn_own, query_map, preferred_element_type=jnp.float32).astype(
        jnp.bfloat16
    )
    pair_rows = jnp.dot(attn_in, pair_map, preferred_element_type=jnp.float32).astype(
        jnp.bfloat16
    )
    attended, mass = attend(query_rows, pair_rows, near_bias)
    attended_rows = attended.astype(jnp.bfloat16)
    mom_blocks, _ = lax.optimization_barrier(((mom_attn, mom_up, mom_down), attended))
    mom_attn_full, mom_up_full, mom_down_full = wide_gather(mom_blocks)
    node_mid = node_in[:node_local] + jnp.dot(
        attended_rows, proj_map, preferred_element_type=jnp.float32
    )
    normed_two, inverse_two = norm_stats(node_mid)
    mlp_in = (normed_two * gain_two + modulation[3 * LATENT_WIDTH :]).astype(jnp.bfloat16)
    up_pre = jnp.dot(mlp_in, up_full, preferred_element_type=jnp.float32) + bias_up
    hidden = jax.nn.silu(up_pre).astype(jnp.bfloat16)
    node_out = node_mid + jnp.dot(hidden, down_full, preferred_element_type=jnp.float32)
    node_low = node_out.astype(jnp.bfloat16)
    node_raw = lax.dot_general(
        dec_low, node_low, (((0,), (1,)), ((), ())), preferred_element_type=jnp.float32
    ).astype(jnp.bfloat16)
    all_raw = jnp.concatenate(ring_slots(node_raw), axis=1)
    raw_output = contract_last(all_raw, m2g_counts) / M2G_K + bias_out[:, None]
    errors = skip_scale * noisy + out_scale * raw_output - target_rows
    weighted = channel_weights[:, None] * pixel_weight[None, :]
    loss_local = loss_scale * jnp.sum(weighted * errors * errors)
    grad_raw = (2.0 * loss_scale * out_scale / weight_total * weighted * errors).astype(
        jnp.bfloat16
    )
    grad_out_bias = jnp.sum(grad_raw.astype(jnp.float32), axis=1)
    raw_spread = jnp.dot(grad_raw, m2g_counts, preferred_element_type=jnp.float32)
    grad_node_raw = (
        ring_sum(
            [
                raw_spread[:, slot * node_local : (slot + 1) * node_local]
                for slot in range(narrow_count)
            ]
        )
        / M2G_K
    )
    grad_dec = lax.dot_general(
        node_low.astype(jnp.float32),
        grad_node_raw,
        (((0,), (1,)), ((), ())),
        precision=highest_precision,
    )
    grad_node_out = lax.dot_general(
        grad_node_raw,
        dec_low.astype(jnp.float32),
        (((0,), (1,)), ((), ())),
        precision=highest_precision,
    )
    grad_mlp = grad_node_out.astype(jnp.bfloat16)
    grad_down = contract_rows(hidden, grad_mlp)
    grad_hidden = contract_last(grad_mlp, down_full)
    grad_up_pre = (grad_hidden * silu_slope(up_pre)).astype(jnp.bfloat16)
    grad_up_bias = jnp.sum(grad_up_pre.astype(jnp.float32), axis=0)
    grad_up = contract_rows(mlp_in, grad_up_pre)
    grad_mlp_in = contract_last(grad_up_pre, up_full)
    grad_node_mid = grad_node_out + norm_back(grad_mlp_in * gain_two, normed_two, inverse_two)
    grad_proj_out = grad_node_mid.astype(jnp.bfloat16)
    grad_proj = contract_rows(attended_rows, grad_proj_out)
    sum_down = large_sum(grad_down, jnp.bfloat16).astype(jnp.float32)
    sum_up = large_sum(grad_up, jnp.bfloat16).astype(jnp.float32)
    sum_proj = large_sum(grad_proj, jnp.bfloat16).astype(jnp.float32)
    gradient_attended = contract_last(grad_proj_out, proj_map).astype(jnp.bfloat16)

    grad_query_rows, grad_key_rows, grad_value_rows = attend_back(
        query_rows, pair_rows, near_bias, mass, attended, gradient_attended
    )
    grad_qkv = jnp.concatenate(
        [
            contract_rows(attn_own, grad_query_rows),
            contract_rows(attn_in, grad_key_rows),
            contract_rows(attn_in, grad_value_rows),
        ],
        axis=1,
    )
    sum_qkv = large_sum(grad_qkv, jnp.bfloat16).astype(jnp.float32)
    grad_attn_in = contract_last(grad_key_rows, pair_map[:, :LATENT_WIDTH])
    grad_attn_in = grad_attn_in + contract_last(grad_value_rows, pair_map[:, LATENT_WIDTH:])
    grad_attn_in = grad_attn_in.at[:node_local].add(contract_last(grad_query_rows, query_map))
    grad_node_in = norm_back(grad_attn_in * gain_one, normed_one, inverse_one)
    grad_node_in = grad_node_in.at[:node_local].add(grad_node_mid)
    grad_modulation = jnp.concatenate(
        [
            jnp.sum(grad_attn_in * normed_one, axis=0),
            jnp.sum(grad_attn_in, axis=0),
            jnp.sum(grad_mlp_in * normed_two, axis=0),
            jnp.sum(grad_mlp_in, axis=0),
        ]
    )
    grad_cond = conditioning[:, None] * grad_modulation[None, :]
    node_grads = (grad_node_in / G2M_K).astype(jnp.bfloat16)
    grad_embed = None
    grad_embed_bias = None
    for slot in range(narrow_count):
        grad_embedded = contract_rows(g2m_counts[slot], node_grads)
        grad_pre = (grad_embedded * silu_slope(embed_pres[slot])).astype(jnp.bfloat16)
        bias_part = jnp.sum(grad_pre.astype(jnp.float32), axis=0)
        embed_part = jnp.dot(feature_slots[slot], grad_pre, preferred_element_type=jnp.float32)
        grad_embed = embed_part if grad_embed is None else grad_embed + embed_part
        grad_embed_bias = bias_part if grad_embed_bias is None else grad_embed_bias + bias_part

    width = LATENT_WIDTH
    channels = w_dec.shape[1]
    late_rows = jnp.concatenate(
        [
            grad_embed,
            grad_embed_bias.reshape(1, width),
            grad_up_bias.reshape(FF // width, width),
            jnp.pad(
                jnp.concatenate([grad_out_bias, loss_local.reshape(1)]), (0, width - channels - 1)
            ).reshape(1, width),
            grad_dec.T,
        ]
        + [grad_cond[:, place * width : (place + 1) * width] for place in range(4)],
        axis=0,
    )
    device_count = lax.axis_size("wide") * narrow_count
    late_rows = jnp.pad(late_rows, ((0, -late_rows.shape[0] % (2 * device_count)), (0, 0)))
    late_rows = large_sum(late_rows, jnp.float32)
    embed_rows = w_embed.shape[0]
    sum_embed = late_rows[:embed_rows]
    place = embed_rows
    bias_rows = late_rows[place : place + 2 + FF // width].reshape(-1)
    sum_bias = bias_rows[: biases.shape[0]]
    loss_sum = bias_rows[biases.shape[0]]
    place += 2 + FF // width
    sum_dec = late_rows[place : place + channels].T
    place += channels
    sum_cond = jnp.concatenate(
        [late_rows[place + COND * part : place + COND * (part + 1)] for part in range(4)], axis=1
    )
    sum_attn = jnp.concatenate([sum_qkv, sum_proj], axis=1)
    square_sum = (
        jnp.sum(sum_embed * sum_embed)
        + jnp.sum(sum_cond * sum_cond)
        + jnp.sum(sum_attn * sum_attn)
        + jnp.sum(sum_up * sum_up)
        + jnp.sum(sum_down * sum_down)
        + jnp.sum(sum_dec * sum_dec)
        + jnp.sum(sum_bias * sum_bias)
    )
    grad_norm = jnp.sqrt(square_sum)
    factor = jnp.minimum(1.0, clip_bound / (grad_norm + 1e-06))
    attn_cols = w_attn.shape[1]
    up_cols = w_up.shape[1]
    down_rows = w_down.shape[0]
    all_attn = muon_decay * mom_attn_full + factor * sum_attn
    all_up = muon_decay * mom_up_full + factor * sum_up
    all_down = muon_decay * mom_down_full + factor * sum_down
    moment_attn = lax.dynamic_slice_in_dim(all_attn, narrow_pos * attn_cols, attn_cols, 1)
    moment_up = lax.dynamic_slice_in_dim(all_up, narrow_pos * up_cols, up_cols, 1)
    moment_down = lax.dynamic_slice_in_dim(all_down, narrow_pos * down_rows, down_rows, 0)
    map_attn = orthogonal_map(high_dot(all_attn, all_attn.T))
    map_up = orthogonal_map(high_dot(all_up, all_up.T))
    map_down = orthogonal_map(
        lax.dot_general(
            all_down, all_down, (((0,), (0,)), ((), ())), precision=highest_precision
        )
    )
    attn_orth = high_dot(map_attn, moment_attn)
    up_orth = high_dot(map_up, moment_up)
    down_orth = lax.dot_general(
        moment_down, map_down, (((1,), (1,)), ((), ())), precision=highest_precision
    )
    new_attn = (
        w_attn - muon_rate * math.sqrt(max(1.0, LATENT_WIDTH / (4 * LATENT_WIDTH))) * attn_orth
    )
    new_up = w_up - muon_rate * math.sqrt(max(1.0, LATENT_WIDTH / FF)) * up_orth
    new_down = w_down - muon_rate * math.sqrt(max(1.0, FF / LATENT_WIDTH)) * down_orth
    new_embed, first_embed, second_embed = adam_update(
        w_embed, factor * sum_embed, m_embed, v_embed
    )
    new_cond, first_cond, second_cond = adam_update(w_cond, factor * sum_cond, m_cond, v_cond)
    new_dec, first_dec, second_dec = adam_update(w_dec, factor * sum_dec, m_dec, v_dec)
    new_bias, first_bias, second_bias = adam_update(biases, factor * sum_bias, m_bias, v_bias)
    keep_rest = 1.0 - ema_keep
    return (
        new_attn,
        new_up,
        new_down,
        moment_attn,
        moment_up,
        moment_down,
        new_embed,
        new_cond,
        new_dec,
        new_bias,
        first_embed,
        second_embed,
        first_cond,
        second_cond,
        first_dec,
        second_dec,
        first_bias,
        second_bias,
        ema_keep * ema_embed + keep_rest * new_embed,
        ema_keep * ema_cond + keep_rest * new_cond,
        ema_keep * ema_attn + keep_rest * new_attn,
        ema_keep * ema_up + keep_rest * new_up,
        ema_keep * ema_down + keep_rest * new_down,
        ema_keep * ema_dec + keep_rest * new_dec,
        ema_keep * ema_bias + keep_rest * new_bias,
        loss_sum,
        weight_total,
        grad_norm,
    )


def solution(mesh):
    in_specs = (
        P("wide", None, None, "narrow"),
        P("wide", None, "narrow"),
        P("wide", None, "narrow"),
        P("wide"),
        P("wide", "narrow", None),
        P("wide", "narrow", None),
        P("wide", "narrow", None),
        P("wide", "narrow"),
        P(),
        P(),
        P(),
        P(None, "narrow"),
        P(None, "narrow"),
        P("narrow", None),
        P(),
        P(),
        P(None, "narrow"),
        P(None, "narrow"),
        P("narrow", None),
        P(),
        P(),
        P(),
        P(),
        P(),
        P(),
        P(),
        P(),
        P(),
        P(),
        P(None, "narrow"),
        P(None, "narrow"),
        P("narrow", None),
        P(),
        P(),
    )
    out_specs = (
        P(None, "narrow"),
        P(None, "narrow"),
        P("narrow", None),
        P(None, "narrow"),
        P(None, "narrow"),
        P("narrow", None),
        P(),
        P(),
        P(),
        P(),
        P(),
        P(),
        P(),
        P(),
        P(),
        P(),
        P(),
        P(),
        P(),
        P(),
        P(None, "narrow"),
        P(None, "narrow"),
        P("narrow", None),
        P(),
        P(),
        P(),
        P(),
        P(),
    )
    return jax.shard_map(
        on_device, mesh=mesh, in_specs=in_specs, out_specs=out_specs, check_vma=False
    )
```

```python
import functools
import math

import jax
import jax.numpy as jnp
from jax import lax
from jax.experimental import pallas as pl
from jax.experimental.pallas import tpu as pltpu
from jax.sharding import PartitionSpec as P

LATENT_WIDTH = 512
HEADS = 4
HEAD_WIDTH = 128
FF = 2048
COND = 32
NBR = 32
G2M_K = 4
M2G_K = 3
NS_ITERS = 5
SIGMA_LEVELS = 8
STEP_NUMBER = 10


highest_precision = lax.Precision.HIGHEST
sigma_low = 0.25
sigma_high = 4.0
clip_bound = 0.02
muon_rate = 0.5
muon_decay = 0.95
adam_rate = 0.03
beta_one = 0.9
beta_two = 0.95
adam_eps = 1e-08
decay_rate = 0.01
ema_keep = 0.9
coef_a = 3.4445
coef_b = -4.775
coef_c = 2.0315


def sigma_terms(level):
    fraction = level.astype(jnp.float32) / (SIGMA_LEVELS - 1)
    noise_level = sigma_low * (sigma_high / sigma_low) ** fraction
    square = noise_level * noise_level + 1.0
    scale_in = lax.rsqrt(square)
    return (
        noise_level,
        scale_in,
        1.0 / square,
        noise_level * scale_in,
        square / (noise_level * noise_level),
    )


def cond_features(noise_level):
    frequencies = 1.0 + jnp.arange(COND // 2).astype(jnp.float32)
    phases = jnp.log(noise_level) * frequencies
    return jnp.concatenate([jnp.sin(phases), jnp.cos(phases)])


def lat_weights(first_row, row_count, pixel_total):
    row_ids = (first_row + jnp.arange(row_count, dtype=jnp.int32)).astype(jnp.float32)
    return jnp.cos(math.pi * ((row_ids + 0.5) / pixel_total - 0.5))


def norm_stats(values):
    centred = values - jnp.mean(values, axis=-1, keepdims=True)
    inverse = lax.rsqrt(jnp.mean(centred * centred, axis=-1, keepdims=True) + 1e-05)
    return (centred * inverse, inverse)


def norm_back(grad_normed, normed, inverse):
    first_mean = jnp.mean(grad_normed, axis=-1, keepdims=True)
    second_mean = jnp.mean(grad_normed * normed, axis=-1, keepdims=True)
    return inverse * (grad_normed - first_mean - normed * second_mean)


def silu_slope(values):
    sigmoid_values = jax.nn.sigmoid(values)
    return sigmoid_values * (1.0 + values * (1.0 - sigmoid_values))


def contract_rows(left, right):
    return lax.dot_general(
        left, right, (((0,), (0,)), ((), ())), preferred_element_type=jnp.float32
    )


def contract_last(left, right):
    return lax.dot_general(
        left, right, (((1,), (1,)), ((), ())), preferred_element_type=jnp.float32
    )


def axis_bits(axis_name):
    bits = []
    reach = 1
    while reach < lax.axis_size(axis_name):
        bits.append((axis_name, len(bits)))
        reach *= 2
    return bits


def sum_stages():
    wide_bits = len(axis_bits("wide"))
    stages = [("wide", 0, 1)]
    first = 1
    while first < wide_bits:
        stages.append(("wide", first, min(2, wide_bits - first)))
        first += 2
    stages.append(("narrow", 0, len(axis_bits("narrow"))))
    return stages


def partner_swap(values, axis_name, distance):
    size = lax.axis_size(axis_name)
    return lax.ppermute(values, axis_name, [(i, i ^ distance) for i in range(size)])


def scatter_stage(values, stage, sent_type):
    axis_name, first, width = stage
    members = 1 << width
    block = values.shape[0] // members
    mine = (lax.axis_index(axis_name) >> first) & (members - 1)
    arrived = [
        partner_swap(
            lax.dynamic_slice_in_dim(values, (mine ^ far) * block, block, 0).astype(sent_type),
            axis_name,
            far << first,
        )
        for far in range(1, members)
    ]
    values = lax.dynamic_slice_in_dim(values, mine * block, block, 0)
    for piece in arrived:
        values = values + piece.astype(jnp.float32)
    return values


def gather_stage(values, stage):
    axis_name, first, width = stage
    members = 1 << width
    mine = (lax.axis_index(axis_name) >> first) & (members - 1)
    pieces = [values] + [
        partner_swap(values, axis_name, far << first) for far in range(1, members)
    ]
    for bit in range(width):
        is_high = ((mine >> bit) & 1) == 1
        step = 1 << bit
        pieces = [
            jnp.where(is_high, pieces[place ^ step], pieces[place]) for place in range(members)
        ]
    return jnp.concatenate(pieces, axis=0)


def sum_steps(sent_type):
    stages = sum_stages()
    steps = [functools.partial(scatter_stage, stage=s, sent_type=sent_type) for s in stages]
    steps.append(lambda values: gather_stage(values.astype(sent_type), stages[-1]))
    return steps + [functools.partial(gather_stage, stage=s) for s in stages[-2::-1]]


def ring_slots(values):
    size = lax.axis_size("narrow")
    slots = [values]
    for shift in range(1, size):
        slots.append(
            lax.ppermute(values, "narrow", [((i + shift) % size, i) for i in range(size)])
        )
    return slots


def line_slots(values):
    size = lax.axis_size("narrow")
    pos = lax.axis_index("narrow")
    from_low, from_high = values, values
    arrived = {}
    slots = [(values, pos)]
    orders = [
        sorted((s for s in range(size) if s != n), key=lambda s, n=n: (abs(s - n), s < n))
        for n in range(size)
    ]
    for step in range(size - 1):
        from_low = lax.ppermute(from_low, "narrow", [(i, i + 1) for i in range(step, size - 1)])
        from_high = lax.ppermute(
            from_high, "narrow", [(i, i - 1) for i in range(1, size - step)]
        )
        arrived[-1 - step] = from_low
        arrived[1 + step] = from_high
        offsets = [orders[n][step] - n for n in range(size)]
        chosen = arrived[offsets[0]]
        for offset in sorted(set(offsets) - {offsets[0]}):
            here = functools.reduce(
                jnp.logical_or, [pos == n for n in range(size) if offsets[n] == offset]
            )
            chosen = jnp.where(here, arrived[offset], chosen)
        slots.append((chosen, pos + jnp.array(offsets, jnp.int32)[pos]))
    return slots


def ring_sum(parts):
    size = lax.axis_size("narrow")
    total = parts[0]
    for shift in range(1, size):
        arrived = lax.ppermute(
            parts[shift].astype(jnp.bfloat16),
            "narrow",
            [(i, (i + shift) % size) for i in range(size)],
        )
        total = total + arrived.astype(jnp.float32)
    return total


def own_rows(blocks):
    rows = blocks.shape[1] // lax.axis_size("wide")
    return lax.dynamic_slice_in_dim(blocks, lax.axis_index("wide") * rows, rows, 1)


def spread_wide(across):
    whole = lax.all_gather(across, "wide", axis=0)
    count = whole.shape[2]
    return whole.transpose(2, 1, 0, 3, 4).reshape(count, -1, whole.shape[4])


def near_gather(own):
    size = lax.axis_size("narrow")
    pos = lax.axis_index("narrow")
    across = jnp.zeros((size,) + own.shape, own.dtype)
    for shift, piece in enumerate(ring_slots(own)):
        across = lax.dynamic_update_slice_in_dim(
            across, piece[None], (pos + shift) % size, 0
        )
    return across


VMEM_LIMIT = 60 * 1024 * 1024
SCORE_SCALE = math.log2(math.e) / math.sqrt(HEAD_WIDTH)
MASKED = -1e30


def kernel_params():
    return pltpu.CompilerParams(vmem_limit_bytes=VMEM_LIMIT)


def count_kernel(ids_ref, out_ref):
    first = pl.program_id(0) * out_ref.shape[1]
    columns = lax.broadcasted_iota(jnp.int32, out_ref.shape, 1).astype(jnp.int16)
    ids = (ids_ref[...] - first).astype(jnp.int16)
    one = jnp.ones(out_ref.shape, jnp.bfloat16)
    zero = jnp.zeros(out_ref.shape, jnp.bfloat16)
    total = zero
    for slot in range(ids.shape[1]):
        total = total + jnp.where(ids[:, slot : slot + 1] == columns, one, zero)
    out_ref[...] = total


def count_matrix(ids, column_count, rows=1024, columns=2048):
    row_count, slots = ids.shape
    rows = min(rows, row_count)
    columns = min(columns, column_count)
    return pl.pallas_call(
        count_kernel,
        grid=(column_count // columns, row_count // rows),
        in_specs=[pl.BlockSpec((rows, slots), lambda j, i: (i, 0))],
        out_specs=pl.BlockSpec((rows, columns), lambda j, i: (i, j)),
        out_shape=jax.ShapeDtypeStruct((row_count, column_count), jnp.bfloat16),
        cost_estimate=pl.CostEstimate(
            flops=4 * slots * row_count * column_count,
            bytes_accessed=2 * row_count * column_count,
            transcendentals=0,
        ),
        compiler_params=kernel_params(),
    )(ids)


def bias_kernel(row_ref, lane_ref, out_ref):
    groups, width = row_ref.shape
    blocks = out_ref.shape[1] // 128
    row_iota = lax.broadcasted_iota(jnp.int32, (8 * blocks, width), 0)
    lane_iota = lax.broadcasted_iota(jnp.int32, (128, width), 0)
    for group in range(groups):
        left = jnp.where(row_iota == row_ref[group : group + 1, :], 1.0, 0.0)
        right = jnp.where(lane_iota == lane_ref[group : group + 1, :], 1.0, 0.0)
        counts = contract_last(left.astype(jnp.bfloat16), right.astype(jnp.bfloat16))
        bias = jnp.where(counts > 0.5, jnp.log2(counts), MASKED)
        for block in range(blocks):
            out_ref[group * 8 : (group + 1) * 8, block * 128 : (block + 1) * 128] = bias[
                block * 8 : (block + 1) * 8, :
            ]


def count_bias(ids, total, per_step=32):
    row_count, slots = ids.shape
    groups = row_count // 8
    member = (jnp.arange(row_count, dtype=jnp.int32) % 8)[:, None]
    row_keys = ((ids // 128) * 8 + member).reshape(groups, 8 * slots)
    lane_keys = (ids % 128).reshape(groups, 8 * slots)
    spec = pl.BlockSpec((per_step, 8 * slots), lambda i: (i, 0))
    return pl.pallas_call(
        bias_kernel,
        grid=(groups // per_step,),
        in_specs=[spec, spec],
        out_specs=pl.BlockSpec((8 * per_step, total), lambda i: (i, 0)),
        out_shape=jax.ShapeDtypeStruct((row_count, total), jnp.float32),
        cost_estimate=pl.CostEstimate(
            flops=16 * row_count * total, bytes_accessed=4 * row_count * total, transcendentals=0
        ),
        compiler_params=kernel_params(),
    )(row_keys, lane_keys)


def attend_kernel(chunk, q_ref, k_ref, v_ref, bias_ref, att_ref, mass_ref, score_ref):
    q = q_ref[...]
    total = k_ref.shape[0]
    top = None
    for start in range(0, total, chunk):
        part = pl.ds(start, chunk)
        scores = contract_last(q, k_ref[part, :]) * SCORE_SCALE + bias_ref[:, part]
        score_ref[:, part] = scores
        highest = jnp.max(scores, axis=1, keepdims=True)
        top = highest if top is None else jnp.maximum(top, highest)
    mass = jnp.zeros((q.shape[0], 1), jnp.float32)
    attended = jnp.zeros(att_ref.shape, jnp.float32)
    for start in range(0, total, chunk):
        part = pl.ds(start, chunk)
        raised = jnp.exp2(score_ref[:, part] - top)
        mass = mass + jnp.sum(raised, axis=1, keepdims=True)
        attended = attended + jnp.dot(
            raised.astype(jnp.bfloat16), v_ref[part, :], preferred_element_type=jnp.float32
        )
    att_ref[...] = attended / mass
    mass_ref[...] = jnp.broadcast_to(top + jnp.log2(mass), mass_ref.shape)


def attend(queries, pairs, bias, rows=256, chunk=512):
    row_count = queries.shape[0]
    total = pairs.shape[0]
    block = pl.BlockSpec((rows, HEAD_WIDTH), lambda h, r: (r, h))
    return pl.pallas_call(
        functools.partial(attend_kernel, chunk),
        grid=(HEADS, row_count // rows),
        in_specs=[
            block,
            pl.BlockSpec((total, HEAD_WIDTH), lambda h, r: (0, h)),
            pl.BlockSpec((total, HEAD_WIDTH), lambda h, r: (0, HEADS + h)),
            pl.BlockSpec((rows, total), lambda h, r: (r, 0)),
        ],
        out_specs=[block, block],
        out_shape=[jax.ShapeDtypeStruct(queries.shape, jnp.float32)] * 2,
        scratch_shapes=[pltpu.VMEM((rows, total), jnp.float32)],
        cost_estimate=pl.CostEstimate(
            flops=16 * row_count * total * HEAD_WIDTH * HEADS,
            bytes_accessed=16 * row_count * total,
            transcendentals=HEADS * row_count * total,
        ),
        compiler_params=kernel_params(),
    )(queries, pairs, pairs, bias)


def attend_back_kernel(
    chunk,
    q_ref,
    k_ref,
    v_ref,
    bias_ref,
    mass_ref,
    att_ref,
    g_ref,
    dq_ref,
    dk_ref,
    dv_ref,
    dk_sum,
    dv_sum,
):
    step = pl.program_id(1)
    q = q_ref[...]
    g = g_ref[...]
    total = k_ref.shape[0]
    mass = mass_ref[:, :1]
    inner = jnp.sum(att_ref[...] * g.astype(jnp.float32), axis=1, keepdims=True)

    @pl.when(step == 0)
    def _():
        dk_sum[...] = jnp.zeros_like(dk_sum)
        dv_sum[...] = jnp.zeros_like(dv_sum)

    dq = jnp.zeros(q.shape, jnp.float32)
    for start in range(0, total, chunk):
        part = pl.ds(start, chunk)
        k = k_ref[part, :]
        v = v_ref[part, :]
        prob = jnp.exp2(contract_last(q, k) * SCORE_SCALE + (bias_ref[:, part] - mass))
        grad_scores = (prob * (contract_last(g, v) - inner)).astype(jnp.bfloat16)
        dq = dq + jnp.dot(grad_scores, k, preferred_element_type=jnp.float32)
        dk_sum[part, :] += contract_rows(grad_scores, q)
        dv_sum[part, :] += contract_rows(prob.astype(jnp.bfloat16), g)
    shrink = 1.0 / math.sqrt(HEAD_WIDTH)
    dq_ref[...] = (dq * shrink).astype(jnp.bfloat16)

    @pl.when(step == pl.num_programs(1) - 1)
    def _():
        dk_ref[...] = (dk_sum[...] * shrink).astype(jnp.bfloat16)
        dv_ref[...] = dv_sum[...].astype(jnp.bfloat16)


def attend_back(queries, pairs, bias, mass, attended, grads, rows=1024, chunk=256):
    row_count = queries.shape[0]
    total = pairs.shape[0]
    rows = min(rows, row_count)
    block = pl.BlockSpec((rows, HEAD_WIDTH), lambda h, r: (r, h))
    column = pl.BlockSpec((total, HEAD_WIDTH), lambda h, r: (0, h))
    key_shape = jax.ShapeDtypeStruct((total, LATENT_WIDTH), jnp.bfloat16)
    return pl.pallas_call(
        functools.partial(attend_back_kernel, chunk),
        grid=(HEADS, row_count // rows),
        in_specs=[
            block,
            column,
            pl.BlockSpec((total, HEAD_WIDTH), lambda h, r: (0, HEADS + h)),
            pl.BlockSpec((rows, total), lambda h, r: (r, 0)),
            block,
            block,
            block,
        ],
        out_specs=[block, column, column],
        out_shape=[jax.ShapeDtypeStruct(queries.shape, jnp.bfloat16), key_shape, key_shape],
        scratch_shapes=[pltpu.VMEM((total, HEAD_WIDTH), jnp.float32)] * 2,
        cost_estimate=pl.CostEstimate(
            flops=24 * row_count * total * HEAD_WIDTH * HEADS,
            bytes_accessed=16 * row_count * total,
            transcendentals=HEADS * row_count * total,
        ),
        compiler_params=kernel_params(),
    )(queries, pairs, pairs, bias, mass, attended, grads)


def gather_kernel(sub, ids_ref, pixel_ref, *rest):
    out_ref = rest[-1]
    pixels = pixel_ref[...]
    columns = lax.broadcasted_iota(jnp.int32, (sub, pixels.shape[0]), 1).astype(jnp.int16)
    one = jnp.ones(columns.shape, jnp.bfloat16)
    zero = jnp.zeros(columns.shape, jnp.bfloat16)
    for block in range(out_ref.shape[0] // sub):
        part = pl.ds(block * sub, sub)
        ids = ids_ref[part, :].astype(jnp.int16)
        counts = zero
        for slot in range(ids.shape[1]):
            counts = counts + jnp.where(ids[:, slot : slot + 1] == columns, one, zero)
        rows = jnp.dot(counts, pixels, preferred_element_type=jnp.float32)
        if len(rest) == 2:
            rows = rows + rest[0][part, :]
        out_ref[part, :] = rows


def gather_sum(ids, pixels, earlier, rows=1024, sub=256):
    row_count, slots = ids.shape
    pixel_count, width = pixels.shape
    block = pl.BlockSpec((rows, width), lambda i: (i, 0))
    more = [] if earlier is None else [earlier]
    return pl.pallas_call(
        functools.partial(gather_kernel, sub),
        grid=(row_count // rows,),
        in_specs=[
            pl.BlockSpec((rows, slots), lambda i: (i, 0)),
            pl.BlockSpec((pixel_count, width), lambda i: (0, 0)),
        ]
        + [block] * len(more),
        out_specs=block,
        out_shape=jax.ShapeDtypeStruct((row_count, width), jnp.float32),
        cost_estimate=pl.CostEstimate(
            flops=2 * row_count * pixel_count * width,
            bytes_accessed=12 * row_count * width,
            transcendentals=0,
        ),
        compiler_params=kernel_params(),
    )(ids, pixels, *more)


def scatter_kernel(chunk, ids_ref, g_ref, pre_ref, feature_ref, grad_ref, bias_ref):
    step = pl.program_id(0)
    rows = pre_ref.shape[0]
    pixel_ids = lax.broadcasted_iota(jnp.int32, (rows, chunk), 0).astype(jnp.int16)
    one = jnp.ones((rows, chunk), jnp.bfloat16)
    zero = jnp.zeros((rows, chunk), jnp.bfloat16)
    spread = jnp.zeros(pre_ref.shape, jnp.float32)
    for start in range(0, g_ref.shape[0], chunk):
        part = pl.ds(start, chunk)
        counts = zero
        for slot in range(ids_ref.shape[0]):
            ids = jnp.broadcast_to(ids_ref[slot : slot + 1, part] - step * rows, (rows, chunk))
            counts = counts + jnp.where(ids.astype(jnp.int16) == pixel_ids, one, zero)
        spread = spread + jnp.dot(counts, g_ref[part, :], preferred_element_type=jnp.float32)
    pre = pre_ref[...]
    sigmoid_values = 1.0 / (1.0 + jnp.exp(-pre))
    lowered = (spread * (sigmoid_values * (1.0 + pre * (1.0 - sigmoid_values)))).astype(
        jnp.bfloat16
    )

    @pl.when(step == 0)
    def _():
        grad_ref[...] = jnp.zeros_like(grad_ref)
        bias_ref[...] = jnp.zeros_like(bias_ref)

    grad_ref[...] += jnp.dot(feature_ref[...], lowered, preferred_element_type=jnp.float32)
    bias_ref[...] += jnp.sum(lowered.astype(jnp.float32), axis=0, keepdims=True)


def scatter_sum(ids, grads, pre, features, rows=512, chunk=1024):
    slots, node_count = ids.shape
    pixel_count, width = pre.shape
    channels = features.shape[0]
    return pl.pallas_call(
        functools.partial(scatter_kernel, chunk),
        grid=(pixel_count // rows,),
        in_specs=[
            pl.BlockSpec((slots, node_count), lambda i: (0, 0)),
            pl.BlockSpec((node_count, width), lambda i: (0, 0)),
            pl.BlockSpec((rows, width), lambda i: (i, 0)),
            pl.BlockSpec((channels, rows), lambda i: (0, i)),
        ],
        out_specs=[
            pl.BlockSpec((channels, width), lambda i: (0, 0)),
            pl.BlockSpec((1, width), lambda i: (0, 0)),
        ],
        out_shape=[
            jax.ShapeDtypeStruct((channels, width), jnp.float32),
            jax.ShapeDtypeStruct((1, width), jnp.float32),
        ],
        cost_estimate=pl.CostEstimate(
            flops=2 * node_count * pixel_count * width,
            bytes_accessed=8 * pixel_count * width,
            transcendentals=pixel_count * width,
        ),
        compiler_params=kernel_params(),
    )(ids, grads, pre, features)


def split_low(values):
    upper = values.astype(jnp.bfloat16)
    return upper, (values - upper.astype(jnp.float32)).astype(jnp.bfloat16)


def plain_dot(left, right):
    return jnp.dot(left, right, preferred_element_type=jnp.float32)


def triple_dot(left, right, dot=plain_dot):
    return dot(left[0], right[0]) + (dot(left[0], right[1]) + dot(left[1], right[0]))


def muon_kernel(factor_ref, pos_ref, mom_ref, attn_ref, rest_ref, moment_ref, turned_ref, full_ref):
    matrix = pl.program_id(0)
    factor = factor_ref[0, 0]
    own, width = moment_ref.shape[1:]
    gram = jnp.zeros((width, width), jnp.float32)
    for start in range(0, mom_ref.shape[1], own):
        part = pl.ds(start, own)
        grads = jnp.where(
            matrix == 0,
            attn_ref[part, :].astype(jnp.float32),
            rest_ref[part, :].astype(jnp.float32),
        )
        moment = muon_decay * mom_ref[0, part, :] + factor * grads
        full_ref[part, :] = moment
        halves = split_low(moment)
        gram = gram + triple_dot(halves, halves, contract_rows)
    mine = full_ref[pl.ds(pos_ref[0, 0] * own, own), :]
    moment_ref[0] = mine
    row_ids = lax.broadcasted_iota(jnp.int32, gram.shape, 0)
    eye = jnp.where(row_ids == lax.broadcasted_iota(jnp.int32, gram.shape, 1), 1.0, 0.0)
    trace = jnp.sum(jnp.sum(gram * eye, axis=1, keepdims=True), axis=0, keepdims=True)
    scale = 1.0 / (jnp.sqrt(trace) + 1e-07)
    gram = gram * (scale * scale)
    turned = mine * scale
    for iteration in range(NS_ITERS):
        gram_halves = split_low(gram)
        poly = coef_a * eye + coef_b * gram + coef_c * triple_dot(gram_halves, gram_halves)
        poly_halves = split_low(poly)
        turned = triple_dot(split_low(turned), poly_halves)
        if iteration < NS_ITERS - 1:
            gram = triple_dot(poly_halves, split_low(triple_dot(poly_halves, gram_halves)))
    turned_ref[0] = turned


def muon_parts(factor, pos, mom_full, sum_attn, sum_rest, own):
    matrices, rows, width = mom_full.shape
    block = pl.BlockSpec((1, own, width), lambda i: (i, 0, 0))
    scalar = pl.BlockSpec(memory_space=pltpu.SMEM)
    shape = jax.ShapeDtypeStruct((matrices, own, width), jnp.float32)
    return pl.pallas_call(
        muon_kernel,
        grid=(matrices,),
        in_specs=[
            scalar,
            scalar,
            pl.BlockSpec((1, rows, width), lambda i: (i, 0, 0)),
            pl.BlockSpec((rows, width), lambda i: (0, 0)),
            pl.BlockSpec((rows, width), lambda i: (jnp.maximum(i - 1, 0), 0)),
        ],
        out_specs=[block, block],
        out_shape=[shape, shape],
        scratch_shapes=[pltpu.VMEM((rows, width), jnp.float32)],
        cost_estimate=pl.CostEstimate(
            flops=100 * matrices * width**3, bytes_accessed=8 * matrices * rows * width, transcendentals=0
        ),
        compiler_params=kernel_params(),
    )(factor.reshape(1, 1), pos.reshape(1, 1), mom_full, sum_attn, sum_rest)


def adam_update(weight, grad, first, second):
    first_new = beta_one * first + (1.0 - beta_one) * grad
    second_new = beta_two * second + (1.0 - beta_two) * grad * grad
    first_hat = first_new / (1.0 - beta_one**STEP_NUMBER)
    second_hat = second_new / (1.0 - beta_two**STEP_NUMBER)
    weight_new = weight - adam_rate * (
        first_hat / (jnp.sqrt(second_hat) + adam_eps) + decay_rate * weight
    )
    return (weight_new, first_new, second_new)


def on_device(
    prior_states,
    target,
    noise_draw,
    level_index,
    g2m_edges,
    neighbours,
    m2g_edges,
    valid_mask,
    channel_weights,
    w_embed,
    w_cond,
    w_attn,
    w_up,
    w_down,
    w_dec,
    biases,
    mom_attn,
    mom_up,
    mom_down,
    m_embed,
    v_embed,
    m_cond,
    v_cond,
    m_dec,
    v_dec,
    m_bias,
    v_bias,
    ema_embed,
    ema_cond,
    ema_attn,
    ema_up,
    ema_down,
    ema_dec,
    ema_bias,
):
    narrow_pos = lax.axis_index("narrow")
    narrow_count = lax.axis_size("narrow")
    pixel_local = valid_mask.shape[1]
    node_local = neighbours.shape[1]
    pixel_total = pixel_local * narrow_count
    node_total = node_local * narrow_count
    embed_low = w_embed.astype(jnp.bfloat16)
    dec_low = w_dec.astype(jnp.bfloat16)
    bias_embed = biases[:LATENT_WIDTH]
    bias_up = biases[LATENT_WIDTH : LATENT_WIDTH + FF]
    bias_out = biases[LATENT_WIDTH + FF :]
    noise_level, scale_in, skip_scale, out_scale, loss_scale = sigma_terms(level_index[0])
    target_rows = target[0].astype(jnp.float32)
    noisy = target_rows + noise_level * noise_draw[0].astype(jnp.float32)
    features = jnp.concatenate(
        [prior_states[0, 0], prior_states[0, 1], (scale_in * noisy).astype(jnp.bfloat16)], axis=0
    )
    g2m_rows = jnp.concatenate(ring_slots(g2m_edges[0].T), axis=1)
    g2m_cols = g2m_rows.T
    feature_slots = line_slots(features)
    low_blocks = jnp.stack([w_attn.T, w_up.T, w_down]).astype(jnp.bfloat16)
    weight_full = spread_wide(near_gather(own_rows(low_blocks)))
    attn_rows, up_rows, down_full = weight_full[0], weight_full[1], weight_full[2]
    lat_weight = lat_weights(narrow_pos * pixel_local, pixel_local, pixel_total)
    pixel_weight = lat_weight * valid_mask[0].astype(jnp.float32)
    near_ids = (neighbours[0] - narrow_pos * node_local) % node_total
    m2g_ids = (m2g_edges[0] - narrow_pos * node_local) % node_total
    near_bias = count_bias(near_ids, node_total)
    m2g_counts = count_matrix(m2g_ids, node_total)

    embed_pres = []
    node_in = None
    for features_here, source in feature_slots:
        embed_pre = contract_rows(features_here, embed_low) + bias_embed
        embedded = jax.nn.silu(embed_pre).astype(jnp.bfloat16)
        node_in = gather_sum(g2m_cols - source * pixel_local, embedded, node_in)
        embed_pres.append(embed_pre)
    node_in = node_in / G2M_K
    conditioning = cond_features(noise_level)
    modulation = jnp.dot(conditioning, w_cond, precision=highest_precision)
    gain_one = 1.0 + modulation[:LATENT_WIDTH]
    gain_two = 1.0 + modulation[2 * LATENT_WIDTH : 3 * LATENT_WIDTH]
    normed_one, inverse_one = norm_stats(node_in)
    attn_in = (normed_one * gain_one + modulation[LATENT_WIDTH : 2 * LATENT_WIDTH]).astype(
        jnp.bfloat16
    )
    attn_own = attn_in[:node_local]
    query_map = attn_rows[:LATENT_WIDTH]
    pair_map = attn_rows[LATENT_WIDTH : 3 * LATENT_WIDTH]
    proj_map = attn_rows[3 * LATENT_WIDTH :]
    query_rows = contract_last(attn_own, query_map).astype(jnp.bfloat16)
    pair_rows = contract_last(attn_in, pair_map).astype(jnp.bfloat16)
    mom_blocks = jnp.stack([mom_attn.T, mom_up.T, mom_down])
    mom_blocks, pair_rows = lax.optimization_barrier((mom_blocks, pair_rows))
    mom_full = spread_wide(lax.all_gather(own_rows(mom_blocks), "narrow", axis=0))

    attended, mass = attend(query_rows, pair_rows, near_bias)
    attended_rows = attended.astype(jnp.bfloat16)
    node_mid = node_in[:node_local] + contract_last(attended_rows, proj_map)
    normed_two, inverse_two = norm_stats(node_mid)
    mlp_in = (normed_two * gain_two + modulation[3 * LATENT_WIDTH :]).astype(jnp.bfloat16)
    up_pre = contract_last(mlp_in, up_rows) + bias_up
    hidden = jax.nn.silu(up_pre).astype(jnp.bfloat16)
    node_out = node_mid + jnp.dot(hidden, down_full, preferred_element_type=jnp.float32)
    node_low = node_out.astype(jnp.bfloat16)
    node_raw = lax.dot_general(
        dec_low, node_low, (((0,), (1,)), ((), ())), preferred_element_type=jnp.float32
    ).astype(jnp.bfloat16)
    all_raw = jnp.concatenate(ring_slots(node_raw), axis=1)
    raw_output = contract_last(all_raw, m2g_counts) / M2G_K + bias_out[:, None]
    errors = skip_scale * noisy + out_scale * raw_output - target_rows
    weighted = channel_weights[:, None] * pixel_weight[None, :]
    loss_local = loss_scale * jnp.sum(weighted * errors * errors)
    grad_raw = (2.0 * loss_scale * out_scale * weighted * errors).astype(jnp.bfloat16)
    grad_out_bias = jnp.sum(grad_raw.astype(jnp.float32), axis=1)
    raw_spread = jnp.dot(grad_raw, m2g_counts, preferred_element_type=jnp.float32)
    grad_node_raw = (
        ring_sum(
            [
                raw_spread[:, slot * node_local : (slot + 1) * node_local]
                for slot in range(narrow_count)
            ]
        )
        / M2G_K
    )
    grad_dec = lax.dot_general(
        node_low.astype(jnp.float32),
        grad_node_raw,
        (((0,), (1,)), ((), ())),
        precision=highest_precision,
    )
    grad_node_out = lax.dot_general(
        grad_node_raw,
        dec_low.astype(jnp.float32),
        (((0,), (1,)), ((), ())),
        precision=highest_precision,
    )
    grad_mlp = grad_node_out.astype(jnp.bfloat16)
    grad_down = contract_rows(hidden, grad_mlp)
    grad_hidden = contract_last(grad_mlp, down_full)
    grad_up_pre = (grad_hidden * silu_slope(up_pre)).astype(jnp.bfloat16)
    grad_up_bias = jnp.sum(grad_up_pre.astype(jnp.float32), axis=0)
    grad_up = contract_rows(grad_up_pre, mlp_in)
    grad_mlp_in = plain_dot(grad_up_pre, up_rows)
    grad_node_mid = grad_node_out + norm_back(grad_mlp_in * gain_two, normed_two, inverse_two)
    grad_proj_out = grad_node_mid.astype(jnp.bfloat16)
    grad_proj = contract_rows(grad_proj_out, attended_rows)
    early = jnp.concatenate([grad_up, grad_down, grad_proj], axis=0).astype(jnp.bfloat16)
    early = lax.psum(early, ("wide", "narrow"))
    gradient_attended = plain_dot(grad_proj_out, proj_map).astype(jnp.bfloat16)
    grad_query_rows, grad_key_rows, grad_value_rows = attend_back(
        query_rows, pair_rows, near_bias, mass, attended, gradient_attended
    )
    grad_qkv = jnp.concatenate(
        [
            contract_rows(grad_query_rows, attn_own),
            contract_rows(grad_key_rows, attn_in),
            contract_rows(grad_value_rows, attn_in),
        ],
        axis=0,
    )
    grad_attn_in = plain_dot(grad_key_rows, pair_map[:LATENT_WIDTH])
    grad_attn_in = grad_attn_in + plain_dot(grad_value_rows, pair_map[LATENT_WIDTH:])
    grad_attn_in = grad_attn_in.at[:node_local].add(plain_dot(grad_query_rows, query_map))
    grad_node_in = norm_back(grad_attn_in * gain_one, normed_one, inverse_one)
    grad_node_in = grad_node_in.at[:node_local].add(grad_node_mid)
    grad_modulation = jnp.concatenate(
        [
            jnp.sum(grad_attn_in * normed_one, axis=0),
            jnp.sum(grad_attn_in, axis=0),
            jnp.sum(grad_mlp_in * normed_two, axis=0),
            jnp.sum(grad_mlp_in, axis=0),
        ]
    )
    grad_cond = conditioning[:, None] * grad_modulation[None, :]
    node_grads = (grad_node_in / G2M_K).astype(jnp.bfloat16)
    grad_embed = None
    grad_embed_bias = None
    steps = sum_steps(jnp.bfloat16)
    grad_qkv = steps[0](grad_qkv)
    for place, (features_here, source) in enumerate(feature_slots):
        node_grads, grad_qkv = lax.optimization_barrier((node_grads, grad_qkv))
        if place + 1 < len(steps):
            grad_qkv = steps[place + 1](grad_qkv)
        embed_part, bias_part = scatter_sum(
            g2m_rows - source * pixel_local, node_grads, embed_pres[place], features_here
        )
        grad_embed = embed_part if grad_embed is None else grad_embed + embed_part
        grad_embed_bias = bias_part if grad_embed_bias is None else grad_embed_bias + bias_part
    for step in steps[len(feature_slots) + 1 :]:
        grad_qkv = step(grad_qkv)

    width = LATENT_WIDTH
    channels = w_dec.shape[1]
    late_rows = jnp.concatenate(
        [
            grad_embed,
            grad_embed_bias.reshape(1, width),
            grad_up_bias.reshape(FF // width, width),
            jnp.pad(
                jnp.concatenate(
                    [grad_out_bias, loss_local.reshape(1), jnp.sum(pixel_weight).reshape(1)]
                ),
                (0, width - channels - 2),
            ).reshape(1, width),
            grad_dec.T,
        ]
        + [grad_cond[:, place * width : (place + 1) * width] for place in range(4)],
        axis=0,
    )
    device_count = lax.axis_size("wide") * narrow_count
    late_rows = jnp.pad(late_rows, ((0, -late_rows.shape[0] % (2 * device_count)), (0, 0)))
    for step in sum_steps(jnp.float32):
        late_rows = step(late_rows)
    embed_rows = w_embed.shape[0]
    sum_embed = late_rows[:embed_rows]
    place = embed_rows
    bias_rows = late_rows[place : place + 2 + FF // width].reshape(-1)
    sum_bias = bias_rows[: biases.shape[0]]
    loss_sum = bias_rows[biases.shape[0]]
    weight_total = bias_rows[biases.shape[0] + 1]
    place += 2 + FF // width
    sum_dec = late_rows[place : place + channels].T
    place += channels
    sum_cond = jnp.concatenate(
        [late_rows[place + COND * part : place + COND * (part + 1)] for part in range(4)], axis=1
    )
    sum_attn = jnp.concatenate([grad_qkv, early[2 * FF :]], axis=0)
    square_sum = (
        jnp.sum(sum_embed * sum_embed)
        + jnp.sum(sum_cond * sum_cond)
        + jnp.sum(jnp.square(grad_qkv.astype(jnp.float32)))
        + jnp.sum(jnp.square(early.astype(jnp.float32)))
        + jnp.sum(sum_dec * sum_dec)
        + jnp.sum(sum_bias * sum_bias)
    )
    grad_norm = jnp.sqrt(square_sum) / weight_total
    factor = jnp.minimum(1.0, clip_bound / (grad_norm + 1e-06)) / weight_total
    moments, turned = muon_parts(
        factor, narrow_pos, mom_full, sum_attn, early, w_down.shape[0]
    )
    moment_attn, moment_up, moment_down = moments[0].T, moments[1].T, moments[2]
    attn_orth, up_orth, down_orth = turned[0].T, turned[1].T, turned[2]
    new_attn = (
        w_attn - muon_rate * math.sqrt(max(1.0, LATENT_WIDTH / (4 * LATENT_WIDTH))) * attn_orth
    )
    new_up = w_up - muon_rate * math.sqrt(max(1.0, LATENT_WIDTH / FF)) * up_orth
    new_down = w_down - muon_rate * math.sqrt(max(1.0, FF / LATENT_WIDTH)) * down_orth
    new_embed, first_embed, second_embed = adam_update(
        w_embed, factor * sum_embed, m_embed, v_embed
    )
    new_cond, first_cond, second_cond = adam_update(w_cond, factor * sum_cond, m_cond, v_cond)
    new_dec, first_dec, second_dec = adam_update(w_dec, factor * sum_dec, m_dec, v_dec)
    new_bias, first_bias, second_bias = adam_update(biases, factor * sum_bias, m_bias, v_bias)
    keep_rest = 1.0 - ema_keep
    return (
        new_attn,
        new_up,
        new_down,
        moment_attn,
        moment_up,
        moment_down,
        new_embed,
        new_cond,
        new_dec,
        new_bias,
        first_embed,
        second_embed,
        first_cond,
        second_cond,
        first_dec,
        second_dec,
        first_bias,
        second_bias,
        ema_keep * ema_embed + keep_rest * new_embed,
        ema_keep * ema_cond + keep_rest * new_cond,
        ema_keep * ema_attn + keep_rest * new_attn,
        ema_keep * ema_up + keep_rest * new_up,
        ema_keep * ema_down + keep_rest * new_down,
        ema_keep * ema_dec + keep_rest * new_dec,
        ema_keep * ema_bias + keep_rest * new_bias,
        loss_sum,
        weight_total,
        grad_norm,
    )


def solution(mesh):
    in_specs = (
        P("wide", None, None, "narrow"),
        P("wide", None, "narrow"),
        P("wide", None, "narrow"),
        P("wide"),
        P("wide", "narrow", None),
        P("wide", "narrow", None),
        P("wide", "narrow", None),
        P("wide", "narrow"),
        P(),
        P(),
        P(),
        P(None, "narrow"),
        P(None, "narrow"),
        P("narrow", None),
        P(),
        P(),
        P(None, "narrow"),
        P(None, "narrow"),
        P("narrow", None),
        P(),
        P(),
        P(),
        P(),
        P(),
        P(),
        P(),
        P(),
        P(),
        P(),
        P(None, "narrow"),
        P(None, "narrow"),
        P("narrow", None),
        P(),
        P(),
    )
    out_specs = (
        P(None, "narrow"),
        P(None, "narrow"),
        P("narrow", None),
        P(None, "narrow"),
        P(None, "narrow"),
        P("narrow", None),
        P(),
        P(),
        P(),
        P(),
        P(),
        P(),
        P(),
        P(),
        P(),
        P(),
        P(),
        P(),
        P(),
        P(),
        P(None, "narrow"),
        P(None, "narrow"),
        P("narrow", None),
        P(),
        P(),
        P(),
        P(),
        P(),
    )
    return jax.shard_map(
        on_device, mesh=mesh, in_specs=in_specs, out_specs=out_specs, check_vma=False
    )
```

```python
import functools
import math

import jax
import jax.numpy as jnp
from jax import lax
from jax.experimental import pallas as pl
from jax.experimental.pallas import tpu as pltpu
from jax.sharding import PartitionSpec as P

LATENT_WIDTH = 512
HEADS = 4
HEAD_WIDTH = 128
FF = 2048
COND = 32
NBR = 32
G2M_K = 4
M2G_K = 3
NS_ITERS = 5
SIGMA_LEVELS = 8
STEP_NUMBER = 10


highest_precision = lax.Precision.HIGHEST
sigma_low = 0.25
sigma_high = 4.0
clip_bound = 0.02
muon_rate = 0.5
muon_decay = 0.95
adam_rate = 0.03
beta_one = 0.9
beta_two = 0.95
adam_eps = 1e-08
decay_rate = 0.01
ema_keep = 0.9
coef_a = 3.4445
coef_b = -4.775
coef_c = 2.0315


def sigma_terms(level):
    fraction = level.astype(jnp.float32) / (SIGMA_LEVELS - 1)
    noise_level = sigma_low * (sigma_high / sigma_low) ** fraction
    square = noise_level * noise_level + 1.0
    scale_in = lax.rsqrt(square)
    return (
        noise_level,
        scale_in,
        1.0 / square,
        noise_level * scale_in,
        square / (noise_level * noise_level),
    )


def cond_features(noise_level):
    frequencies = 1.0 + jnp.arange(COND // 2).astype(jnp.float32)
    phases = jnp.log(noise_level) * frequencies
    return jnp.concatenate([jnp.sin(phases), jnp.cos(phases)])


def lat_weights(first_row, row_count, pixel_total):
    row_ids = (first_row + jnp.arange(row_count, dtype=jnp.int32)).astype(jnp.float32)
    return jnp.cos(math.pi * ((row_ids + 0.5) / pixel_total - 0.5))


def norm_stats(values):
    centred = values - jnp.mean(values, axis=-1, keepdims=True)
    inverse = lax.rsqrt(jnp.mean(centred * centred, axis=-1, keepdims=True) + 1e-05)
    return (centred * inverse, inverse)


def norm_back(grad_normed, normed, inverse):
    first_mean = jnp.mean(grad_normed, axis=-1, keepdims=True)
    second_mean = jnp.mean(grad_normed * normed, axis=-1, keepdims=True)
    return inverse * (grad_normed - first_mean - normed * second_mean)


def silu_slope(values):
    sigmoid_values = jax.nn.sigmoid(values)
    return sigmoid_values * (1.0 + values * (1.0 - sigmoid_values))


def contract_rows(left, right):
    return lax.dot_general(
        left, right, (((0,), (0,)), ((), ())), preferred_element_type=jnp.float32
    )


def contract_last(left, right):
    return lax.dot_general(
        left, right, (((1,), (1,)), ((), ())), preferred_element_type=jnp.float32
    )


def axis_bits(axis_name):
    bits = []
    reach = 1
    while reach < lax.axis_size(axis_name):
        bits.append((axis_name, len(bits)))
        reach *= 2
    return bits


def sum_stages():
    wide_bits = len(axis_bits("wide"))
    stages = [("wide", 0, 1)]
    first = 1
    while first < wide_bits:
        stages.append(("wide", first, min(2, wide_bits - first)))
        first += 2
    stages.append(("narrow", 0, len(axis_bits("narrow"))))
    return stages


def partner_swap(values, axis_name, distance):
    size = lax.axis_size(axis_name)
    return lax.ppermute(values, axis_name, [(i, i ^ distance) for i in range(size)])


def joint_pieces(coarse, fine):
    upper = fine.astype(jnp.bfloat16)
    lower = (fine - lax.optimization_barrier(upper).astype(jnp.float32)).astype(jnp.bfloat16)
    return jnp.concatenate([coarse.astype(jnp.bfloat16), upper, lower], axis=1)


def joint_split(pieces, coarse_width):
    coarse = pieces[:, :coarse_width]
    fine_width = (pieces.shape[1] - coarse_width) // 2
    upper = pieces[:, coarse_width : coarse_width + fine_width].astype(jnp.float32)
    return coarse, upper + pieces[:, coarse_width + fine_width :].astype(jnp.float32)


def joint_sum(coarse, fine, beside):
    coarse_width = coarse.shape[1]
    stages = sum_stages()
    for axis_name, first, width in stages:
        members = 1 << width
        block = fine.shape[0] // members
        mine = (lax.axis_index(axis_name) >> first) & (members - 1)
        arrived = []
        for far in range(1, members):
            begin = (mine ^ far) * block
            piece = joint_pieces(
                lax.dynamic_slice_in_dim(coarse, begin, block, 0),
                lax.dynamic_slice_in_dim(fine, begin, block, 0),
            )
            arrived.append(partner_swap(piece, axis_name, far << first))
        coarse = lax.dynamic_slice_in_dim(coarse, mine * block, block, 0)
        fine = lax.dynamic_slice_in_dim(fine, mine * block, block, 0)
        for piece in arrived:
            more_coarse, more_fine = joint_split(piece, coarse_width)
            coarse = coarse + more_coarse.astype(jnp.float32)
            fine = fine + more_fine
    values = joint_pieces(coarse, fine)
    values, beside = lax.optimization_barrier((values, beside))
    for axis_name, first, width in stages[::-1]:
        members = 1 << width
        mine = (lax.axis_index(axis_name) >> first) & (members - 1)
        pieces = [values] + [
            partner_swap(values, axis_name, far << first) for far in range(1, members)
        ]
        for bit in range(width):
            is_high = ((mine >> bit) & 1) == 1
            step = 1 << bit
            pieces = [
                jnp.where(is_high, pieces[place ^ step], pieces[place])
                for place in range(members)
            ]
        values = jnp.concatenate(pieces, axis=0)
    return values, *beside


def ring_slots(values):
    size = lax.axis_size("narrow")
    slots = [values]
    for shift in range(1, size):
        slots.append(
            lax.ppermute(values, "narrow", [((i + shift) % size, i) for i in range(size)])
        )
    return slots


def line_slots(values, use_slot, later):
    size = lax.axis_size("narrow")
    pos = lax.axis_index("narrow")
    from_low, from_high = values, values
    arrived = {}
    orders = [
        sorted((s for s in range(size) if s != n), key=lambda s, n=n: (abs(s - n), s < n))
        for n in range(size)
    ]
    chosen, source = values, pos
    for step in range(size):
        if step < size - 1:
            from_low = lax.ppermute(
                from_low, "narrow", [(i, i + 1) for i in range(step, size - 1)]
            )
            from_high = lax.ppermute(
                from_high, "narrow", [(i, i - 1) for i in range(1, size - step)]
            )
        result = use_slot(chosen, source)
        if step == size - 1:
            return later
        if step == 0:
            result = (result, later)
        from_low, from_high, result = lax.optimization_barrier((from_low, from_high, result))
        if step == 0:
            later = result[1]
        arrived[-1 - step] = from_low
        arrived[1 + step] = from_high
        offsets = [orders[n][step] - n for n in range(size)]
        chosen = arrived[offsets[0]]
        for offset in sorted(set(offsets) - {offsets[0]}):
            here = functools.reduce(
                jnp.logical_or, [pos == n for n in range(size) if offsets[n] == offset]
            )
            chosen = jnp.where(here, arrived[offset], chosen)
        source = pos + jnp.array(offsets, jnp.int32)[pos]


def ring_sum(parts):
    size = lax.axis_size("narrow")
    total = parts[0]
    for shift in range(1, size):
        arrived = lax.ppermute(
            parts[shift].astype(jnp.bfloat16),
            "narrow",
            [(i, (i + shift) % size) for i in range(size)],
        )
        total = total + arrived.astype(jnp.float32)
    return total


VMEM_LIMIT = 60 * 1024 * 1024
SCORE_SCALE = math.log2(math.e) / math.sqrt(HEAD_WIDTH)
MASKED = -1e30


def small_cost():
    return pl.CostEstimate(flops=1 << 20, bytes_accessed=1 << 20, transcendentals=0)


def kernel_params():
    return pltpu.CompilerParams(vmem_limit_bytes=VMEM_LIMIT)


def count_kernel(ids_ref, out_ref):
    first = pl.program_id(0) * out_ref.shape[1]
    columns = lax.broadcasted_iota(jnp.int32, out_ref.shape, 1).astype(jnp.int16)
    ids = (ids_ref[...] - first).astype(jnp.int16)
    one = jnp.ones(out_ref.shape, jnp.bfloat16)
    zero = jnp.zeros(out_ref.shape, jnp.bfloat16)
    total = zero
    for slot in range(ids.shape[1]):
        total = total + jnp.where(ids[:, slot : slot + 1] == columns, one, zero)
    out_ref[...] = total


def count_matrix(ids, column_count, rows=1024, columns=2048):
    row_count, slots = ids.shape
    rows = min(rows, row_count)
    columns = min(columns, column_count)
    return pl.pallas_call(
        count_kernel,
        grid=(column_count // columns, row_count // rows),
        in_specs=[pl.BlockSpec((rows, slots), lambda j, i: (i, 0))],
        out_specs=pl.BlockSpec((rows, columns), lambda j, i: (i, j)),
        out_shape=jax.ShapeDtypeStruct((row_count, column_count), jnp.bfloat16),
        cost_estimate=small_cost(),
        compiler_params=kernel_params(),
    )(ids)


def bias_kernel(row_ref, lane_ref, out_ref):
    groups, width = row_ref.shape
    blocks = out_ref.shape[1] // 128
    row_iota = lax.broadcasted_iota(jnp.int32, (8 * blocks, width), 0)
    lane_iota = lax.broadcasted_iota(jnp.int32, (128, width), 0)
    for group in range(groups):
        left = jnp.where(row_iota == row_ref[group : group + 1, :], 1.0, 0.0)
        right = jnp.where(lane_iota == lane_ref[group : group + 1, :], 1.0, 0.0)
        counts = contract_last(left.astype(jnp.bfloat16), right.astype(jnp.bfloat16))
        bias = jnp.where(counts > 0.5, jnp.log2(counts), MASKED)
        for block in range(blocks):
            out_ref[group * 8 : (group + 1) * 8, block * 128 : (block + 1) * 128] = bias[
                block * 8 : (block + 1) * 8, :
            ]


def count_bias(ids, total, per_step=32):
    row_count, slots = ids.shape
    groups = row_count // 8
    member = (jnp.arange(row_count, dtype=jnp.int32) % 8)[:, None]
    row_keys = ((ids // 128) * 8 + member).reshape(groups, 8 * slots)
    lane_keys = (ids % 128).reshape(groups, 8 * slots)
    spec = pl.BlockSpec((per_step, 8 * slots), lambda i: (i, 0))
    return pl.pallas_call(
        bias_kernel,
        grid=(groups // per_step,),
        in_specs=[spec, spec],
        out_specs=pl.BlockSpec((8 * per_step, total), lambda i: (i, 0)),
        out_shape=jax.ShapeDtypeStruct((row_count, total), jnp.float32),
        cost_estimate=small_cost(),
        compiler_params=kernel_params(),
    )(row_keys, lane_keys)


def attend_kernel(chunk, q_ref, k_ref, v_ref, bias_ref, att_ref, mass_ref, score_ref):
    q = q_ref[...]
    total = k_ref.shape[0]
    top = None
    for start in range(0, total, chunk):
        part = pl.ds(start, chunk)
        scores = contract_last(q, k_ref[part, :]) * SCORE_SCALE + bias_ref[:, part]
        score_ref[:, part] = scores
        highest = jnp.max(scores, axis=1, keepdims=True)
        top = highest if top is None else jnp.maximum(top, highest)
    mass = jnp.zeros((q.shape[0], 1), jnp.float32)
    attended = jnp.zeros(att_ref.shape, jnp.float32)
    for start in range(0, total, chunk):
        part = pl.ds(start, chunk)
        raised = jnp.exp2(score_ref[:, part] - top)
        mass = mass + jnp.sum(raised, axis=1, keepdims=True)
        attended = attended + jnp.dot(
            raised.astype(jnp.bfloat16), v_ref[part, :], preferred_element_type=jnp.float32
        )
    att_ref[...] = attended / mass
    mass_ref[...] = jnp.broadcast_to(top + jnp.log2(mass), mass_ref.shape)


def attend(queries, pairs, bias, rows=256, chunk=512):
    row_count = queries.shape[0]
    total = pairs.shape[0]
    block = pl.BlockSpec((rows, HEAD_WIDTH), lambda h, r: (r, h))
    return pl.pallas_call(
        functools.partial(attend_kernel, chunk),
        grid=(HEADS, row_count // rows),
        in_specs=[
            block,
            pl.BlockSpec((total, HEAD_WIDTH), lambda h, r: (0, h)),
            pl.BlockSpec((total, HEAD_WIDTH), lambda h, r: (0, HEADS + h)),
            pl.BlockSpec((rows, total), lambda h, r: (r, 0)),
        ],
        out_specs=[block, block],
        out_shape=[jax.ShapeDtypeStruct(queries.shape, jnp.float32)] * 2,
        scratch_shapes=[pltpu.VMEM((rows, total), jnp.float32)],
        cost_estimate=small_cost(),
        compiler_params=kernel_params(),
    )(queries, pairs, pairs, bias)


def attend_back_kernel(
    chunk,
    q_ref,
    k_ref,
    v_ref,
    bias_ref,
    mass_ref,
    att_ref,
    g_ref,
    dq_ref,
    dk_ref,
    dv_ref,
    dk_sum,
    dv_sum,
):
    step = pl.program_id(1)
    q = q_ref[...]
    g = g_ref[...]
    total = k_ref.shape[0]
    mass = mass_ref[:, :1]
    inner = jnp.sum(att_ref[...] * g.astype(jnp.float32), axis=1, keepdims=True)

    @pl.when(step == 0)
    def _():
        dk_sum[...] = jnp.zeros_like(dk_sum)
        dv_sum[...] = jnp.zeros_like(dv_sum)

    dq = jnp.zeros(q.shape, jnp.float32)
    for start in range(0, total, chunk):
        part = pl.ds(start, chunk)
        k = k_ref[part, :]
        v = v_ref[part, :]
        prob = jnp.exp2(contract_last(q, k) * SCORE_SCALE + (bias_ref[:, part] - mass))
        grad_scores = (prob * (contract_last(g, v) - inner)).astype(jnp.bfloat16)
        dq = dq + jnp.dot(grad_scores, k, preferred_element_type=jnp.float32)
        dk_sum[part, :] += contract_rows(grad_scores, q)
        dv_sum[part, :] += contract_rows(prob.astype(jnp.bfloat16), g)
    shrink = 1.0 / math.sqrt(HEAD_WIDTH)
    dq_ref[...] = (dq * shrink).astype(jnp.bfloat16)

    @pl.when(step == pl.num_programs(1) - 1)
    def _():
        dk_ref[...] = (dk_sum[...] * shrink).astype(jnp.bfloat16)
        dv_ref[...] = dv_sum[...].astype(jnp.bfloat16)


def attend_back(queries, pairs, bias, mass, attended, grads, rows=1024, chunk=256):
    row_count = queries.shape[0]
    total = pairs.shape[0]
    rows = min(rows, row_count)
    block = pl.BlockSpec((rows, HEAD_WIDTH), lambda h, r: (r, h))
    column = pl.BlockSpec((total, HEAD_WIDTH), lambda h, r: (0, h))
    key_shape = jax.ShapeDtypeStruct((total, LATENT_WIDTH), jnp.bfloat16)
    return pl.pallas_call(
        functools.partial(attend_back_kernel, chunk),
        grid=(HEADS, row_count // rows),
        in_specs=[
            block,
            column,
            pl.BlockSpec((total, HEAD_WIDTH), lambda h, r: (0, HEADS + h)),
            pl.BlockSpec((rows, total), lambda h, r: (r, 0)),
            block,
            block,
            block,
        ],
        out_specs=[block, column, column],
        out_shape=[jax.ShapeDtypeStruct(queries.shape, jnp.bfloat16), key_shape, key_shape],
        scratch_shapes=[pltpu.VMEM((total, HEAD_WIDTH), jnp.float32)] * 2,
        cost_estimate=small_cost(),
        compiler_params=kernel_params(),
    )(queries, pairs, pairs, bias, mass, attended, grads)


def gather_kernel(sub, first_ref, ids_ref, feature_ref, map_ref, bias_ref, *rest):
    out_ref, pixel_ref = rest[-2:]

    @pl.when(pl.program_id(0) == 0)
    def _():
        pre = contract_rows(feature_ref[...], map_ref[...]) + bias_ref[...]
        pixel_ref[...] = (pre / (1.0 + jnp.exp(-pre))).astype(jnp.bfloat16)

    pixels = pixel_ref[...]
    columns = lax.broadcasted_iota(jnp.int32, (sub, pixels.shape[0]), 1).astype(jnp.int16)
    one = jnp.ones(columns.shape, jnp.bfloat16)
    zero = jnp.zeros(columns.shape, jnp.bfloat16)
    for block in range(out_ref.shape[0] // sub):
        part = pl.ds(block * sub, sub)
        ids = (ids_ref[part, :] - first_ref[0, 0]).astype(jnp.int16)
        counts = zero
        for slot in range(ids.shape[1]):
            counts = counts + jnp.where(ids[:, slot : slot + 1] == columns, one, zero)
        rows = jnp.dot(counts, pixels, preferred_element_type=jnp.float32)
        if len(rest) == 3:
            rows = rows + rest[0][part, :]
        out_ref[part, :] = rows


def gather_sum(first, ids, features, embed_map, embed_bias, earlier, rows=1024, sub=256):
    row_count, slots = ids.shape
    channels, pixel_count = features.shape
    width = embed_map.shape[1]
    block = pl.BlockSpec((rows, width), lambda i: (i, 0))
    more = [] if earlier is None else [earlier]
    return pl.pallas_call(
        functools.partial(gather_kernel, sub),
        grid=(row_count // rows,),
        in_specs=[
            pl.BlockSpec(memory_space=pltpu.SMEM),
            pl.BlockSpec((rows, slots), lambda i: (i, 0)),
            pl.BlockSpec((channels, pixel_count), lambda i: (0, 0)),
            pl.BlockSpec((channels, width), lambda i: (0, 0)),
            pl.BlockSpec((1, width), lambda i: (0, 0)),
        ]
        + [block] * len(more),
        out_specs=block,
        out_shape=jax.ShapeDtypeStruct((row_count, width), jnp.float32),
        scratch_shapes=[pltpu.VMEM((pixel_count, width), jnp.bfloat16)],
        cost_estimate=small_cost(),
        compiler_params=kernel_params(),
    )(first.reshape(1, 1), ids, features, embed_map, embed_bias, *more)


def scatter_kernel(
    chunk, first_ref, ids_ref, g_ref, feature_ref, map_ref, shift_ref, grad_ref, bias_ref
):
    step = pl.program_id(0)
    rows = feature_ref.shape[1]
    pixel_ids = lax.broadcasted_iota(jnp.int32, (rows, chunk), 0).astype(jnp.int16)
    one = jnp.ones((rows, chunk), jnp.bfloat16)
    zero = jnp.zeros((rows, chunk), jnp.bfloat16)
    spread = jnp.zeros((rows, g_ref.shape[1]), jnp.float32)
    for start in range(0, g_ref.shape[0], chunk):
        part = pl.ds(start, chunk)
        counts = zero
        for slot in range(ids_ref.shape[0]):
            ids = ids_ref[slot : slot + 1, part] - (first_ref[0, 0] + step * rows)
            ids = jnp.broadcast_to(ids, (rows, chunk))
            counts = counts + jnp.where(ids.astype(jnp.int16) == pixel_ids, one, zero)
        spread = spread + jnp.dot(counts, g_ref[part, :], preferred_element_type=jnp.float32)
    pre = contract_rows(feature_ref[...], map_ref[...]) + shift_ref[...]
    sigmoid_values = 1.0 / (1.0 + jnp.exp(-pre))
    lowered = (spread * (sigmoid_values * (1.0 + pre * (1.0 - sigmoid_values)))).astype(
        jnp.bfloat16
    )

    @pl.when(step == 0)
    def _():
        grad_ref[...] = jnp.zeros_like(grad_ref)
        bias_ref[...] = jnp.zeros_like(bias_ref)

    grad_ref[...] += jnp.dot(feature_ref[...], lowered, preferred_element_type=jnp.float32)
    bias_ref[...] += jnp.sum(lowered.astype(jnp.float32), axis=0, keepdims=True)


def scatter_sum(first, ids, grads, features, embed_map, embed_bias, rows=512, chunk=1024):
    slots, node_count = ids.shape
    width = grads.shape[1]
    channels, pixel_count = features.shape
    return pl.pallas_call(
        functools.partial(scatter_kernel, chunk),
        grid=(pixel_count // rows,),
        in_specs=[
            pl.BlockSpec(memory_space=pltpu.SMEM),
            pl.BlockSpec((slots, node_count), lambda i: (0, 0)),
            pl.BlockSpec((node_count, width), lambda i: (0, 0)),
            pl.BlockSpec((channels, rows), lambda i: (0, i)),
            pl.BlockSpec((channels, width), lambda i: (0, 0)),
            pl.BlockSpec((1, width), lambda i: (0, 0)),
        ],
        out_specs=[
            pl.BlockSpec((channels, width), lambda i: (0, 0)),
            pl.BlockSpec((1, width), lambda i: (0, 0)),
        ],
        out_shape=[
            jax.ShapeDtypeStruct((channels, width), jnp.float32),
            jax.ShapeDtypeStruct((1, width), jnp.float32),
        ],
        cost_estimate=small_cost(),
        compiler_params=kernel_params(),
    )(first.reshape(1, 1), ids, grads, features, embed_map, embed_bias)


def row_norm(sums):
    values = sums * (1.0 / G2M_K)
    centred = values - jnp.mean(values, axis=1, keepdims=True)
    inverse = lax.rsqrt(jnp.mean(centred * centred, axis=1, keepdims=True) + 1e-05)
    return centred * inverse, inverse


def project_kernel(sum_ref, shift_ref, map_ref, attn_ref, query_ref, pair_ref):
    width = sum_ref.shape[1]
    normed, _ = row_norm(sum_ref[...])
    attn_in = (normed * shift_ref[0:1, :] + shift_ref[1:2, :]).astype(jnp.bfloat16)
    attn_ref[...] = attn_in
    for place in range(2):
        part = pl.ds(place * width, width)
        weights = map_ref[pl.ds((place + 1) * width, width), :]
        pair_ref[:, part] = contract_last(attn_in, weights).astype(jnp.bfloat16)

    @pl.when(pl.program_id(0) == 0)
    def _():
        query_ref[...] = contract_last(attn_in, map_ref[pl.ds(0, width), :]).astype(jnp.bfloat16)


def project(sums, shifts, attn_map, rows):
    row_count, width = sums.shape
    block = pl.BlockSpec((rows, width), lambda i: (i, 0))
    return pl.pallas_call(
        project_kernel,
        grid=(row_count // rows,),
        in_specs=[
            block,
            pl.BlockSpec(shifts.shape, lambda i: (0, 0)),
            pl.BlockSpec(attn_map.shape, lambda i: (0, 0)),
        ],
        out_specs=[
            block,
            pl.BlockSpec((rows, width), lambda i: (0, 0)),
            pl.BlockSpec((rows, 2 * width), lambda i: (i, 0)),
        ],
        out_shape=[
            jax.ShapeDtypeStruct((row_count, width), jnp.bfloat16),
            jax.ShapeDtypeStruct((rows, width), jnp.bfloat16),
            jax.ShapeDtypeStruct((row_count, 2 * width), jnp.bfloat16),
        ],
        cost_estimate=small_cost(),
        compiler_params=kernel_params(),
    )(sums, shifts, attn_map)


def project_back_kernel(
    dq_ref,
    dk_ref,
    dv_ref,
    sum_ref,
    attn_ref,
    mid_ref,
    shift_ref,
    map_ref,
    node_ref,
    grad_ref,
    column_ref,
    back_ref,
):
    step = pl.program_id(0)
    width = sum_ref.shape[1]
    attn_in = attn_ref[...]
    dk, dv = dk_ref[...], dv_ref[...]
    back_ref[...] = plain_dot(dk, map_ref[pl.ds(width, width), :]) + plain_dot(
        dv, map_ref[pl.ds(2 * width, width), :]
    )

    @pl.when(step == 0)
    def _():
        grad_ref[...] = jnp.zeros_like(grad_ref)
        column_ref[...] = jnp.zeros_like(column_ref)
        dq = dq_ref[...]
        back_ref[...] += plain_dot(dq, map_ref[pl.ds(0, width), :])
        grad_ref[:, pl.ds(0, width)] = contract_rows(dq, attn_in)

    grad_ref[:, pl.ds(width, width)] += contract_rows(dk, attn_in)
    grad_ref[:, pl.ds(2 * width, width)] += contract_rows(dv, attn_in)
    back = back_ref[...]
    normed, inverse = row_norm(sum_ref[...])
    column_ref[0:1, :] += jnp.sum(back * normed, axis=0, keepdims=True)
    column_ref[1:2, :] += jnp.sum(back, axis=0, keepdims=True)
    grads = back * shift_ref[0:1, :]
    first_mean = jnp.mean(grads, axis=1, keepdims=True)
    second_mean = jnp.mean(grads * normed, axis=1, keepdims=True)
    grads = inverse * (grads - first_mean - normed * second_mean)
    own_share = jnp.where(step == 0, 1.0, 0.0)
    node_ref[...] = ((grads + own_share * mid_ref[...]) * (1.0 / G2M_K)).astype(jnp.bfloat16)


def project_back(dq, dk, dv, sums, attn_in, mid, shifts, attn_map):
    row_count, width = sums.shape
    rows = dq.shape[0]
    block = pl.BlockSpec((rows, width), lambda i: (i, 0))
    own = pl.BlockSpec((rows, width), lambda i: (0, 0))
    return pl.pallas_call(
        project_back_kernel,
        grid=(row_count // rows,),
        in_specs=[
            own,
            block,
            block,
            block,
            block,
            own,
            pl.BlockSpec(shifts.shape, lambda i: (0, 0)),
            pl.BlockSpec(attn_map.shape, lambda i: (0, 0)),
        ],
        out_specs=[
            block,
            pl.BlockSpec((width, 3 * width), lambda i: (0, 0)),
            pl.BlockSpec((8, width), lambda i: (0, 0)),
        ],
        out_shape=[
            jax.ShapeDtypeStruct((row_count, width), jnp.bfloat16),
            jax.ShapeDtypeStruct((width, 3 * width), jnp.float32),
            jax.ShapeDtypeStruct((8, width), jnp.float32),
        ],
        scratch_shapes=[pltpu.VMEM((rows, width), jnp.float32)],
        cost_estimate=small_cost(),
        compiler_params=kernel_params(),
    )(dq, dk, dv, sums, attn_in, mid, shifts, attn_map)


def split_low(values):
    upper = values.astype(jnp.bfloat16)
    return upper, (values - upper.astype(jnp.float32)).astype(jnp.bfloat16)


def plain_dot(left, right):
    return jnp.dot(left, right, preferred_element_type=jnp.float32)


def triple_dot(left, right, dot=plain_dot):
    return dot(left[0], right[0]) + (dot(left[0], right[1]) + dot(left[1], right[0]))


def muon_kernel(choice_ref, factor_ref, mom_ref, qkv_ref, proj_ref, rest_ref, turned_ref, full_ref):
    matrix, pos = choice_ref[0], choice_ref[1]
    factor = factor_ref[0, 0]
    own, width = turned_ref.shape
    gram = jnp.zeros((width, width), jnp.float32)
    for place in range(FF // width):
        part = pl.ds(place * width, width)
        if place < 3:
            first = qkv_ref[:, part]
        else:
            first = proj_ref[...]
        grads = jnp.where(
            matrix == 0, first.astype(jnp.float32), rest_ref[part, :].astype(jnp.float32)
        )
        moment = muon_decay * mom_ref[0, part, :].astype(jnp.float32) + factor * grads
        full_ref[part, :] = moment
        halves = split_low(moment)
        gram = gram + triple_dot(halves, halves, contract_rows)
    row_ids = lax.broadcasted_iota(jnp.int32, gram.shape, 0)
    eye = jnp.where(row_ids == lax.broadcasted_iota(jnp.int32, gram.shape, 1), 1.0, 0.0)
    trace = jnp.sum(jnp.sum(gram * eye, axis=1, keepdims=True), axis=0, keepdims=True)
    scale = 1.0 / (jnp.sqrt(trace) + 1e-07)
    gram = gram * (scale * scale)
    turned = full_ref[pl.ds(pos * own, own), :] * scale
    for iteration in range(NS_ITERS):
        gram_halves = split_low(gram)
        poly = coef_a * eye + coef_b * gram + coef_c * triple_dot(gram_halves, gram_halves)
        poly_halves = split_low(poly)
        turned = triple_dot(split_low(turned), poly_halves)
        if iteration < NS_ITERS - 1:
            gram = triple_dot(poly_halves, split_low(triple_dot(poly_halves, gram_halves)))
    turned_ref[...] = turned.astype(jnp.bfloat16)


def turn_moment(matrix, pos, factor, mom_full, sum_qkv, sum_rest, own):
    rows, width = mom_full.shape[1:]
    return pl.pallas_call(
        muon_kernel,
        grid_spec=pltpu.PrefetchScalarGridSpec(
            num_scalar_prefetch=1,
            grid=(1,),
            in_specs=[
                pl.BlockSpec(memory_space=pltpu.SMEM),
                pl.BlockSpec((1, rows, width), lambda i, choice: (choice[0], 0, 0)),
                pl.BlockSpec((width, 3 * width), lambda i, choice: (0, 0)),
                pl.BlockSpec((width, width), lambda i, choice: (2 * FF // width, 0)),
                pl.BlockSpec(
                    (rows, width), lambda i, choice: (jnp.maximum(choice[0] - 1, 0), 0)
                ),
            ],
            out_specs=pl.BlockSpec((own, width), lambda i, choice: (0, 0)),
            scratch_shapes=[pltpu.VMEM((rows, width), jnp.float32)],
        ),
        out_shape=jax.ShapeDtypeStruct((own, width), jnp.bfloat16),
        cost_estimate=small_cost(),
        compiler_params=kernel_params(),
    )(jnp.stack([matrix, pos]), factor.reshape(1, 1), mom_full, sum_qkv, sum_rest, sum_rest)


def share_turned(turned, group, moments):
    across = partner_swap(turned, "wide", 2)
    across, moments = lax.optimization_barrier((across, moments))
    beside = partner_swap(turned, "wide", 1)
    corner = partner_swap(across, "wide", 1)
    low_side = group < 2
    even = group % 2 == 0
    first = jnp.where(even, turned, beside)
    second = jnp.where(even, beside, turned)
    far_first = jnp.where(even, across, corner)
    far_second = jnp.where(even, corner, across)
    return (
        jnp.where(low_side, first, far_first),
        jnp.where(low_side, second, far_second),
        jnp.where(low_side, across, turned),
    ), moments


def moment_kernel(pos_ref, factor_ref, qkv_ref, proj_ref, up_ref, down_ref, *refs):
    own_refs, moment_refs = refs[:3], refs[3:]
    pos = pos_ref[0]
    factor = factor_ref[0, 0]
    own = own_refs[2].shape[0]
    proj_share = jnp.where(pos == FF // own - 1, 1.0, 0.0)
    first = jnp.where(
        proj_share > 0.5, proj_ref[...].astype(jnp.float32), qkv_ref[...].astype(jnp.float32)
    )
    moment_refs[0][...] = muon_decay * own_refs[0][...] + factor * first.T
    second = up_ref[...].astype(jnp.float32)
    moment_refs[1][...] = muon_decay * own_refs[1][...] + factor * second.T
    third = down_ref[...].astype(jnp.float32)
    moment_refs[2][...] = muon_decay * own_refs[2][...] + factor * third


def own_moments(pos, factor, sum_qkv, sum_rest, moms):
    own, width = moms[2].shape
    parts = FF // own
    whole = pl.BlockSpec((own, width), lambda i, pos: (0, 0))
    return pl.pallas_call(
        moment_kernel,
        grid_spec=pltpu.PrefetchScalarGridSpec(
            num_scalar_prefetch=1,
            grid=(1,),
            in_specs=[
                pl.BlockSpec(memory_space=pltpu.SMEM),
                pl.BlockSpec((width, width), lambda i, pos: (0, jnp.minimum(pos[0], 2))),
                pl.BlockSpec((width, width), lambda i, pos: (2 * FF // width, 0)),
                pl.BlockSpec((own, width), lambda i, pos: (pos[0], 0)),
                pl.BlockSpec((own, width), lambda i, pos: (parts + pos[0], 0)),
            ]
            + [whole] * 3,
            out_specs=[whole] * 3,
        ),
        out_shape=[jax.ShapeDtypeStruct((own, width), jnp.float32)] * 3,
        cost_estimate=small_cost(),
        compiler_params=kernel_params(),
    )(
        pos.reshape(1),
        factor.reshape(1, 1),
        sum_qkv,
        sum_rest,
        sum_rest,
        sum_rest,
        *moms,
    )


def step_kernel(*refs):
    rates = [
        muon_rate * math.sqrt(max(1.0, LATENT_WIDTH / FF)),
        muon_rate * math.sqrt(max(1.0, LATENT_WIDTH / FF)),
        muon_rate * math.sqrt(max(1.0, FF / LATENT_WIDTH)),
    ]
    for place in range(3):
        turned = refs[place][...].astype(jnp.float32)
        change = turned if place == 2 else turned.T
        new = refs[3 + place][...] - rates[place] * change
        refs[9 + place][...] = new
        refs[12 + place][...] = ema_keep * refs[6 + place][...] + (1.0 - ema_keep) * new


def take_step(turned, weights, averages):
    return pl.pallas_call(
        step_kernel,
        out_shape=[jax.ShapeDtypeStruct(weights[0].shape, jnp.float32)] * 6,
        cost_estimate=small_cost(),
        compiler_params=kernel_params(),
    )(*turned, *weights, *averages)


def adam_update(weight, grad, first, second):
    first_new = beta_one * first + (1.0 - beta_one) * grad
    second_new = beta_two * second + (1.0 - beta_two) * grad * grad
    first_hat = first_new / (1.0 - beta_one**STEP_NUMBER)
    second_hat = second_new / (1.0 - beta_two**STEP_NUMBER)
    weight_new = weight - adam_rate * (
        first_hat / (jnp.sqrt(second_hat) + adam_eps) + decay_rate * weight
    )
    return (weight_new, first_new, second_new)


def on_device(
    prior_states,
    target,
    noise_draw,
    level_index,
    g2m_edges,
    neighbours,
    m2g_edges,
    valid_mask,
    channel_weights,
    w_embed,
    w_cond,
    w_attn,
    w_up,
    w_down,
    w_dec,
    biases,
    mom_attn,
    mom_up,
    mom_down,
    m_embed,
    v_embed,
    m_cond,
    v_cond,
    m_dec,
    v_dec,
    m_bias,
    v_bias,
    ema_embed,
    ema_cond,
    ema_attn,
    ema_up,
    ema_down,
    ema_dec,
    ema_bias,
):
    narrow_pos = lax.axis_index("narrow")
    narrow_count = lax.axis_size("narrow")
    pixel_local = valid_mask.shape[1]
    node_local = neighbours.shape[1]
    pixel_total = pixel_local * narrow_count
    node_total = node_local * narrow_count
    embed_low = w_embed.astype(jnp.bfloat16)
    dec_low = w_dec.astype(jnp.bfloat16)
    bias_embed = biases[:LATENT_WIDTH].reshape(1, LATENT_WIDTH)
    bias_up = biases[LATENT_WIDTH : LATENT_WIDTH + FF]
    bias_out = biases[LATENT_WIDTH + FF :]
    noise_level, scale_in, skip_scale, out_scale, loss_scale = sigma_terms(level_index[0])
    target_rows = target[0].astype(jnp.float32)
    noisy = target_rows + noise_level * noise_draw[0].astype(jnp.float32)
    features = jnp.concatenate(
        [prior_states[0, 0], prior_states[0, 1], (scale_in * noisy).astype(jnp.bfloat16)], axis=0
    )
    g2m_rows = jnp.concatenate(ring_slots(g2m_edges[0].T), axis=1)
    lat_weight = lat_weights(narrow_pos * pixel_local, pixel_local, pixel_total)
    pixel_weight = lat_weight * valid_mask[0].astype(jnp.float32)
    near_ids = (neighbours[0] - narrow_pos * node_local) % node_total
    m2g_ids = (m2g_edges[0] - narrow_pos * node_local) % node_total
    near_bias = count_bias(near_ids, node_total)
    m2g_counts = count_matrix(m2g_ids, node_total)

    feature_slots, node_sums = [], []

    def use_slot(features_here, source):
        node_sums.append(
            gather_sum(
                source * pixel_local,
                g2m_cols,
                features_here,
                embed_low,
                bias_embed,
                node_sums[-1] if node_sums else None,
            )
        )
        feature_slots.append((features_here, source))
        return node_sums[-1], near_bias

    g2m_cols = g2m_rows.T
    piece_rows = LATENT_WIDTH // lax.axis_size("wide")
    piece_first = lax.axis_index("wide") * piece_rows
    low_own = jnp.stack(
        [
            lax.dynamic_slice_in_dim(one, piece_first, piece_rows, 0)
            if place % 3 == 2
            else lax.dynamic_slice_in_dim(one, piece_first, piece_rows, 1).T
            for place, one in enumerate((w_attn, w_up, w_down, mom_attn, mom_up, mom_down))
        ]
    ).astype(jnp.bfloat16)
    near_blocks = lax.all_gather(low_own, "narrow", axis=0)
    near_blocks = line_slots(features, use_slot, near_blocks)
    weight_all = lax.all_gather(near_blocks[:, :3], "wide", axis=0)
    mom_near, _ = lax.optimization_barrier((near_blocks, node_sums[3]))
    mom_all = lax.all_gather(mom_near[:, 3:], "wide", axis=0)
    weight_full = weight_all.transpose(2, 1, 0, 3, 4).reshape(3, -1, LATENT_WIDTH)
    attn_rows, up_rows, down_full = weight_full[0], weight_full[1], weight_full[2]
    conditioning = cond_features(noise_level)
    modulation = jnp.dot(conditioning, w_cond, precision=highest_precision)
    gain_two = 1.0 + modulation[2 * LATENT_WIDTH : 3 * LATENT_WIDTH]
    shifts = modulation.reshape(4, LATENT_WIDTH) + jnp.array([[1.0], [0.0], [1.0], [0.0]])
    node_sum = node_sums[-1]
    proj_map = attn_rows[3 * LATENT_WIDTH :]
    attn_in, query_rows, pair_rows = project(node_sum, shifts, attn_rows, node_local)
    attended, mass = attend(query_rows, pair_rows, near_bias)
    attended_rows = attended.astype(jnp.bfloat16)
    node_mid = node_sum[:node_local] / G2M_K + contract_last(attended_rows, proj_map)
    normed_two, inverse_two = norm_stats(node_mid)
    mlp_in = (normed_two * gain_two + modulation[3 * LATENT_WIDTH :]).astype(jnp.bfloat16)
    up_pre = contract_last(mlp_in, up_rows) + bias_up
    hidden = jax.nn.silu(up_pre).astype(jnp.bfloat16)
    node_out = node_mid + jnp.dot(hidden, down_full, preferred_element_type=jnp.float32)
    node_low = node_out.astype(jnp.bfloat16)
    node_raw = lax.dot_general(
        dec_low, node_low, (((0,), (1,)), ((), ())), preferred_element_type=jnp.float32
    ).astype(jnp.bfloat16)
    all_raw = jnp.concatenate(ring_slots(node_raw), axis=1)
    raw_output = contract_last(all_raw, m2g_counts) / M2G_K + bias_out[:, None]
    errors = skip_scale * noisy + out_scale * raw_output - target_rows
    weighted = channel_weights[:, None] * pixel_weight[None, :]
    loss_local = loss_scale * jnp.sum(weighted * errors * errors)
    grad_raw = (2.0 * loss_scale * out_scale * weighted * errors).astype(jnp.bfloat16)
    grad_out_bias = jnp.sum(grad_raw.astype(jnp.float32), axis=1)
    raw_spread = jnp.dot(grad_raw, m2g_counts, preferred_element_type=jnp.float32)
    grad_node_raw = (
        ring_sum(
            [
                raw_spread[:, slot * node_local : (slot + 1) * node_local]
                for slot in range(narrow_count)
            ]
        )
        / M2G_K
    )
    grad_dec = lax.dot_general(
        node_low.astype(jnp.float32),
        grad_node_raw,
        (((0,), (1,)), ((), ())),
        precision=highest_precision,
    )
    grad_node_out = lax.dot_general(
        grad_node_raw,
        dec_low.astype(jnp.float32),
        (((0,), (1,)), ((), ())),
        precision=highest_precision,
    )
    grad_node_out, mom_all = lax.optimization_barrier((grad_node_out, mom_all))
    grad_mlp = grad_node_out.astype(jnp.bfloat16)
    grad_down = contract_rows(hidden, grad_mlp)
    grad_hidden = contract_last(grad_mlp, down_full)
    grad_up_pre = (grad_hidden * silu_slope(up_pre)).astype(jnp.bfloat16)
    grad_up_bias = jnp.sum(grad_up_pre.astype(jnp.float32), axis=0)
    grad_up = contract_rows(grad_up_pre, mlp_in)
    grad_mlp_in = plain_dot(grad_up_pre, up_rows)
    grad_node_mid = grad_node_out + norm_back(grad_mlp_in * gain_two, normed_two, inverse_two)
    grad_proj_out = grad_node_mid.astype(jnp.bfloat16)
    grad_proj = contract_rows(grad_proj_out, attended_rows)
    early = jnp.concatenate([grad_up, grad_down, grad_proj], axis=0).astype(jnp.bfloat16)
    gradient_attended = plain_dot(grad_proj_out, proj_map).astype(jnp.bfloat16)
    early, gradient_attended = lax.optimization_barrier((early, gradient_attended))
    early = lax.psum(early, ("wide", "narrow"))
    grad_query_rows, grad_key_rows, grad_value_rows = attend_back(
        query_rows, pair_rows, near_bias, mass, attended, gradient_attended
    )
    node_grads, grad_qkv, column_sums = project_back(
        grad_query_rows,
        grad_key_rows,
        grad_value_rows,
        node_sum,
        attn_in,
        grad_node_mid,
        shifts,
        attn_rows,
    )
    grad_modulation = jnp.concatenate(
        [
            column_sums[0],
            column_sums[1],
            jnp.sum(grad_mlp_in * normed_two, axis=0),
            jnp.sum(grad_mlp_in, axis=0),
        ]
    )
    grad_cond = conditioning[:, None] * grad_modulation[None, :]
    grad_embed = None
    grad_embed_bias = None
    for features_here, source in feature_slots:
        embed_part, bias_part = scatter_sum(
            source * pixel_local, g2m_rows, node_grads, features_here, embed_low, bias_embed
        )
        grad_embed = embed_part if grad_embed is None else grad_embed + embed_part
        grad_embed_bias = bias_part if grad_embed_bias is None else grad_embed_bias + bias_part
    width = LATENT_WIDTH
    channels = w_dec.shape[1]
    late_rows = jnp.concatenate(
        [
            grad_embed,
            grad_embed_bias.reshape(1, width),
            grad_up_bias.reshape(FF // width, width),
            jnp.pad(grad_out_bias, (0, width - channels)).reshape(1, width),
            grad_dec.T,
        ]
        + [grad_cond[:, place * width : (place + 1) * width] for place in range(4)]
        + [
            jnp.pad(
                jnp.concatenate([loss_local.reshape(1), jnp.sum(pixel_weight).reshape(1)]),
                (0, width - 2),
            ).reshape(1, width),
        ],
        axis=0,
    )
    scalar_row = late_rows.shape[0] - 1
    late_rows = jnp.pad(late_rows, ((0, width - late_rows.shape[0]), (0, 0)))
    late_rows, grad_qkv, early = lax.optimization_barrier((late_rows, grad_qkv, early))
    early_square = jnp.sum(jnp.square(early.astype(jnp.float32)))
    late_rows, mom_all = lax.optimization_barrier((late_rows, mom_all))
    mom_full = mom_all.transpose(2, 1, 0, 3, 4).reshape(3, -1, LATENT_WIDTH)
    joint, early_square, mom_full = joint_sum(grad_qkv, late_rows, (early_square, mom_full))
    sum_qkv, late_rows = joint_split(joint, 3 * LATENT_WIDTH)
    embed_rows = w_embed.shape[0]
    sum_embed = late_rows[:embed_rows]
    place = embed_rows
    bias_rows = late_rows[place : place + 2 + FF // width].reshape(-1)
    sum_bias = bias_rows[: biases.shape[0]]
    loss_sum = late_rows[scalar_row, 0]
    weight_total = late_rows[scalar_row, 1]
    place += 2 + FF // width
    sum_dec = late_rows[place : place + channels].T
    place += channels
    sum_cond = jnp.concatenate(
        [late_rows[place + COND * part : place + COND * (part + 1)] for part in range(4)], axis=1
    )
    square_sum = (
        jnp.sum(jnp.square(late_rows[:scalar_row]))
        + jnp.sum(jnp.square(sum_qkv.astype(jnp.float32)))
        + early_square
    )
    grad_norm = jnp.sqrt(square_sum) / weight_total
    factor = jnp.minimum(1.0, clip_bound / (grad_norm + 1e-06)) / weight_total
    group = lax.axis_index("wide") % 4
    turned = turn_moment(
        jnp.minimum(group, 2), narrow_pos, factor, mom_full, joint, early, w_down.shape[0]
    )
    moments = own_moments(
        narrow_pos, factor, joint, early, (mom_attn, mom_up, mom_down)
    )
    turned, moments = share_turned(turned, group, moments)
    moment_attn, moment_up, moment_down = moments
    new_attn, new_up, new_down, average_attn, average_up, average_down = take_step(
        turned, (w_attn, w_up, w_down), (ema_attn, ema_up, ema_down)
    )
    new_embed, first_embed, second_embed = adam_update(
        w_embed, factor * sum_embed, m_embed, v_embed
    )
    new_cond, first_cond, second_cond = adam_update(w_cond, factor * sum_cond, m_cond, v_cond)
    new_dec, first_dec, second_dec = adam_update(w_dec, factor * sum_dec, m_dec, v_dec)
    new_bias, first_bias, second_bias = adam_update(biases, factor * sum_bias, m_bias, v_bias)
    keep_rest = 1.0 - ema_keep
    return (
        new_attn,
        new_up,
        new_down,
        moment_attn,
        moment_up,
        moment_down,
        new_embed,
        new_cond,
        new_dec,
        new_bias,
        first_embed,
        second_embed,
        first_cond,
        second_cond,
        first_dec,
        second_dec,
        first_bias,
        second_bias,
        ema_keep * ema_embed + keep_rest * new_embed,
        ema_keep * ema_cond + keep_rest * new_cond,
        average_attn,
        average_up,
        average_down,
        ema_keep * ema_dec + keep_rest * new_dec,
        ema_keep * ema_bias + keep_rest * new_bias,
        loss_sum,
        weight_total,
        grad_norm,
    )


def solution(mesh):
    in_specs = (
        P("wide", None, None, "narrow"),
        P("wide", None, "narrow"),
        P("wide", None, "narrow"),
        P("wide"),
        P("wide", "narrow", None),
        P("wide", "narrow", None),
        P("wide", "narrow", None),
        P("wide", "narrow"),
        P(),
        P(),
        P(),
        P(None, "narrow"),
        P(None, "narrow"),
        P("narrow", None),
        P(),
        P(),
        P(None, "narrow"),
        P(None, "narrow"),
        P("narrow", None),
        P(),
        P(),
        P(),
        P(),
        P(),
        P(),
        P(),
        P(),
        P(),
        P(),
        P(None, "narrow"),
        P(None, "narrow"),
        P("narrow", None),
        P(),
        P(),
    )
    out_specs = (
        P(None, "narrow"),
        P(None, "narrow"),
        P("narrow", None),
        P(None, "narrow"),
        P(None, "narrow"),
        P("narrow", None),
        P(),
        P(),
        P(),
        P(),
        P(),
        P(),
        P(),
        P(),
        P(),
        P(),
        P(),
        P(),
        P(),
        P(),
        P(None, "narrow"),
        P(None, "narrow"),
        P("narrow", None),
        P(),
        P(),
        P(),
        P(),
        P(),
    )
    return jax.shard_map(
        on_device, mesh=mesh, in_specs=in_specs, out_specs=out_specs, check_vma=False
    )
```

```python
import functools
import math

import jax
import jax.numpy as jnp
from jax import lax
from jax.experimental import pallas as pl
from jax.experimental.pallas import tpu as pltpu
from jax.sharding import PartitionSpec as P

LATENT_WIDTH = 512
HEADS = 4
HEAD_WIDTH = 128
FF = 2048
COND = 32
NBR = 32
G2M_K = 4
M2G_K = 3
NS_ITERS = 5
SIGMA_LEVELS = 8
STEP_NUMBER = 10


highest_precision = lax.Precision.HIGHEST
sigma_low = 0.25
sigma_high = 4.0
clip_bound = 0.02
muon_rate = 0.5
muon_decay = 0.95
adam_rate = 0.03
beta_one = 0.9
beta_two = 0.95
adam_eps = 1e-08
decay_rate = 0.01
ema_keep = 0.9
coef_a = 3.4445
coef_b = -4.775
coef_c = 2.0315


def sigma_terms(level):
    fraction = level.astype(jnp.float32) / (SIGMA_LEVELS - 1)
    noise_level = sigma_low * (sigma_high / sigma_low) ** fraction
    square = noise_level * noise_level + 1.0
    scale_in = lax.rsqrt(square)
    return (
        noise_level,
        scale_in,
        1.0 / square,
        noise_level * scale_in,
        square / (noise_level * noise_level),
    )


def cond_features(noise_level):
    frequencies = 1.0 + jnp.arange(COND // 2).astype(jnp.float32)
    phases = jnp.log(noise_level) * frequencies
    return jnp.concatenate([jnp.sin(phases), jnp.cos(phases)])


def lat_weights(first_row, row_count, pixel_total):
    row_ids = (first_row + jnp.arange(row_count, dtype=jnp.int32)).astype(jnp.float32)
    return jnp.cos(math.pi * ((row_ids + 0.5) / pixel_total - 0.5))


def norm_stats(values):
    centred = values - jnp.mean(values, axis=-1, keepdims=True)
    inverse = lax.rsqrt(jnp.mean(centred * centred, axis=-1, keepdims=True) + 1e-05)
    return (centred * inverse, inverse)


def norm_back(grad_normed, normed, inverse):
    first_mean = jnp.mean(grad_normed, axis=-1, keepdims=True)
    second_mean = jnp.mean(grad_normed * normed, axis=-1, keepdims=True)
    return inverse * (grad_normed - first_mean - normed * second_mean)


def silu_slope(values):
    sigmoid_values = jax.nn.sigmoid(values)
    return sigmoid_values * (1.0 + values * (1.0 - sigmoid_values))


def contract_rows(left, right):
    return lax.dot_general(
        left, right, (((0,), (0,)), ((), ())), preferred_element_type=jnp.float32
    )


def contract_last(left, right):
    return lax.dot_general(
        left, right, (((1,), (1,)), ((), ())), preferred_element_type=jnp.float32
    )


def axis_bits(axis_name):
    bits = []
    reach = 1
    while reach < lax.axis_size(axis_name):
        bits.append((axis_name, len(bits)))
        reach *= 2
    return bits


def sum_stages():
    wide_bits = len(axis_bits("wide"))
    stages = [("wide", 0, 1)]
    first = 1
    while first < wide_bits:
        stages.append(("wide", first, min(2, wide_bits - first)))
        first += 2
    stages.append(("narrow", 0, len(axis_bits("narrow"))))
    return stages


def partner_swap(values, axis_name, distance):
    size = lax.axis_size(axis_name)
    return lax.ppermute(values, axis_name, [(i, i ^ distance) for i in range(size)])


def joint_pieces(coarse, fine):
    upper = fine.astype(jnp.bfloat16)
    lower = (fine - lax.optimization_barrier(upper).astype(jnp.float32)).astype(jnp.bfloat16)
    return jnp.concatenate([coarse.astype(jnp.bfloat16), upper, lower], axis=1)


def joint_split(pieces, coarse_width):
    coarse = pieces[:, :coarse_width]
    fine_width = (pieces.shape[1] - coarse_width) // 2
    upper = pieces[:, coarse_width : coarse_width + fine_width].astype(jnp.float32)
    return coarse, upper + pieces[:, coarse_width + fine_width :].astype(jnp.float32)


def joint_sum(coarse, fine, beside):
    coarse_width = coarse.shape[1]
    stages = sum_stages()
    for axis_name, first, width in stages:
        members = 1 << width
        block = fine.shape[0] // members
        mine = (lax.axis_index(axis_name) >> first) & (members - 1)
        arrived = []
        for far in range(1, members):
            begin = (mine ^ far) * block
            piece = joint_pieces(
                lax.dynamic_slice_in_dim(coarse, begin, block, 0),
                lax.dynamic_slice_in_dim(fine, begin, block, 0),
            )
            arrived.append(partner_swap(piece, axis_name, far << first))
        if first == 1 and axis_name == "wide":
            arrived, beside = lax.optimization_barrier((arrived, beside))
        coarse = lax.dynamic_slice_in_dim(coarse, mine * block, block, 0)
        fine = lax.dynamic_slice_in_dim(fine, mine * block, block, 0)
        for piece in arrived:
            more_coarse, more_fine = joint_split(piece, coarse_width)
            coarse = coarse + more_coarse.astype(jnp.float32)
            fine = fine + more_fine
    values = joint_pieces(coarse, fine)
    for axis_name, first, width in stages[::-1]:
        members = 1 << width
        mine = (lax.axis_index(axis_name) >> first) & (members - 1)
        pieces = [values] + [
            partner_swap(values, axis_name, far << first) for far in range(1, members)
        ]
        for bit in range(width):
            is_high = ((mine >> bit) & 1) == 1
            step = 1 << bit
            pieces = [
                jnp.where(is_high, pieces[place ^ step], pieces[place])
                for place in range(members)
            ]
        values = jnp.concatenate(pieces, axis=0)
    return values, *beside


def ring_slots(values):
    size = lax.axis_size("narrow")
    slots = [values]
    for shift in range(1, size):
        slots.append(
            lax.ppermute(values, "narrow", [((i + shift) % size, i) for i in range(size)])
        )
    return slots


def line_slots(values, use_slot, later):
    size = lax.axis_size("narrow")
    pos = lax.axis_index("narrow")
    from_low, from_high = values, values
    arrived = {}
    orders = [
        sorted((s for s in range(size) if s != n), key=lambda s, n=n: (abs(s - n), s < n))
        for n in range(size)
    ]
    chosen, source = values, pos
    for step in range(size):
        if step < size - 1:
            from_low = lax.ppermute(
                from_low, "narrow", [(i, i + 1) for i in range(step, size - 1)]
            )
            from_high = lax.ppermute(
                from_high, "narrow", [(i, i - 1) for i in range(1, size - step)]
            )
        result = use_slot(chosen, source)
        if step == size - 1:
            return
        from_low, from_high, _, later[step] = lax.optimization_barrier(
            (from_low, from_high, result, later[step])
        )
        arrived[-1 - step] = from_low
        arrived[1 + step] = from_high
        offsets = [orders[n][step] - n for n in range(size)]
        chosen = arrived[offsets[0]]
        for offset in sorted(set(offsets) - {offsets[0]}):
            here = functools.reduce(
                jnp.logical_or, [pos == n for n in range(size) if offsets[n] == offset]
            )
            chosen = jnp.where(here, arrived[offset], chosen)
        source = pos + jnp.array(offsets, jnp.int32)[pos]


def in_order(slots):
    size = lax.axis_size("narrow")
    pos = lax.axis_index("narrow")
    rows, width = slots[0].shape
    across = jnp.zeros((size, 3, rows // 3, width), slots[0].dtype)
    for shift, piece in enumerate(slots):
        across = lax.dynamic_update_slice_in_dim(
            across, piece.reshape(1, 3, rows // 3, width), (pos + shift) % size, 0
        )
    return across


def ring_sum(parts):
    size = lax.axis_size("narrow")
    total = parts[0]
    for shift in range(1, size):
        arrived = lax.ppermute(
            parts[shift].astype(jnp.bfloat16),
            "narrow",
            [(i, (i + shift) % size) for i in range(size)],
        )
        total = total + arrived.astype(jnp.float32)
    return total


VMEM_LIMIT = 60 * 1024 * 1024
SCORE_SCALE = math.log2(math.e) / math.sqrt(HEAD_WIDTH)
MASKED = -1e30


def small_cost():
    return pl.CostEstimate(flops=1 << 20, bytes_accessed=1 << 20, transcendentals=0)


def kernel_params():
    return pltpu.CompilerParams(vmem_limit_bytes=VMEM_LIMIT)


def count_kernel(ids_ref, out_ref):
    first = pl.program_id(0) * out_ref.shape[1]
    columns = lax.broadcasted_iota(jnp.int32, out_ref.shape, 1).astype(jnp.int16)
    ids = (ids_ref[...] - first).astype(jnp.int16)
    one = jnp.ones(out_ref.shape, jnp.bfloat16)
    zero = jnp.zeros(out_ref.shape, jnp.bfloat16)
    total = zero
    for slot in range(ids.shape[1]):
        total = total + jnp.where(ids[:, slot : slot + 1] == columns, one, zero)
    out_ref[...] = total


def count_matrix(ids, column_count, rows=1024, columns=2048):
    row_count, slots = ids.shape
    rows = min(rows, row_count)
    columns = min(columns, column_count)
    return pl.pallas_call(
        count_kernel,
        grid=(column_count // columns, row_count // rows),
        in_specs=[pl.BlockSpec((rows, slots), lambda j, i: (i, 0))],
        out_specs=pl.BlockSpec((rows, columns), lambda j, i: (i, j)),
        out_shape=jax.ShapeDtypeStruct((row_count, column_count), jnp.bfloat16),
        cost_estimate=small_cost(),
        compiler_params=kernel_params(),
    )(ids)


def bias_kernel(row_ref, lane_ref, out_ref):
    groups, width = row_ref.shape
    blocks = out_ref.shape[1] // 128
    row_iota = lax.broadcasted_iota(jnp.int32, (8 * blocks, width), 0)
    lane_iota = lax.broadcasted_iota(jnp.int32, (128, width), 0)
    for group in range(groups):
        left = jnp.where(row_iota == row_ref[group : group + 1, :], 1.0, 0.0)
        right = jnp.where(lane_iota == lane_ref[group : group + 1, :], 1.0, 0.0)
        counts = contract_last(left.astype(jnp.bfloat16), right.astype(jnp.bfloat16))
        bias = jnp.where(counts > 0.5, jnp.log2(counts), MASKED)
        for block in range(blocks):
            out_ref[group * 8 : (group + 1) * 8, block * 128 : (block + 1) * 128] = bias[
                block * 8 : (block + 1) * 8, :
            ]


def count_bias(ids, total, per_step=32):
    row_count, slots = ids.shape
    groups = row_count // 8
    member = (jnp.arange(row_count, dtype=jnp.int32) % 8)[:, None]
    row_keys = ((ids // 128) * 8 + member).reshape(groups, 8 * slots)
    lane_keys = (ids % 128).reshape(groups, 8 * slots)
    spec = pl.BlockSpec((per_step, 8 * slots), lambda i: (i, 0))
    return pl.pallas_call(
        bias_kernel,
        grid=(groups // per_step,),
        in_specs=[spec, spec],
        out_specs=pl.BlockSpec((8 * per_step, total), lambda i: (i, 0)),
        out_shape=jax.ShapeDtypeStruct((row_count, total), jnp.float32),
        cost_estimate=small_cost(),
        compiler_params=kernel_params(),
    )(row_keys, lane_keys)


def attend_kernel(chunk, q_ref, k_ref, v_ref, bias_ref, att_ref, mass_ref):
    q = q_ref[...]
    top = jnp.full((q.shape[0], 1), -jnp.inf, jnp.float32)
    mass = jnp.zeros((q.shape[0], 1), jnp.float32)
    attended = jnp.zeros(att_ref.shape, jnp.float32)
    for start in range(0, k_ref.shape[0], chunk):
        part = pl.ds(start, chunk)
        scores = contract_last(q, k_ref[part, :]) * SCORE_SCALE + bias_ref[:, part]
        higher = jnp.maximum(top, jnp.max(scores, axis=1, keepdims=True))
        raised = jnp.exp2(scores - higher)
        shrink = jnp.exp2(top - higher)
        mass = mass * shrink + jnp.sum(raised, axis=1, keepdims=True)
        attended = attended * shrink + jnp.dot(
            raised.astype(jnp.bfloat16), v_ref[part, :], preferred_element_type=jnp.float32
        )
        top = higher
    att_ref[...] = attended / mass
    mass_ref[...] = jnp.broadcast_to(top + jnp.log2(mass), mass_ref.shape)


def attend(queries, pairs, bias, rows=1024, chunk=512):
    row_count = queries.shape[0]
    rows = min(rows, row_count)
    total = pairs.shape[0]
    block = pl.BlockSpec((rows, HEAD_WIDTH), lambda h, r: (r, h))
    return pl.pallas_call(
        functools.partial(attend_kernel, chunk),
        grid=(HEADS, row_count // rows),
        in_specs=[
            block,
            pl.BlockSpec((total, HEAD_WIDTH), lambda h, r: (0, h)),
            pl.BlockSpec((total, HEAD_WIDTH), lambda h, r: (0, HEADS + h)),
            pl.BlockSpec((rows, total), lambda h, r: (r, 0)),
        ],
        out_specs=[block, block],
        out_shape=[jax.ShapeDtypeStruct(queries.shape, jnp.float32)] * 2,
        cost_estimate=small_cost(),
        compiler_params=kernel_params(),
    )(queries, pairs, pairs, bias)


def attend_back_kernel(
    chunk,
    q_ref,
    k_ref,
    v_ref,
    bias_ref,
    mass_ref,
    att_ref,
    g_ref,
    dq_ref,
    dk_ref,
    dv_ref,
    dk_sum,
    dv_sum,
):
    step = pl.program_id(1)
    q = q_ref[...]
    g = g_ref[...]
    total = k_ref.shape[0]
    mass = mass_ref[:, :1]
    inner = jnp.sum(att_ref[...] * g.astype(jnp.float32), axis=1, keepdims=True)

    @pl.when(step == 0)
    def _():
        dk_sum[...] = jnp.zeros_like(dk_sum)
        dv_sum[...] = jnp.zeros_like(dv_sum)

    dq = jnp.zeros(q.shape, jnp.float32)
    for start in range(0, total, chunk):
        part = pl.ds(start, chunk)
        k = k_ref[part, :]
        v = v_ref[part, :]
        prob = jnp.exp2(contract_last(q, k) * SCORE_SCALE + (bias_ref[:, part] - mass))
        grad_scores = (prob * (contract_last(g, v) - inner)).astype(jnp.bfloat16)
        dq = dq + jnp.dot(grad_scores, k, preferred_element_type=jnp.float32)
        dk_sum[part, :] += contract_rows(grad_scores, q)
        dv_sum[part, :] += contract_rows(prob.astype(jnp.bfloat16), g)
    shrink = 1.0 / math.sqrt(HEAD_WIDTH)
    dq_ref[...] = (dq * shrink).astype(jnp.bfloat16)

    @pl.when(step == pl.num_programs(1) - 1)
    def _():
        dk_ref[...] = (dk_sum[...] * shrink).astype(jnp.bfloat16)
        dv_ref[...] = dv_sum[...].astype(jnp.bfloat16)


def attend_back(queries, pairs, bias, mass, attended, grads, rows=1024, chunk=256):
    row_count = queries.shape[0]
    total = pairs.shape[0]
    rows = min(rows, row_count)
    block = pl.BlockSpec((rows, HEAD_WIDTH), lambda h, r: (r, h))
    column = pl.BlockSpec((total, HEAD_WIDTH), lambda h, r: (0, h))
    key_shape = jax.ShapeDtypeStruct((total, LATENT_WIDTH), jnp.bfloat16)
    return pl.pallas_call(
        functools.partial(attend_back_kernel, chunk),
        grid=(HEADS, row_count // rows),
        in_specs=[
            block,
            column,
            pl.BlockSpec((total, HEAD_WIDTH), lambda h, r: (0, HEADS + h)),
            pl.BlockSpec((rows, total), lambda h, r: (r, 0)),
            block,
            block,
            block,
        ],
        out_specs=[block, column, column],
        out_shape=[jax.ShapeDtypeStruct(queries.shape, jnp.bfloat16), key_shape, key_shape],
        scratch_shapes=[pltpu.VMEM((total, HEAD_WIDTH), jnp.float32)] * 2,
        cost_estimate=small_cost(),
        compiler_params=kernel_params(),
    )(queries, pairs, pairs, bias, mass, attended, grads)


def gather_kernel(sub, first_ref, ids_ref, feature_ref, map_ref, bias_ref, *rest):
    out_ref, pixel_ref = rest[-2:]

    @pl.when(pl.program_id(0) == 0)
    def _():
        pre = contract_rows(feature_ref[...], map_ref[...]) + bias_ref[...]
        pixel_ref[...] = (pre / (1.0 + jnp.exp(-pre))).astype(jnp.bfloat16)

    pixels = pixel_ref[...]
    columns = lax.broadcasted_iota(jnp.int32, (sub, pixels.shape[0]), 1).astype(jnp.int16)
    one = jnp.ones(columns.shape, jnp.bfloat16)
    zero = jnp.zeros(columns.shape, jnp.bfloat16)
    for block in range(out_ref.shape[0] // sub):
        part = pl.ds(block * sub, sub)
        ids = (ids_ref[part, :] - first_ref[0, 0]).astype(jnp.int16)
        counts = zero
        for slot in range(ids.shape[1]):
            counts = counts + jnp.where(ids[:, slot : slot + 1] == columns, one, zero)
        rows = jnp.dot(counts, pixels, preferred_element_type=jnp.float32)
        if len(rest) == 3:
            rows = rows + rest[0][part, :]
        out_ref[part, :] = rows


def gather_sum(first, ids, features, embed_map, embed_bias, earlier, rows=1024, sub=256):
    row_count, slots = ids.shape
    channels, pixel_count = features.shape
    width = embed_map.shape[1]
    block = pl.BlockSpec((rows, width), lambda i: (i, 0))
    more = [] if earlier is None else [earlier]
    return pl.pallas_call(
        functools.partial(gather_kernel, sub),
        grid=(row_count // rows,),
        in_specs=[
            pl.BlockSpec(memory_space=pltpu.SMEM),
            pl.BlockSpec((rows, slots), lambda i: (i, 0)),
            pl.BlockSpec((channels, pixel_count), lambda i: (0, 0)),
            pl.BlockSpec((channels, width), lambda i: (0, 0)),
            pl.BlockSpec((1, width), lambda i: (0, 0)),
        ]
        + [block] * len(more),
        out_specs=block,
        out_shape=jax.ShapeDtypeStruct((row_count, width), jnp.float32),
        scratch_shapes=[pltpu.VMEM((pixel_count, width), jnp.bfloat16)],
        cost_estimate=small_cost(),
        compiler_params=kernel_params(),
    )(first.reshape(1, 1), ids, features, embed_map, embed_bias, *more)


def scatter_kernel(
    chunk, first_ref, ids_ref, g_ref, feature_ref, map_ref, shift_ref, grad_ref, bias_ref
):
    step = pl.program_id(0)
    rows = feature_ref.shape[1]
    pixel_ids = lax.broadcasted_iota(jnp.int32, (rows, chunk), 0).astype(jnp.int16)
    one = jnp.ones((rows, chunk), jnp.bfloat16)
    zero = jnp.zeros((rows, chunk), jnp.bfloat16)
    spread = jnp.zeros((rows, g_ref.shape[1]), jnp.float32)
    for start in range(0, g_ref.shape[0], chunk):
        part = pl.ds(start, chunk)
        counts = zero
        for slot in range(ids_ref.shape[0]):
            ids = ids_ref[slot : slot + 1, part] - (first_ref[0, 0] + step * rows)
            ids = jnp.broadcast_to(ids, (rows, chunk))
            counts = counts + jnp.where(ids.astype(jnp.int16) == pixel_ids, one, zero)
        spread = spread + jnp.dot(counts, g_ref[part, :], preferred_element_type=jnp.float32)
    pre = contract_rows(feature_ref[...], map_ref[...]) + shift_ref[...]
    sigmoid_values = 1.0 / (1.0 + jnp.exp(-pre))
    lowered = (spread * (sigmoid_values * (1.0 + pre * (1.0 - sigmoid_values)))).astype(
        jnp.bfloat16
    )

    @pl.when(step == 0)
    def _():
        grad_ref[...] = jnp.zeros_like(grad_ref)
        bias_ref[...] = jnp.zeros_like(bias_ref)

    grad_ref[...] += jnp.dot(feature_ref[...], lowered, preferred_element_type=jnp.float32)
    bias_ref[...] += jnp.sum(lowered.astype(jnp.float32), axis=0, keepdims=True)


def scatter_sum(first, ids, grads, features, embed_map, embed_bias, rows=512, chunk=1024):
    slots, node_count = ids.shape
    width = grads.shape[1]
    channels, pixel_count = features.shape
    return pl.pallas_call(
        functools.partial(scatter_kernel, chunk),
        grid=(pixel_count // rows,),
        in_specs=[
            pl.BlockSpec(memory_space=pltpu.SMEM),
            pl.BlockSpec((slots, node_count), lambda i: (0, 0)),
            pl.BlockSpec((node_count, width), lambda i: (0, 0)),
            pl.BlockSpec((channels, rows), lambda i: (0, i)),
            pl.BlockSpec((channels, width), lambda i: (0, 0)),
            pl.BlockSpec((1, width), lambda i: (0, 0)),
        ],
        out_specs=[
            pl.BlockSpec((channels, width), lambda i: (0, 0)),
            pl.BlockSpec((1, width), lambda i: (0, 0)),
        ],
        out_shape=[
            jax.ShapeDtypeStruct((channels, width), jnp.float32),
            jax.ShapeDtypeStruct((1, width), jnp.float32),
        ],
        cost_estimate=small_cost(),
        compiler_params=kernel_params(),
    )(first.reshape(1, 1), ids, grads, features, embed_map, embed_bias)


def pad_rows(values):
    return jnp.pad(values, ((0, 128 - values.shape[0]), (0, 0)))


def decode_kernel(
    scale_ref,
    count_ref,
    raw_ref,
    target_ref,
    noise_ref,
    pixel_ref,
    channel_ref,
    shift_ref,
    spread_ref,
    bias_ref,
    loss_ref,
):
    step = pl.program_id(0)
    noise_level, skip_scale, out_scale, loss_scale = [scale_ref[place] for place in range(4)]
    counts = count_ref[...]
    raw = contract_last(counts, raw_ref[...]).T * (1.0 / M2G_K) + shift_ref[...]
    target = target_ref[...].astype(jnp.float32)
    noisy = target + noise_level * noise_ref[...].astype(jnp.float32)
    errors = skip_scale * noisy + out_scale * raw - target
    weighted = channel_ref[...] * pixel_ref[...] * errors
    grads = ((2.0 * loss_scale * out_scale) * weighted).astype(jnp.bfloat16).astype(jnp.float32)

    @pl.when(step == 0)
    def _():
        spread_ref[...] = jnp.zeros_like(spread_ref)
        bias_ref[...] = jnp.zeros_like(bias_ref)
        loss_ref[...] = jnp.zeros_like(loss_ref)

    row_loss = jnp.sum(weighted * errors, axis=1, keepdims=True)
    loss_ref[...] += loss_scale * jnp.sum(row_loss, axis=0, keepdims=True)
    bias_ref[...] += jnp.sum(grads, axis=1, keepdims=True)
    spread_ref[...] += plain_dot(grads.astype(jnp.bfloat16), counts)


def decode(scales, counts, raw, target, noise, pixel_weight, channels, shifts, rows=512):
    pixel_count, node_count = counts.shape
    wide_block = pl.BlockSpec((128, rows), lambda i: (0, i))
    column = pl.BlockSpec((128, 1), lambda i: (0, 0))
    return pl.pallas_call(
        decode_kernel,
        grid=(pixel_count // rows,),
        in_specs=[
            pl.BlockSpec(memory_space=pltpu.SMEM),
            pl.BlockSpec((rows, node_count), lambda i: (i, 0)),
            pl.BlockSpec((128, node_count), lambda i: (0, 0)),
            wide_block,
            wide_block,
            pl.BlockSpec((1, rows), lambda i: (0, i)),
            column,
            column,
        ],
        out_specs=[
            pl.BlockSpec((128, node_count), lambda i: (0, 0)),
            column,
            pl.BlockSpec((1, 1), lambda i: (0, 0)),
        ],
        out_shape=[
            jax.ShapeDtypeStruct((128, node_count), jnp.float32),
            jax.ShapeDtypeStruct((128, 1), jnp.float32),
            jax.ShapeDtypeStruct((1, 1), jnp.float32),
        ],
        cost_estimate=small_cost(),
        compiler_params=kernel_params(),
    )(scales, counts, raw, target, noise, pixel_weight, channels, shifts)


def row_norm(sums):
    values = sums * (1.0 / G2M_K)
    centred = values - jnp.mean(values, axis=1, keepdims=True)
    inverse = lax.rsqrt(jnp.mean(centred * centred, axis=1, keepdims=True) + 1e-05)
    return centred * inverse, inverse


def project_kernel(sum_ref, shift_ref, map_ref, attn_ref, query_ref, pair_ref):
    width = sum_ref.shape[1]
    normed, _ = row_norm(sum_ref[...])
    attn_in = (normed * shift_ref[0:1, :] + shift_ref[1:2, :]).astype(jnp.bfloat16)
    attn_ref[...] = attn_in
    for place in range(2):
        part = pl.ds(place * width, width)
        weights = map_ref[pl.ds((place + 1) * width, width), :]
        pair_ref[:, part] = contract_last(attn_in, weights).astype(jnp.bfloat16)

    @pl.when(pl.program_id(0) == 0)
    def _():
        query_ref[...] = contract_last(attn_in, map_ref[pl.ds(0, width), :]).astype(jnp.bfloat16)


def project(sums, shifts, attn_map, rows):
    row_count, width = sums.shape
    block = pl.BlockSpec((rows, width), lambda i: (i, 0))
    return pl.pallas_call(
        project_kernel,
        grid=(row_count // rows,),
        in_specs=[
            block,
            pl.BlockSpec(shifts.shape, lambda i: (0, 0)),
            pl.BlockSpec(attn_map.shape, lambda i: (0, 0)),
        ],
        out_specs=[
            block,
            pl.BlockSpec((rows, width), lambda i: (0, 0)),
            pl.BlockSpec((rows, 2 * width), lambda i: (i, 0)),
        ],
        out_shape=[
            jax.ShapeDtypeStruct((row_count, width), jnp.bfloat16),
            jax.ShapeDtypeStruct((rows, width), jnp.bfloat16),
            jax.ShapeDtypeStruct((row_count, 2 * width), jnp.bfloat16),
        ],
        cost_estimate=small_cost(),
        compiler_params=kernel_params(),
    )(sums, shifts, attn_map)


def project_back_kernel(
    dq_ref,
    dk_ref,
    dv_ref,
    sum_ref,
    attn_ref,
    mid_ref,
    shift_ref,
    map_ref,
    node_ref,
    grad_ref,
    column_ref,
    back_ref,
):
    step = pl.program_id(0)
    width = sum_ref.shape[1]
    attn_in = attn_ref[...]
    dk, dv = dk_ref[...], dv_ref[...]
    back_ref[...] = plain_dot(dk, map_ref[pl.ds(width, width), :]) + plain_dot(
        dv, map_ref[pl.ds(2 * width, width), :]
    )

    @pl.when(step == 0)
    def _():
        grad_ref[...] = jnp.zeros_like(grad_ref)
        column_ref[...] = jnp.zeros_like(column_ref)
        dq = dq_ref[...]
        back_ref[...] += plain_dot(dq, map_ref[pl.ds(0, width), :])
        grad_ref[:, pl.ds(0, width)] = contract_rows(dq, attn_in)

    grad_ref[:, pl.ds(width, width)] += contract_rows(dk, attn_in)
    grad_ref[:, pl.ds(2 * width, width)] += contract_rows(dv, attn_in)
    back = back_ref[...]
    normed, inverse = row_norm(sum_ref[...])
    column_ref[0:1, :] += jnp.sum(back * normed, axis=0, keepdims=True)
    column_ref[1:2, :] += jnp.sum(back, axis=0, keepdims=True)
    grads = back * shift_ref[0:1, :]
    first_mean = jnp.mean(grads, axis=1, keepdims=True)
    second_mean = jnp.mean(grads * normed, axis=1, keepdims=True)
    grads = inverse * (grads - first_mean - normed * second_mean)
    own_share = jnp.where(step == 0, 1.0, 0.0)
    node_ref[...] = ((grads + own_share * mid_ref[...]) * (1.0 / G2M_K)).astype(jnp.bfloat16)


def project_back(dq, dk, dv, sums, attn_in, mid, shifts, attn_map):
    row_count, width = sums.shape
    rows = dq.shape[0]
    block = pl.BlockSpec((rows, width), lambda i: (i, 0))
    own = pl.BlockSpec((rows, width), lambda i: (0, 0))
    return pl.pallas_call(
        project_back_kernel,
        grid=(row_count // rows,),
        in_specs=[
            own,
            block,
            block,
            block,
            block,
            own,
            pl.BlockSpec(shifts.shape, lambda i: (0, 0)),
            pl.BlockSpec(attn_map.shape, lambda i: (0, 0)),
        ],
        out_specs=[
            block,
            pl.BlockSpec((width, 3 * width), lambda i: (0, 0)),
            pl.BlockSpec((8, width), lambda i: (0, 0)),
        ],
        out_shape=[
            jax.ShapeDtypeStruct((row_count, width), jnp.bfloat16),
            jax.ShapeDtypeStruct((width, 3 * width), jnp.float32),
            jax.ShapeDtypeStruct((8, width), jnp.float32),
        ],
        scratch_shapes=[pltpu.VMEM((rows, width), jnp.float32)],
        cost_estimate=small_cost(),
        compiler_params=kernel_params(),
    )(dq, dk, dv, sums, attn_in, mid, shifts, attn_map)


def split_low(values):
    upper = values.astype(jnp.bfloat16)
    return upper, (values - upper.astype(jnp.float32)).astype(jnp.bfloat16)


def plain_dot(left, right):
    return jnp.dot(left, right, preferred_element_type=jnp.float32)


def triple_dot(left, right, dot=plain_dot):
    return dot(left[0], right[0]) + (dot(left[0], right[1]) + dot(left[1], right[0]))


def muon_kernel(
    scalar_row,
    choice_ref,
    square_ref,
    mom_ref,
    joint_ref,
    proj_ref,
    rest_ref,
    turned_ref,
    factor_ref,
    norm_ref,
    full_ref,
):
    matrix, pos = choice_ref[0], choice_ref[1]
    width = turned_ref.shape[1]
    coarse = joint_ref[:, pl.ds(0, 3 * width)].astype(jnp.float32)
    fine = joint_ref[:, pl.ds(3 * width, width)].astype(jnp.float32)
    fine = fine + joint_ref[:, pl.ds(4 * width, width)].astype(jnp.float32)
    in_norm = lax.broadcasted_iota(jnp.int32, fine.shape, 0) < scalar_row
    square = jnp.sum(jnp.where(in_norm, fine * fine, 0.0), axis=1, keepdims=True)
    square = square + jnp.sum(coarse * coarse, axis=1, keepdims=True)
    square = jnp.sum(square, axis=0, keepdims=True) + square_ref[0, 0]
    weight_total = fine[scalar_row : scalar_row + 1, 1:2]
    grad_norm = jnp.sqrt(square) / weight_total
    factor = jnp.minimum(1.0, clip_bound / (grad_norm + 1e-06)) / weight_total
    norm_ref[...] = grad_norm
    factor_ref[...] = factor
    own, width = turned_ref.shape
    gram = jnp.zeros((width, width), jnp.float32)
    for place in range(FF // width):
        part = pl.ds(place * width, width)
        if place < 3:
            first = joint_ref[:, part]
        else:
            first = proj_ref[...]
        grads = jnp.where(
            matrix == 0, first.astype(jnp.float32), rest_ref[part, :].astype(jnp.float32)
        )
        moment = muon_decay * mom_ref[0, part, :].astype(jnp.float32) + factor * grads
        full_ref[part, :] = moment
        halves = split_low(moment)
        gram = gram + triple_dot(halves, halves, contract_rows)
    row_ids = lax.broadcasted_iota(jnp.int32, gram.shape, 0)
    eye = jnp.where(row_ids == lax.broadcasted_iota(jnp.int32, gram.shape, 1), 1.0, 0.0)
    trace = jnp.sum(jnp.sum(gram * eye, axis=1, keepdims=True), axis=0, keepdims=True)
    scale = 1.0 / (jnp.sqrt(trace) + 1e-07)
    gram = gram * (scale * scale)
    turned = full_ref[pl.ds(pos * own, own), :] * scale
    for iteration in range(NS_ITERS):
        gram_halves = split_low(gram)
        poly = coef_a * eye + coef_b * gram + coef_c * triple_dot(gram_halves, gram_halves)
        poly_halves = split_low(poly)
        turned = triple_dot(split_low(turned), poly_halves)
        if iteration < NS_ITERS - 1:
            gram = triple_dot(poly_halves, split_low(triple_dot(poly_halves, gram_halves)))
    turned_ref[...] = turned.astype(jnp.bfloat16)


def turn_moment(matrix, pos, rest_square, scalar_row, mom_full, joint, sum_rest, own):
    rows, width = mom_full.shape[1:]
    single = pl.BlockSpec((1, 1), lambda i, choice: (0, 0))
    return pl.pallas_call(
        functools.partial(muon_kernel, scalar_row),
        grid_spec=pltpu.PrefetchScalarGridSpec(
            num_scalar_prefetch=1,
            grid=(1,),
            in_specs=[
                pl.BlockSpec(memory_space=pltpu.SMEM),
                pl.BlockSpec((1, rows, width), lambda i, choice: (choice[0], 0, 0)),
                pl.BlockSpec(joint.shape, lambda i, choice: (0, 0)),
                pl.BlockSpec((width, width), lambda i, choice: (2 * FF // width, 0)),
                pl.BlockSpec(
                    (rows, width), lambda i, choice: (jnp.maximum(choice[0] - 1, 0), 0)
                ),
            ],
            out_specs=[pl.BlockSpec((own, width), lambda i, choice: (0, 0)), single, single],
            scratch_shapes=[pltpu.VMEM((rows, width), jnp.float32)],
        ),
        out_shape=[
            jax.ShapeDtypeStruct((own, width), jnp.bfloat16),
            jax.ShapeDtypeStruct((1, 1), jnp.float32),
            jax.ShapeDtypeStruct((1, 1), jnp.float32),
        ],
        cost_estimate=small_cost(),
        compiler_params=kernel_params(),
    )(jnp.stack([matrix, pos]), rest_square.reshape(1, 1), mom_full, joint, sum_rest, sum_rest)


def share_turned(turned, moments):
    across = partner_swap(turned, "wide", 2)
    across, moments = lax.optimization_barrier((across, moments))
    beside = partner_swap(turned, "wide", 1)
    corner = partner_swap(across, "wide", 1)
    return (turned, beside, across, corner), moments


def moment_kernel(pos_ref, factor_ref, qkv_ref, proj_ref, up_ref, down_ref, *refs):
    own_refs, moment_refs = refs[:3], refs[3:]
    pos = pos_ref[0]
    factor = factor_ref[0, 0]
    own = own_refs[2].shape[0]
    proj_share = jnp.where(pos == FF // own - 1, 1.0, 0.0)
    first = jnp.where(
        proj_share > 0.5, proj_ref[...].astype(jnp.float32), qkv_ref[...].astype(jnp.float32)
    )
    moment_refs[0][...] = muon_decay * own_refs[0][...] + factor * first.T
    second = up_ref[...].astype(jnp.float32)
    moment_refs[1][...] = muon_decay * own_refs[1][...] + factor * second.T
    third = down_ref[...].astype(jnp.float32)
    moment_refs[2][...] = muon_decay * own_refs[2][...] + factor * third


def own_moments(pos, factor, sum_qkv, sum_rest, moms):
    own, width = moms[2].shape
    parts = FF // own
    whole = pl.BlockSpec((own, width), lambda i, pos: (0, 0))
    return pl.pallas_call(
        moment_kernel,
        grid_spec=pltpu.PrefetchScalarGridSpec(
            num_scalar_prefetch=1,
            grid=(1,),
            in_specs=[
                pl.BlockSpec(memory_space=pltpu.SMEM),
                pl.BlockSpec((width, width), lambda i, pos: (0, jnp.minimum(pos[0], 2))),
                pl.BlockSpec((width, width), lambda i, pos: (2 * FF // width, 0)),
                pl.BlockSpec((own, width), lambda i, pos: (pos[0], 0)),
                pl.BlockSpec((own, width), lambda i, pos: (parts + pos[0], 0)),
            ]
            + [whole] * 3,
            out_specs=[whole] * 3,
        ),
        out_shape=[jax.ShapeDtypeStruct((own, width), jnp.float32)] * 3,
        cost_estimate=small_cost(),
        compiler_params=kernel_params(),
    )(
        pos.reshape(1),
        factor.reshape(1, 1),
        sum_qkv,
        sum_rest,
        sum_rest,
        sum_rest,
        *moms,
    )


def step_kernel(group_ref, own_ref, beside_ref, across_ref, corner_ref, *refs):
    rates = [
        muon_rate * math.sqrt(max(1.0, LATENT_WIDTH / FF)),
        muon_rate * math.sqrt(max(1.0, LATENT_WIDTH / FF)),
        muon_rate * math.sqrt(max(1.0, FF / LATENT_WIDTH)),
    ]
    group = group_ref[0]
    low_side = group < 2
    even = group % 2 == 0
    own, beside, across, corner = [
        ref[...].astype(jnp.float32) for ref in (own_ref, beside_ref, across_ref, corner_ref)
    ]
    near, far = jnp.where(low_side, own, across), jnp.where(low_side, beside, corner)
    parts = [
        jnp.where(even, near, far),
        jnp.where(even, far, near),
        jnp.where(low_side, across, own),
    ]
    for place in range(3):
        change = parts[place] if place == 2 else parts[place].T
        new = refs[place][...] - rates[place] * change
        refs[6 + place][...] = new
        refs[9 + place][...] = ema_keep * refs[3 + place][...] + (1.0 - ema_keep) * new


def take_step(group, turned, weights, averages):
    whole = pl.BlockSpec(memory_space=pltpu.VMEM)
    return pl.pallas_call(
        step_kernel,
        in_specs=[pl.BlockSpec(memory_space=pltpu.SMEM)] + [whole] * 10,
        out_specs=[whole] * 6,
        out_shape=[jax.ShapeDtypeStruct(weights[0].shape, jnp.float32)] * 6,
        cost_estimate=small_cost(),
        compiler_params=kernel_params(),
    )(group.reshape(1), *turned, *weights, *averages)


def adam_update(weight, grad, first, second):
    first_new = beta_one * first + (1.0 - beta_one) * grad
    second_new = beta_two * second + (1.0 - beta_two) * grad * grad
    first_hat = first_new / (1.0 - beta_one**STEP_NUMBER)
    second_hat = second_new / (1.0 - beta_two**STEP_NUMBER)
    weight_new = weight - adam_rate * (
        first_hat / (jnp.sqrt(second_hat) + adam_eps) + decay_rate * weight
    )
    return (weight_new, first_new, second_new)


def on_device(
    prior_states,
    target,
    noise_draw,
    level_index,
    g2m_edges,
    neighbours,
    m2g_edges,
    valid_mask,
    channel_weights,
    w_embed,
    w_cond,
    w_attn,
    w_up,
    w_down,
    w_dec,
    biases,
    mom_attn,
    mom_up,
    mom_down,
    m_embed,
    v_embed,
    m_cond,
    v_cond,
    m_dec,
    v_dec,
    m_bias,
    v_bias,
    ema_embed,
    ema_cond,
    ema_attn,
    ema_up,
    ema_down,
    ema_dec,
    ema_bias,
):
    narrow_pos = lax.axis_index("narrow")
    narrow_count = lax.axis_size("narrow")
    pixel_local = valid_mask.shape[1]
    node_local = neighbours.shape[1]
    pixel_total = pixel_local * narrow_count
    node_total = node_local * narrow_count
    embed_low = w_embed.astype(jnp.bfloat16)
    dec_low = w_dec.astype(jnp.bfloat16)
    bias_embed = biases[:LATENT_WIDTH].reshape(1, LATENT_WIDTH)
    bias_up = biases[LATENT_WIDTH : LATENT_WIDTH + FF]
    bias_out = biases[LATENT_WIDTH + FF :]
    noise_level, scale_in, skip_scale, out_scale, loss_scale = sigma_terms(level_index[0])
    target_rows = target[0].astype(jnp.float32)
    noisy = target_rows + noise_level * noise_draw[0].astype(jnp.float32)
    features = jnp.concatenate(
        [prior_states[0, 0], prior_states[0, 1], (scale_in * noisy).astype(jnp.bfloat16)], axis=0
    )
    lat_weight = lat_weights(narrow_pos * pixel_local, pixel_local, pixel_total)
    pixel_weight = lat_weight * valid_mask[0].astype(jnp.float32)
    near_ids = (neighbours[0] - narrow_pos * node_local) % node_total
    m2g_ids = (m2g_edges[0] - narrow_pos * node_local) % node_total
    near_bias = count_bias(near_ids, node_total)
    m2g_counts = count_matrix(m2g_ids, node_total)

    feature_slots, node_sums = [], []

    def use_slot(features_here, source):
        node_sums.append(
            gather_sum(
                source * pixel_local,
                g2m_cols,
                features_here,
                embed_low,
                bias_embed,
                node_sums[-1] if node_sums else None,
            )
        )
        feature_slots.append((features_here, source))
        return node_sums[-1], near_bias

    piece_rows = LATENT_WIDTH // lax.axis_size("wide")
    piece_first = lax.axis_index("wide") * piece_rows
    def own_pieces(one, two, three):
        pieces = [
            lax.dynamic_slice_in_dim(part, piece_first, piece_rows, 1).T for part in (one, two)
        ] + [lax.dynamic_slice_in_dim(three, piece_first, piece_rows, 0)]
        return jnp.concatenate(pieces, axis=0).astype(jnp.bfloat16)

    g2m_own = g2m_edges[0].T
    id_rows = g2m_own.size // LATENT_WIDTH
    packed = jnp.concatenate(
        [
            (g2m_own // 128).reshape(id_rows, LATENT_WIDTH).astype(jnp.bfloat16),
            (g2m_own % 128).reshape(id_rows, LATENT_WIDTH).astype(jnp.bfloat16),
            own_pieces(w_attn, w_up, w_down),
        ],
        axis=0,
    )
    padded = [
        pad_rows(values)
        for values in (
            target[0],
            noise_draw[0],
            channel_weights.reshape(-1, 1),
            bias_out.reshape(-1, 1),
        )
    ]
    packed_slots, near_bias, padded = lax.optimization_barrier(
        (ring_slots(packed), near_bias, padded)
    )
    id_slots = [
        (
            slot[:id_rows].astype(jnp.float32) * 128.0
            + slot[id_rows : 2 * id_rows].astype(jnp.float32)
        )
        .astype(jnp.int32)
        .reshape(g2m_own.shape)
        for slot in packed_slots
    ]
    g2m_rows = jnp.concatenate(id_slots, axis=1)
    g2m_cols = g2m_rows.T
    weight_near = in_order([slot[2 * id_rows :] for slot in packed_slots])
    weight_all = lax.all_gather(weight_near, "wide", axis=0)
    weight_full = weight_all.transpose(2, 1, 0, 3, 4).reshape(3, -1, LATENT_WIDTH)
    later = [() for _ in range(narrow_count)]
    later[narrow_count - 2] = own_pieces(mom_attn, mom_up, mom_down)
    later[max(narrow_count - 3, 0)] = weight_full
    line_slots(features, use_slot, later)
    mom_near = in_order(ring_slots(later[narrow_count - 2]))
    weight_full = later[max(narrow_count - 3, 0)]
    attn_rows, up_rows, down_full = weight_full[0], weight_full[1], weight_full[2]
    conditioning = cond_features(noise_level)
    modulation = jnp.dot(conditioning, w_cond, precision=highest_precision)
    gain_two = 1.0 + modulation[2 * LATENT_WIDTH : 3 * LATENT_WIDTH]
    shifts = modulation.reshape(4, LATENT_WIDTH) + jnp.array([[1.0], [0.0], [1.0], [0.0]])
    node_sum = node_sums[-1]
    proj_map = attn_rows[3 * LATENT_WIDTH :]
    attn_in, query_rows, pair_rows = project(node_sum, shifts, attn_rows, node_local)
    pair_rows, mom_near = lax.optimization_barrier((pair_rows, mom_near))
    mom_all = lax.all_gather(mom_near, "wide", axis=0)
    attended, mass = attend(query_rows, pair_rows, near_bias)
    attended_rows = attended.astype(jnp.bfloat16)
    node_mid = node_sum[:node_local] / G2M_K + contract_last(attended_rows, proj_map)
    normed_two, inverse_two = norm_stats(node_mid)
    mlp_in = (normed_two * gain_two + modulation[3 * LATENT_WIDTH :]).astype(jnp.bfloat16)
    up_pre = contract_last(mlp_in, up_rows) + bias_up
    hidden = jax.nn.silu(up_pre).astype(jnp.bfloat16)
    node_out = node_mid + jnp.dot(hidden, down_full, preferred_element_type=jnp.float32)
    node_low = node_out.astype(jnp.bfloat16)
    node_raw = lax.dot_general(
        dec_low, node_low, (((0,), (1,)), ((), ())), preferred_element_type=jnp.float32
    ).astype(jnp.bfloat16)
    node_raw, mom_all = lax.optimization_barrier((node_raw, mom_all))
    all_raw = jnp.concatenate(ring_slots(node_raw), axis=1)
    raw_spread, out_bias_sum, loss_sum_local = decode(
        jnp.stack([noise_level, skip_scale, out_scale, loss_scale]),
        m2g_counts,
        pad_rows(all_raw),
        padded[0],
        padded[1],
        pixel_weight.reshape(1, pixel_local),
        padded[2],
        padded[3],
    )
    loss_local = loss_sum_local[0, 0]
    grad_out_bias = out_bias_sum[: bias_out.shape[0], 0]
    raw_spread = raw_spread[: bias_out.shape[0]]
    grad_node_raw = (
        ring_sum(
            [
                raw_spread[:, slot * node_local : (slot + 1) * node_local]
                for slot in range(narrow_count)
            ]
        )
        / M2G_K
    )
    grad_dec = lax.dot_general(
        node_low.astype(jnp.float32),
        grad_node_raw,
        (((0,), (1,)), ((), ())),
        precision=highest_precision,
    )
    grad_node_out = lax.dot_general(
        grad_node_raw,
        dec_low.astype(jnp.float32),
        (((0,), (1,)), ((), ())),
        precision=highest_precision,
    )
    grad_mlp = grad_node_out.astype(jnp.bfloat16)
    grad_down = contract_rows(hidden, grad_mlp)
    grad_hidden = contract_last(grad_mlp, down_full)
    grad_up_pre = (grad_hidden * silu_slope(up_pre)).astype(jnp.bfloat16)
    grad_up_bias = jnp.sum(grad_up_pre.astype(jnp.float32), axis=0)
    grad_up = contract_rows(grad_up_pre, mlp_in)
    grad_mlp_in = plain_dot(grad_up_pre, up_rows)
    grad_node_mid = grad_node_out + norm_back(grad_mlp_in * gain_two, normed_two, inverse_two)
    grad_proj_out = grad_node_mid.astype(jnp.bfloat16)
    grad_proj = contract_rows(grad_proj_out, attended_rows)
    early = jnp.concatenate([grad_up, grad_down, grad_proj], axis=0).astype(jnp.bfloat16)
    gradient_attended = plain_dot(grad_proj_out, proj_map).astype(jnp.bfloat16)
    early, gradient_attended = lax.optimization_barrier((early, gradient_attended))
    early = lax.psum(early, ("wide", "narrow"))
    grad_query_rows, grad_key_rows, grad_value_rows = attend_back(
        query_rows, pair_rows, near_bias, mass, attended, gradient_attended
    )
    node_grads, grad_qkv, column_sums = project_back(
        grad_query_rows,
        grad_key_rows,
        grad_value_rows,
        node_sum,
        attn_in,
        grad_node_mid,
        shifts,
        attn_rows,
    )
    grad_modulation = jnp.concatenate(
        [
            column_sums[0],
            column_sums[1],
            jnp.sum(grad_mlp_in * normed_two, axis=0),
            jnp.sum(grad_mlp_in, axis=0),
        ]
    )
    grad_cond = conditioning[:, None] * grad_modulation[None, :]
    grad_embed = None
    grad_embed_bias = None
    for features_here, source in feature_slots:
        embed_part, bias_part = scatter_sum(
            source * pixel_local, g2m_rows, node_grads, features_here, embed_low, bias_embed
        )
        grad_embed = embed_part if grad_embed is None else grad_embed + embed_part
        grad_embed_bias = bias_part if grad_embed_bias is None else grad_embed_bias + bias_part
    width = LATENT_WIDTH
    channels = w_dec.shape[1]
    late_rows = jnp.concatenate(
        [
            grad_embed,
            grad_embed_bias.reshape(1, width),
            grad_up_bias.reshape(FF // width, width),
            jnp.pad(grad_out_bias, (0, width - channels)).reshape(1, width),
            grad_dec.T,
        ]
        + [grad_cond[:, place * width : (place + 1) * width] for place in range(4)]
        + [
            jnp.pad(
                jnp.concatenate([loss_local.reshape(1), jnp.sum(pixel_weight).reshape(1)]),
                (0, width - 2),
            ).reshape(1, width),
        ],
        axis=0,
    )
    scalar_row = late_rows.shape[0] - 1
    late_rows = jnp.pad(late_rows, ((0, width - late_rows.shape[0]), (0, 0)))
    late_rows, grad_qkv, early = lax.optimization_barrier((late_rows, grad_qkv, early))
    early_square = jnp.sum(jnp.square(early.astype(jnp.float32)))
    late_rows, mom_all = lax.optimization_barrier((late_rows, mom_all))
    mom_full = mom_all.transpose(2, 1, 0, 3, 4).reshape(3, -1, LATENT_WIDTH)
    joint, early_square, mom_full = joint_sum(grad_qkv, late_rows, (early_square, mom_full))
    _, late_rows = joint_split(joint, 3 * LATENT_WIDTH)
    embed_rows = w_embed.shape[0]
    sum_embed = late_rows[:embed_rows]
    place = embed_rows
    bias_rows = late_rows[place : place + 2 + FF // width].reshape(-1)
    sum_bias = bias_rows[: biases.shape[0]]
    loss_sum = late_rows[scalar_row, 0]
    weight_total = late_rows[scalar_row, 1]
    place += 2 + FF // width
    sum_dec = late_rows[place : place + channels].T
    place += channels
    sum_cond = jnp.concatenate(
        [late_rows[place + COND * part : place + COND * (part + 1)] for part in range(4)], axis=1
    )
    group = lax.axis_index("wide") % 4
    turned, factor, grad_norm = turn_moment(
        jnp.minimum(group, 2),
        narrow_pos,
        early_square,
        scalar_row,
        mom_full,
        joint,
        early,
        w_down.shape[0],
    )
    factor, grad_norm = factor[0, 0], grad_norm[0, 0]
    moments = own_moments(
        narrow_pos, factor, joint, early, (mom_attn, mom_up, mom_down)
    )
    turned, moments = share_turned(turned, moments)
    moment_attn, moment_up, moment_down = moments
    new_attn, new_up, new_down, average_attn, average_up, average_down = take_step(
        group, turned, (w_attn, w_up, w_down), (ema_attn, ema_up, ema_down)
    )
    new_embed, first_embed, second_embed = adam_update(
        w_embed, factor * sum_embed, m_embed, v_embed
    )
    new_cond, first_cond, second_cond = adam_update(w_cond, factor * sum_cond, m_cond, v_cond)
    new_dec, first_dec, second_dec = adam_update(w_dec, factor * sum_dec, m_dec, v_dec)
    new_bias, first_bias, second_bias = adam_update(biases, factor * sum_bias, m_bias, v_bias)
    keep_rest = 1.0 - ema_keep
    return (
        new_attn,
        new_up,
        new_down,
        moment_attn,
        moment_up,
        moment_down,
        new_embed,
        new_cond,
        new_dec,
        new_bias,
        first_embed,
        second_embed,
        first_cond,
        second_cond,
        first_dec,
        second_dec,
        first_bias,
        second_bias,
        ema_keep * ema_embed + keep_rest * new_embed,
        ema_keep * ema_cond + keep_rest * new_cond,
        average_attn,
        average_up,
        average_down,
        ema_keep * ema_dec + keep_rest * new_dec,
        ema_keep * ema_bias + keep_rest * new_bias,
        loss_sum,
        weight_total,
        grad_norm,
    )


def solution(mesh):
    in_specs = (
        P("wide", None, None, "narrow"),
        P("wide", None, "narrow"),
        P("wide", None, "narrow"),
        P("wide"),
        P("wide", "narrow", None),
        P("wide", "narrow", None),
        P("wide", "narrow", None),
        P("wide", "narrow"),
        P(),
        P(),
        P(),
        P(None, "narrow"),
        P(None, "narrow"),
        P("narrow", None),
        P(),
        P(),
        P(None, "narrow"),
        P(None, "narrow"),
        P("narrow", None),
        P(),
        P(),
        P(),
        P(),
        P(),
        P(),
        P(),
        P(),
        P(),
        P(),
        P(None, "narrow"),
        P(None, "narrow"),
        P("narrow", None),
        P(),
        P(),
    )
    out_specs = (
        P(None, "narrow"),
        P(None, "narrow"),
        P("narrow", None),
        P(None, "narrow"),
        P(None, "narrow"),
        P("narrow", None),
        P(),
        P(),
        P(),
        P(),
        P(),
        P(),
        P(),
        P(),
        P(),
        P(),
        P(),
        P(),
        P(),
        P(),
        P(None, "narrow"),
        P(None, "narrow"),
        P("narrow", None),
        P(),
        P(),
        P(),
        P(),
        P(),
    )
    return jax.shard_map(
        on_device, mesh=mesh, in_specs=in_specs, out_specs=out_specs, check_vma=False
    )
```

```python
import functools
import math

import jax
import jax.numpy as jnp
from jax import lax
from jax.experimental import pallas as pl
from jax.experimental.pallas import tpu as pltpu
from jax.sharding import PartitionSpec as P

LATENT_WIDTH = 512
HEADS = 4
HEAD_WIDTH = 128
FF = 2048
COND = 32
NBR = 32
G2M_K = 4
M2G_K = 3
NS_ITERS = 5
SIGMA_LEVELS = 8
STEP_NUMBER = 10


highest_precision = lax.Precision.HIGHEST
sigma_low = 0.25
sigma_high = 4.0
clip_bound = 0.02
muon_rate = 0.5
muon_decay = 0.95
adam_rate = 0.03
beta_one = 0.9
beta_two = 0.95
adam_eps = 1e-08
decay_rate = 0.01
ema_keep = 0.9
coef_a = 3.4445
coef_b = -4.775
coef_c = 2.0315


def sigma_terms(level):
    fraction = level.astype(jnp.float32) / (SIGMA_LEVELS - 1)
    noise_level = sigma_low * (sigma_high / sigma_low) ** fraction
    square = noise_level * noise_level + 1.0
    scale_in = lax.rsqrt(square)
    return (
        noise_level,
        scale_in,
        1.0 / square,
        noise_level * scale_in,
        square / (noise_level * noise_level),
    )


def cond_features(noise_level):
    frequencies = 1.0 + jnp.arange(COND // 2).astype(jnp.float32)
    phases = jnp.log(noise_level) * frequencies
    return jnp.concatenate([jnp.sin(phases), jnp.cos(phases)])


def lat_weights(first_row, row_count, pixel_total):
    row_ids = (first_row + jnp.arange(row_count, dtype=jnp.int32)).astype(jnp.float32)
    return jnp.cos(math.pi * ((row_ids + 0.5) / pixel_total - 0.5))


def norm_stats(values):
    centred = values - jnp.mean(values, axis=-1, keepdims=True)
    inverse = lax.rsqrt(jnp.mean(centred * centred, axis=-1, keepdims=True) + 1e-05)
    return (centred * inverse, inverse)


def norm_back(grad_normed, normed, inverse):
    first_mean = jnp.mean(grad_normed, axis=-1, keepdims=True)
    second_mean = jnp.mean(grad_normed * normed, axis=-1, keepdims=True)
    return inverse * (grad_normed - first_mean - normed * second_mean)


def silu_slope(values):
    sigmoid_values = jax.nn.sigmoid(values)
    return sigmoid_values * (1.0 + values * (1.0 - sigmoid_values))


def contract_rows(left, right):
    return lax.dot_general(
        left, right, (((0,), (0,)), ((), ())), preferred_element_type=jnp.float32
    )


def contract_last(left, right):
    return lax.dot_general(
        left, right, (((1,), (1,)), ((), ())), preferred_element_type=jnp.float32
    )


def axis_bits(axis_name):
    bits = []
    reach = 1
    while reach < lax.axis_size(axis_name):
        bits.append((axis_name, len(bits)))
        reach *= 2
    return bits


def sum_stages():
    wide_bits = len(axis_bits("wide"))
    stages = [("wide", 0, 1)]
    first = 1
    while first < wide_bits:
        stages.append(("wide", first, min(2, wide_bits - first)))
        first += 2
    stages.append(("narrow", 0, len(axis_bits("narrow"))))
    return stages


def partner_swap(values, axis_name, distance):
    size = lax.axis_size(axis_name)
    return lax.ppermute(values, axis_name, [(i, i ^ distance) for i in range(size)])


def joint_pieces(coarse, fine):
    upper = fine.astype(jnp.bfloat16)
    lower = (fine - lax.optimization_barrier(upper).astype(jnp.float32)).astype(jnp.bfloat16)
    return jnp.concatenate([coarse.astype(jnp.bfloat16), upper, lower], axis=1)


def joint_split(pieces, coarse_width):
    coarse = pieces[:, :coarse_width]
    fine_width = (pieces.shape[1] - coarse_width) // 2
    upper = pieces[:, coarse_width : coarse_width + fine_width].astype(jnp.float32)
    return coarse, upper + pieces[:, coarse_width + fine_width :].astype(jnp.float32)


def joint_sum(coarse, fine, beside):
    coarse_width = coarse.shape[1]
    stages = sum_stages()
    for axis_name, first, width in stages:
        members = 1 << width
        block = fine.shape[0] // members
        mine = (lax.axis_index(axis_name) >> first) & (members - 1)
        arrived = []
        for far in range(1, members):
            begin = (mine ^ far) * block
            piece = joint_pieces(
                lax.dynamic_slice_in_dim(coarse, begin, block, 0),
                lax.dynamic_slice_in_dim(fine, begin, block, 0),
            )
            arrived.append(partner_swap(piece, axis_name, far << first))
        if first == 1 and axis_name == "wide":
            arrived, beside = lax.optimization_barrier((arrived, beside))
        coarse = lax.dynamic_slice_in_dim(coarse, mine * block, block, 0)
        fine = lax.dynamic_slice_in_dim(fine, mine * block, block, 0)
        for piece in arrived:
            more_coarse, more_fine = joint_split(piece, coarse_width)
            coarse = coarse + more_coarse.astype(jnp.float32)
            fine = fine + more_fine
    values = joint_pieces(coarse, fine)
    for axis_name, first, width in stages[::-1]:
        members = 1 << width
        mine = (lax.axis_index(axis_name) >> first) & (members - 1)
        pieces = [values] + [
            partner_swap(values, axis_name, far << first) for far in range(1, members)
        ]
        for bit in range(width):
            is_high = ((mine >> bit) & 1) == 1
            step = 1 << bit
            pieces = [
                jnp.where(is_high, pieces[place ^ step], pieces[place])
                for place in range(members)
            ]
        values = jnp.concatenate(pieces, axis=0)
    return values, *beside


def ring_slots(values):
    size = lax.axis_size("narrow")
    slots = [values]
    for shift in range(1, size):
        slots.append(
            lax.ppermute(values, "narrow", [((i + shift) % size, i) for i in range(size)])
        )
    return slots


def line_slots(values, use_slot, later):
    size = lax.axis_size("narrow")
    pos = lax.axis_index("narrow")
    from_low, from_high = values, values
    arrived = {}
    orders = [
        sorted((s for s in range(size) if s != n), key=lambda s, n=n: (abs(s - n), s < n))
        for n in range(size)
    ]
    chosen, source = values, pos
    for step in range(size):
        if step < size - 1:
            from_low = lax.ppermute(
                from_low, "narrow", [(i, i + 1) for i in range(step, size - 1)]
            )
            from_high = lax.ppermute(
                from_high, "narrow", [(i, i - 1) for i in range(1, size - step)]
            )
        result = use_slot(chosen, source)
        if step == size - 1:
            return
        from_low, from_high, _, later[step] = lax.optimization_barrier(
            (from_low, from_high, result, later[step])
        )
        arrived[-1 - step] = from_low
        arrived[1 + step] = from_high
        offsets = [orders[n][step] - n for n in range(size)]
        chosen = arrived[offsets[0]]
        for offset in sorted(set(offsets) - {offsets[0]}):
            here = functools.reduce(
                jnp.logical_or, [pos == n for n in range(size) if offsets[n] == offset]
            )
            chosen = jnp.where(here, arrived[offset], chosen)
        source = pos + jnp.array(offsets, jnp.int32)[pos]


def in_order(slots):
    size = lax.axis_size("narrow")
    pos = lax.axis_index("narrow")
    rows, width = slots[0].shape
    across = jnp.zeros((size, 3, rows // 3, width), slots[0].dtype)
    for shift, piece in enumerate(slots):
        across = lax.dynamic_update_slice_in_dim(
            across, piece.reshape(1, 3, rows // 3, width), (pos + shift) % size, 0
        )
    return across


def ring_sum(parts, beside):
    size = lax.axis_size("narrow")
    arrived = [
        lax.ppermute(
            parts[shift], "narrow", [(i, (i + shift) % size) for i in range(size)]
        )
        for shift in range(1, size)
    ]
    arrived, beside = lax.optimization_barrier((arrived, beside))
    total = parts[0].astype(jnp.float32)
    for piece in arrived:
        total = total + piece.astype(jnp.float32)
    return total, beside


VMEM_LIMIT = 60 * 1024 * 1024
SCORE_SCALE = math.log2(math.e) / math.sqrt(HEAD_WIDTH)
MASKED = -1e30


def small_cost():
    return pl.CostEstimate(flops=1 << 20, bytes_accessed=1 << 20, transcendentals=0)


def kernel_params():
    return pltpu.CompilerParams(vmem_limit_bytes=VMEM_LIMIT)


def count_kernel(ids_ref, out_ref):
    first = pl.program_id(0) * out_ref.shape[1]
    columns = lax.broadcasted_iota(jnp.int32, out_ref.shape, 1).astype(jnp.int16)
    ids = (ids_ref[...] - first).astype(jnp.int16)
    one = jnp.ones(out_ref.shape, jnp.bfloat16)
    zero = jnp.zeros(out_ref.shape, jnp.bfloat16)
    total = zero
    for slot in range(ids.shape[1]):
        total = total + jnp.where(ids[:, slot : slot + 1] == columns, one, zero)
    out_ref[...] = total


def count_matrix(ids, column_count, rows=1024, columns=2048):
    row_count, slots = ids.shape
    rows = min(rows, row_count)
    columns = min(columns, column_count)
    return pl.pallas_call(
        count_kernel,
        grid=(column_count // columns, row_count // rows),
        in_specs=[pl.BlockSpec((rows, slots), lambda j, i: (i, 0))],
        out_specs=pl.BlockSpec((rows, columns), lambda j, i: (i, j)),
        out_shape=jax.ShapeDtypeStruct((row_count, column_count), jnp.bfloat16),
        cost_estimate=small_cost(),
        compiler_params=kernel_params(),
    )(ids)


def bias_kernel(row_ref, lane_ref, out_ref):
    groups, width = row_ref.shape
    blocks = out_ref.shape[1] // 128
    row_iota = lax.broadcasted_iota(jnp.int32, (8 * blocks, width), 0)
    lane_iota = lax.broadcasted_iota(jnp.int32, (128, width), 0)
    for group in range(groups):
        left = jnp.where(row_iota == row_ref[group : group + 1, :], 1.0, 0.0)
        right = jnp.where(lane_iota == lane_ref[group : group + 1, :], 1.0, 0.0)
        counts = contract_last(left.astype(jnp.bfloat16), right.astype(jnp.bfloat16))
        bias = jnp.where(counts > 0.5, jnp.log2(counts), MASKED)
        for block in range(blocks):
            out_ref[group * 8 : (group + 1) * 8, block * 128 : (block + 1) * 128] = bias[
                block * 8 : (block + 1) * 8, :
            ]


def count_bias(ids, total, per_step=32):
    row_count, slots = ids.shape
    groups = row_count // 8
    member = (jnp.arange(row_count, dtype=jnp.int32) % 8)[:, None]
    row_keys = ((ids // 128) * 8 + member).reshape(groups, 8 * slots)
    lane_keys = (ids % 128).reshape(groups, 8 * slots)
    spec = pl.BlockSpec((per_step, 8 * slots), lambda i: (i, 0))
    return pl.pallas_call(
        bias_kernel,
        grid=(groups // per_step,),
        in_specs=[spec, spec],
        out_specs=pl.BlockSpec((8 * per_step, total), lambda i: (i, 0)),
        out_shape=jax.ShapeDtypeStruct((row_count, total), jnp.float32),
        cost_estimate=small_cost(),
        compiler_params=kernel_params(),
    )(row_keys, lane_keys)


def attend_kernel(chunk, q_ref, k_ref, v_ref, bias_ref, att_ref, mass_ref):
    q = q_ref[...]
    top = jnp.full((q.shape[0], 1), -jnp.inf, jnp.float32)
    mass = jnp.zeros((q.shape[0], 1), jnp.float32)
    attended = jnp.zeros(att_ref.shape, jnp.float32)
    for start in range(0, k_ref.shape[0], chunk):
        part = pl.ds(start, chunk)
        scores = contract_last(q, k_ref[part, :]) * SCORE_SCALE + bias_ref[:, part]
        higher = jnp.maximum(top, jnp.max(scores, axis=1, keepdims=True))
        raised = jnp.exp2(scores - higher)
        shrink = jnp.exp2(top - higher)
        mass = mass * shrink + jnp.sum(raised, axis=1, keepdims=True)
        attended = attended * shrink + jnp.dot(
            raised.astype(jnp.bfloat16), v_ref[part, :], preferred_element_type=jnp.float32
        )
        top = higher
    att_ref[...] = attended / mass
    mass_ref[...] = jnp.broadcast_to(top + jnp.log2(mass), mass_ref.shape)


def attend(queries, pairs, bias, rows=1024, chunk=512):
    row_count = queries.shape[0]
    rows = min(rows, row_count)
    total = pairs.shape[0]
    block = pl.BlockSpec((rows, HEAD_WIDTH), lambda h, r: (r, h))
    return pl.pallas_call(
        functools.partial(attend_kernel, chunk),
        grid=(HEADS, row_count // rows),
        in_specs=[
            block,
            pl.BlockSpec((total, HEAD_WIDTH), lambda h, r: (0, h)),
            pl.BlockSpec((total, HEAD_WIDTH), lambda h, r: (0, HEADS + h)),
            pl.BlockSpec((rows, total), lambda h, r: (r, 0)),
        ],
        out_specs=[block, block],
        out_shape=[jax.ShapeDtypeStruct(queries.shape, jnp.float32)] * 2,
        cost_estimate=small_cost(),
        compiler_params=kernel_params(),
    )(queries, pairs, pairs, bias)


def attend_back_kernel(
    chunk,
    q_ref,
    k_ref,
    v_ref,
    bias_ref,
    mass_ref,
    att_ref,
    g_ref,
    dq_ref,
    dk_ref,
    dv_ref,
    dk_sum,
    dv_sum,
):
    step = pl.program_id(1)
    q = q_ref[...]
    g = g_ref[...]
    total = k_ref.shape[0]
    mass = mass_ref[:, :1]
    inner = jnp.sum(att_ref[...] * g.astype(jnp.float32), axis=1, keepdims=True)

    @pl.when(step == 0)
    def _():
        dk_sum[...] = jnp.zeros_like(dk_sum)
        dv_sum[...] = jnp.zeros_like(dv_sum)

    dq = jnp.zeros(q.shape, jnp.float32)
    for start in range(0, total, chunk):
        part = pl.ds(start, chunk)
        k = k_ref[part, :]
        v = v_ref[part, :]
        prob = jnp.exp2(contract_last(q, k) * SCORE_SCALE + (bias_ref[:, part] - mass))
        grad_scores = (prob * (contract_last(g, v) - inner)).astype(jnp.bfloat16)
        dq = dq + jnp.dot(grad_scores, k, preferred_element_type=jnp.float32)
        dk_sum[part, :] += contract_rows(grad_scores, q)
        dv_sum[part, :] += contract_rows(prob.astype(jnp.bfloat16), g)
    shrink = 1.0 / math.sqrt(HEAD_WIDTH)
    dq_ref[...] = (dq * shrink).astype(jnp.bfloat16)

    @pl.when(step == pl.num_programs(1) - 1)
    def _():
        dk_ref[...] = (dk_sum[...] * shrink).astype(jnp.bfloat16)
        dv_ref[...] = dv_sum[...].astype(jnp.bfloat16)


def attend_back(queries, pairs, bias, mass, attended, grads, rows=1024, chunk=256):
    row_count = queries.shape[0]
    total = pairs.shape[0]
    rows = min(rows, row_count)
    block = pl.BlockSpec((rows, HEAD_WIDTH), lambda h, r: (r, h))
    column = pl.BlockSpec((total, HEAD_WIDTH), lambda h, r: (0, h))
    key_shape = jax.ShapeDtypeStruct((total, LATENT_WIDTH), jnp.bfloat16)
    return pl.pallas_call(
        functools.partial(attend_back_kernel, chunk),
        grid=(HEADS, row_count // rows),
        in_specs=[
            block,
            column,
            pl.BlockSpec((total, HEAD_WIDTH), lambda h, r: (0, HEADS + h)),
            pl.BlockSpec((rows, total), lambda h, r: (r, 0)),
            block,
            block,
            block,
        ],
        out_specs=[block, column, column],
        out_shape=[jax.ShapeDtypeStruct(queries.shape, jnp.bfloat16), key_shape, key_shape],
        scratch_shapes=[pltpu.VMEM((total, HEAD_WIDTH), jnp.float32)] * 2,
        cost_estimate=small_cost(),
        compiler_params=kernel_params(),
    )(queries, pairs, pairs, bias, mass, attended, grads)


def gather_kernel(sub, first_ref, ids_ref, feature_ref, map_ref, bias_ref, *rest):
    out_ref, pixel_ref = rest[-2:]

    @pl.when(pl.program_id(0) == 0)
    def _():
        pre = contract_rows(feature_ref[...], map_ref[...]) + bias_ref[...]
        pixel_ref[...] = (pre / (1.0 + jnp.exp(-pre))).astype(jnp.bfloat16)

    pixels = pixel_ref[...]
    columns = lax.broadcasted_iota(jnp.int32, (sub, pixels.shape[0]), 1).astype(jnp.int16)
    one = jnp.ones(columns.shape, jnp.bfloat16)
    zero = jnp.zeros(columns.shape, jnp.bfloat16)
    for block in range(out_ref.shape[0] // sub):
        part = pl.ds(block * sub, sub)
        ids = (ids_ref[part, :] - first_ref[0, 0]).astype(jnp.int16)
        counts = zero
        for slot in range(ids.shape[1]):
            counts = counts + jnp.where(ids[:, slot : slot + 1] == columns, one, zero)
        rows = jnp.dot(counts, pixels, preferred_element_type=jnp.float32)
        if len(rest) == 3:
            rows = rows + rest[0][part, :]
        out_ref[part, :] = rows


def gather_sum(first, ids, features, embed_map, embed_bias, earlier, rows=1024, sub=256):
    row_count, slots = ids.shape
    channels, pixel_count = features.shape
    width = embed_map.shape[1]
    block = pl.BlockSpec((rows, width), lambda i: (i, 0))
    more = [] if earlier is None else [earlier]
    return pl.pallas_call(
        functools.partial(gather_kernel, sub),
        grid=(row_count // rows,),
        in_specs=[
            pl.BlockSpec(memory_space=pltpu.SMEM),
            pl.BlockSpec((rows, slots), lambda i: (i, 0)),
            pl.BlockSpec((channels, pixel_count), lambda i: (0, 0)),
            pl.BlockSpec((channels, width), lambda i: (0, 0)),
            pl.BlockSpec((1, width), lambda i: (0, 0)),
        ]
        + [block] * len(more),
        out_specs=block,
        out_shape=jax.ShapeDtypeStruct((row_count, width), jnp.float32),
        scratch_shapes=[pltpu.VMEM((pixel_count, width), jnp.bfloat16)],
        cost_estimate=small_cost(),
        compiler_params=kernel_params(),
    )(first.reshape(1, 1), ids, features, embed_map, embed_bias, *more)


def scatter_kernel(
    chunk, first_ref, ids_ref, g_ref, feature_ref, map_ref, shift_ref, grad_ref, bias_ref
):
    step = pl.program_id(0)
    rows = feature_ref.shape[1]
    pixel_ids = lax.broadcasted_iota(jnp.int32, (rows, chunk), 0).astype(jnp.int16)
    one = jnp.ones((rows, chunk), jnp.bfloat16)
    zero = jnp.zeros((rows, chunk), jnp.bfloat16)
    spread = jnp.zeros((rows, g_ref.shape[1]), jnp.float32)
    for start in range(0, g_ref.shape[0], chunk):
        part = pl.ds(start, chunk)
        counts = zero
        for slot in range(ids_ref.shape[0]):
            ids = ids_ref[slot : slot + 1, part] - (first_ref[0, 0] + step * rows)
            ids = jnp.broadcast_to(ids, (rows, chunk))
            counts = counts + jnp.where(ids.astype(jnp.int16) == pixel_ids, one, zero)
        spread = spread + jnp.dot(counts, g_ref[part, :], preferred_element_type=jnp.float32)
    pre = contract_rows(feature_ref[...], map_ref[...]) + shift_ref[...]
    sigmoid_values = 1.0 / (1.0 + jnp.exp(-pre))
    lowered = (spread * (sigmoid_values * (1.0 + pre * (1.0 - sigmoid_values)))).astype(
        jnp.bfloat16
    )

    @pl.when(step == 0)
    def _():
        grad_ref[...] = jnp.zeros_like(grad_ref)
        bias_ref[...] = jnp.zeros_like(bias_ref)

    grad_ref[...] += jnp.dot(feature_ref[...], lowered, preferred_element_type=jnp.float32)
    bias_ref[...] += jnp.sum(lowered.astype(jnp.float32), axis=0, keepdims=True)


def scatter_sum(first, ids, grads, features, embed_map, embed_bias, rows=512, chunk=1024):
    slots, node_count = ids.shape
    width = grads.shape[1]
    channels, pixel_count = features.shape
    return pl.pallas_call(
        functools.partial(scatter_kernel, chunk),
        grid=(pixel_count // rows,),
        in_specs=[
            pl.BlockSpec(memory_space=pltpu.SMEM),
            pl.BlockSpec((slots, node_count), lambda i: (0, 0)),
            pl.BlockSpec((node_count, width), lambda i: (0, 0)),
            pl.BlockSpec((channels, rows), lambda i: (0, i)),
            pl.BlockSpec((channels, width), lambda i: (0, 0)),
            pl.BlockSpec((1, width), lambda i: (0, 0)),
        ],
        out_specs=[
            pl.BlockSpec((channels, width), lambda i: (0, 0)),
            pl.BlockSpec((1, width), lambda i: (0, 0)),
        ],
        out_shape=[
            jax.ShapeDtypeStruct((channels, width), jnp.float32),
            jax.ShapeDtypeStruct((1, width), jnp.float32),
        ],
        cost_estimate=small_cost(),
        compiler_params=kernel_params(),
    )(first.reshape(1, 1), ids, grads, features, embed_map, embed_bias)


def pad_rows(values):
    return jnp.pad(values, ((0, 128 - values.shape[0]), (0, 0)))


def decode_kernel(
    scale_ref,
    count_ref,
    raw_ref,
    target_ref,
    noise_ref,
    pixel_ref,
    channel_ref,
    shift_ref,
    spread_ref,
    bias_ref,
    loss_ref,
    total_ref,
):
    step = pl.program_id(0)
    noise_level, skip_scale, out_scale, loss_scale = [scale_ref[place] for place in range(4)]
    counts = count_ref[...]
    raw = contract_last(counts, raw_ref[...]).T * (1.0 / M2G_K) + shift_ref[...]
    target = target_ref[...].astype(jnp.float32)
    noisy = target + noise_level * noise_ref[...].astype(jnp.float32)
    errors = skip_scale * noisy + out_scale * raw - target
    weighted = channel_ref[...] * pixel_ref[...] * errors
    grads = ((2.0 * loss_scale * out_scale) * weighted).astype(jnp.bfloat16).astype(jnp.float32)

    @pl.when(step == 0)
    def _():
        total_ref[...] = jnp.zeros_like(total_ref)
        bias_ref[...] = jnp.zeros_like(bias_ref)
        loss_ref[...] = jnp.zeros_like(loss_ref)

    row_loss = jnp.sum(weighted * errors, axis=1, keepdims=True)
    loss_ref[...] += loss_scale * jnp.sum(row_loss, axis=0, keepdims=True)
    bias_ref[...] += jnp.sum(grads, axis=1, keepdims=True)
    total_ref[...] += plain_dot(grads.astype(jnp.bfloat16), counts)

    @pl.when(step == pl.num_programs(0) - 1)
    def _():
        spread_ref[...] = total_ref[...].astype(jnp.bfloat16)


def decode(scales, counts, raw, target, noise, pixel_weight, channels, shifts, rows=512):
    pixel_count, node_count = counts.shape
    wide_block = pl.BlockSpec((128, rows), lambda i: (0, i))
    column = pl.BlockSpec((128, 1), lambda i: (0, 0))
    return pl.pallas_call(
        decode_kernel,
        grid=(pixel_count // rows,),
        in_specs=[
            pl.BlockSpec(memory_space=pltpu.SMEM),
            pl.BlockSpec((rows, node_count), lambda i: (i, 0)),
            pl.BlockSpec((128, node_count), lambda i: (0, 0)),
            wide_block,
            wide_block,
            pl.BlockSpec((1, rows), lambda i: (0, i)),
            column,
            column,
        ],
        out_specs=[
            pl.BlockSpec((128, node_count), lambda i: (0, 0)),
            column,
            pl.BlockSpec((1, 1), lambda i: (0, 0)),
        ],
        out_shape=[
            jax.ShapeDtypeStruct((128, node_count), jnp.bfloat16),
            jax.ShapeDtypeStruct((128, 1), jnp.float32),
            jax.ShapeDtypeStruct((1, 1), jnp.float32),
        ],
        scratch_shapes=[pltpu.VMEM((128, node_count), jnp.float32)],
        cost_estimate=small_cost(),
        compiler_params=kernel_params(),
    )(scales, counts, raw, target, noise, pixel_weight, channels, shifts)


def row_norm(sums):
    values = sums * (1.0 / G2M_K)
    centred = values - jnp.mean(values, axis=1, keepdims=True)
    inverse = lax.rsqrt(jnp.mean(centred * centred, axis=1, keepdims=True) + 1e-05)
    return centred * inverse, inverse


def project_kernel(sum_ref, shift_ref, map_ref, attn_ref, query_ref, pair_ref):
    width = sum_ref.shape[1]
    normed, _ = row_norm(sum_ref[...])
    attn_in = (normed * shift_ref[0:1, :] + shift_ref[1:2, :]).astype(jnp.bfloat16)
    attn_ref[...] = attn_in
    for place in range(2):
        part = pl.ds(place * width, width)
        weights = map_ref[pl.ds((place + 1) * width, width), :]
        pair_ref[:, part] = contract_last(attn_in, weights).astype(jnp.bfloat16)

    @pl.when(pl.program_id(0) == 0)
    def _():
        query_ref[...] = contract_last(attn_in, map_ref[pl.ds(0, width), :]).astype(jnp.bfloat16)


def project(sums, shifts, attn_map, rows):
    row_count, width = sums.shape
    block = pl.BlockSpec((rows, width), lambda i: (i, 0))
    return pl.pallas_call(
        project_kernel,
        grid=(row_count // rows,),
        in_specs=[
            block,
            pl.BlockSpec(shifts.shape, lambda i: (0, 0)),
            pl.BlockSpec(attn_map.shape, lambda i: (0, 0)),
        ],
        out_specs=[
            block,
            pl.BlockSpec((rows, width), lambda i: (0, 0)),
            pl.BlockSpec((rows, 2 * width), lambda i: (i, 0)),
        ],
        out_shape=[
            jax.ShapeDtypeStruct((row_count, width), jnp.bfloat16),
            jax.ShapeDtypeStruct((rows, width), jnp.bfloat16),
            jax.ShapeDtypeStruct((row_count, 2 * width), jnp.bfloat16),
        ],
        cost_estimate=small_cost(),
        compiler_params=kernel_params(),
    )(sums, shifts, attn_map)


def project_back_kernel(
    dq_ref,
    dk_ref,
    dv_ref,
    sum_ref,
    attn_ref,
    mid_ref,
    shift_ref,
    map_ref,
    node_ref,
    grad_ref,
    column_ref,
    back_ref,
):
    step = pl.program_id(0)
    width = sum_ref.shape[1]
    attn_in = attn_ref[...]
    dk, dv = dk_ref[...], dv_ref[...]
    back_ref[...] = plain_dot(dk, map_ref[pl.ds(width, width), :]) + plain_dot(
        dv, map_ref[pl.ds(2 * width, width), :]
    )

    @pl.when(step == 0)
    def _():
        grad_ref[...] = jnp.zeros_like(grad_ref)
        column_ref[...] = jnp.zeros_like(column_ref)
        dq = dq_ref[...]
        back_ref[...] += plain_dot(dq, map_ref[pl.ds(0, width), :])
        grad_ref[:, pl.ds(0, width)] = contract_rows(dq, attn_in)

    grad_ref[:, pl.ds(width, width)] += contract_rows(dk, attn_in)
    grad_ref[:, pl.ds(2 * width, width)] += contract_rows(dv, attn_in)
    back = back_ref[...]
    normed, inverse = row_norm(sum_ref[...])
    column_ref[0:1, :] += jnp.sum(back * normed, axis=0, keepdims=True)
    column_ref[1:2, :] += jnp.sum(back, axis=0, keepdims=True)
    grads = back * shift_ref[0:1, :]
    first_mean = jnp.mean(grads, axis=1, keepdims=True)
    second_mean = jnp.mean(grads * normed, axis=1, keepdims=True)
    grads = inverse * (grads - first_mean - normed * second_mean)
    own_share = jnp.where(step == 0, 1.0, 0.0)
    node_ref[...] = ((grads + own_share * mid_ref[...]) * (1.0 / G2M_K)).astype(jnp.bfloat16)


def project_back(dq, dk, dv, sums, attn_in, mid, shifts, attn_map):
    row_count, width = sums.shape
    rows = dq.shape[0]
    block = pl.BlockSpec((rows, width), lambda i: (i, 0))
    own = pl.BlockSpec((rows, width), lambda i: (0, 0))
    return pl.pallas_call(
        project_back_kernel,
        grid=(row_count // rows,),
        in_specs=[
            own,
            block,
            block,
            block,
            block,
            own,
            pl.BlockSpec(shifts.shape, lambda i: (0, 0)),
            pl.BlockSpec(attn_map.shape, lambda i: (0, 0)),
        ],
        out_specs=[
            block,
            pl.BlockSpec((width, 3 * width), lambda i: (0, 0)),
            pl.BlockSpec((8, width), lambda i: (0, 0)),
        ],
        out_shape=[
            jax.ShapeDtypeStruct((row_count, width), jnp.bfloat16),
            jax.ShapeDtypeStruct((width, 3 * width), jnp.float32),
            jax.ShapeDtypeStruct((8, width), jnp.float32),
        ],
        scratch_shapes=[pltpu.VMEM((rows, width), jnp.float32)],
        cost_estimate=small_cost(),
        compiler_params=kernel_params(),
    )(dq, dk, dv, sums, attn_in, mid, shifts, attn_map)


def split_low(values):
    upper = values.astype(jnp.bfloat16)
    return upper, (values - upper.astype(jnp.float32)).astype(jnp.bfloat16)


def plain_dot(left, right):
    return jnp.dot(left, right, preferred_element_type=jnp.float32)


def triple_dot(left, right, dot=plain_dot):
    return dot(left[0], right[0]) + (dot(left[0], right[1]) + dot(left[1], right[0]))


def muon_kernel(
    scalar_row,
    choice_ref,
    square_ref,
    mom_ref,
    joint_ref,
    proj_ref,
    rest_ref,
    turned_ref,
    factor_ref,
    norm_ref,
    full_ref,
):
    matrix, pos = choice_ref[0], choice_ref[1]
    width = turned_ref.shape[1]
    coarse = joint_ref[:, pl.ds(0, 3 * width)].astype(jnp.float32)
    fine = joint_ref[:, pl.ds(3 * width, width)].astype(jnp.float32)
    fine = fine + joint_ref[:, pl.ds(4 * width, width)].astype(jnp.float32)
    in_norm = lax.broadcasted_iota(jnp.int32, fine.shape, 0) < scalar_row
    square = jnp.sum(jnp.where(in_norm, fine * fine, 0.0), axis=1, keepdims=True)
    square = square + jnp.sum(coarse * coarse, axis=1, keepdims=True)
    square = jnp.sum(square, axis=0, keepdims=True) + square_ref[0, 0]
    weight_total = fine[scalar_row : scalar_row + 1, 1:2]
    grad_norm = jnp.sqrt(square) / weight_total
    factor = jnp.minimum(1.0, clip_bound / (grad_norm + 1e-06)) / weight_total
    norm_ref[...] = grad_norm
    factor_ref[...] = factor
    own, width = turned_ref.shape
    gram = jnp.zeros((width, width), jnp.float32)
    for place in range(FF // width):
        part = pl.ds(place * width, width)
        if place < 3:
            first = joint_ref[:, part]
        else:
            first = proj_ref[...]
        grads = jnp.where(
            matrix == 0, first.astype(jnp.float32), rest_ref[part, :].astype(jnp.float32)
        )
        moment = muon_decay * mom_ref[0, part, :].astype(jnp.float32) + factor * grads
        full_ref[part, :] = moment
        halves = split_low(moment)
        gram = gram + triple_dot(halves, halves, contract_rows)
    row_ids = lax.broadcasted_iota(jnp.int32, gram.shape, 0)
    eye = jnp.where(row_ids == lax.broadcasted_iota(jnp.int32, gram.shape, 1), 1.0, 0.0)
    trace = jnp.sum(jnp.sum(gram * eye, axis=1, keepdims=True), axis=0, keepdims=True)
    scale = 1.0 / (jnp.sqrt(trace) + 1e-07)
    gram = gram * (scale * scale)
    turned = full_ref[pl.ds(pos * own, own), :] * scale
    for iteration in range(NS_ITERS):
        gram_halves = split_low(gram)
        poly = coef_a * eye + coef_b * gram + coef_c * triple_dot(gram_halves, gram_halves)
        poly_halves = split_low(poly)
        turned = triple_dot(split_low(turned), poly_halves)
        if iteration < NS_ITERS - 1:
            gram = triple_dot(poly_halves, split_low(triple_dot(poly_halves, gram_halves)))
    turned_ref[...] = turned.astype(jnp.bfloat16)


def turn_moment(matrix, pos, rest_square, scalar_row, mom_full, joint, sum_rest, own):
    rows, width = mom_full.shape[1:]
    single = pl.BlockSpec((1, 1), lambda i, choice: (0, 0))
    return pl.pallas_call(
        functools.partial(muon_kernel, scalar_row),
        grid_spec=pltpu.PrefetchScalarGridSpec(
            num_scalar_prefetch=1,
            grid=(1,),
            in_specs=[
                pl.BlockSpec(memory_space=pltpu.SMEM),
                pl.BlockSpec((1, rows, width), lambda i, choice: (choice[0], 0, 0)),
                pl.BlockSpec(joint.shape, lambda i, choice: (0, 0)),
                pl.BlockSpec((width, width), lambda i, choice: (2 * FF // width, 0)),
                pl.BlockSpec(
                    (rows, width), lambda i, choice: (jnp.maximum(choice[0] - 1, 0), 0)
                ),
            ],
            out_specs=[pl.BlockSpec((own, width), lambda i, choice: (0, 0)), single, single],
            scratch_shapes=[pltpu.VMEM((rows, width), jnp.float32)],
        ),
        out_shape=[
            jax.ShapeDtypeStruct((own, width), jnp.bfloat16),
            jax.ShapeDtypeStruct((1, 1), jnp.float32),
            jax.ShapeDtypeStruct((1, 1), jnp.float32),
        ],
        cost_estimate=small_cost(),
        compiler_params=kernel_params(),
    )(jnp.stack([matrix, pos]), rest_square.reshape(1, 1), mom_full, joint, sum_rest, sum_rest)


def share_turned(turned, moments):
    across = partner_swap(turned, "wide", 2)
    across, moments = lax.optimization_barrier((across, moments))
    beside = partner_swap(turned, "wide", 1)
    corner = partner_swap(across, "wide", 1)
    return (turned, beside, across, corner), moments


def moment_kernel(pos_ref, factor_ref, qkv_ref, proj_ref, up_ref, down_ref, *refs):
    own_refs, moment_refs = refs[:3], refs[3:]
    pos = pos_ref[0]
    factor = factor_ref[0, 0]
    own = own_refs[2].shape[0]
    proj_share = jnp.where(pos == FF // own - 1, 1.0, 0.0)
    first = jnp.where(
        proj_share > 0.5, proj_ref[...].astype(jnp.float32), qkv_ref[...].astype(jnp.float32)
    )
    moment_refs[0][...] = muon_decay * own_refs[0][...] + factor * first.T
    second = up_ref[...].astype(jnp.float32)
    moment_refs[1][...] = muon_decay * own_refs[1][...] + factor * second.T
    third = down_ref[...].astype(jnp.float32)
    moment_refs[2][...] = muon_decay * own_refs[2][...] + factor * third


def own_moments(pos, factor, sum_qkv, sum_rest, moms):
    own, width = moms[2].shape
    parts = FF // own
    whole = pl.BlockSpec((own, width), lambda i, pos: (0, 0))
    return pl.pallas_call(
        moment_kernel,
        grid_spec=pltpu.PrefetchScalarGridSpec(
            num_scalar_prefetch=1,
            grid=(1,),
            in_specs=[
                pl.BlockSpec(memory_space=pltpu.SMEM),
                pl.BlockSpec((width, width), lambda i, pos: (0, jnp.minimum(pos[0], 2))),
                pl.BlockSpec((width, width), lambda i, pos: (2 * FF // width, 0)),
                pl.BlockSpec((own, width), lambda i, pos: (pos[0], 0)),
                pl.BlockSpec((own, width), lambda i, pos: (parts + pos[0], 0)),
            ]
            + [whole] * 3,
            out_specs=[whole] * 3,
        ),
        out_shape=[jax.ShapeDtypeStruct((own, width), jnp.float32)] * 3,
        cost_estimate=small_cost(),
        compiler_params=kernel_params(),
    )(
        pos.reshape(1),
        factor.reshape(1, 1),
        sum_qkv,
        sum_rest,
        sum_rest,
        sum_rest,
        *moms,
    )


def step_kernel(group_ref, own_ref, beside_ref, across_ref, corner_ref, *refs):
    rates = [
        muon_rate * math.sqrt(max(1.0, LATENT_WIDTH / FF)),
        muon_rate * math.sqrt(max(1.0, LATENT_WIDTH / FF)),
        muon_rate * math.sqrt(max(1.0, FF / LATENT_WIDTH)),
    ]
    group = group_ref[0]
    low_side = group < 2
    even = group % 2 == 0
    own, beside, across, corner = [
        ref[...].astype(jnp.float32) for ref in (own_ref, beside_ref, across_ref, corner_ref)
    ]
    near, far = jnp.where(low_side, own, across), jnp.where(low_side, beside, corner)
    parts = [
        jnp.where(even, near, far),
        jnp.where(even, far, near),
        jnp.where(low_side, across, own),
    ]
    for place in range(3):
        change = parts[place] if place == 2 else parts[place].T
        new = refs[place][...] - rates[place] * change
        refs[6 + place][...] = new
        refs[9 + place][...] = ema_keep * refs[3 + place][...] + (1.0 - ema_keep) * new


def take_step(group, turned, weights, averages):
    whole = pl.BlockSpec(memory_space=pltpu.VMEM)
    return pl.pallas_call(
        step_kernel,
        in_specs=[pl.BlockSpec(memory_space=pltpu.SMEM)] + [whole] * 10,
        out_specs=[whole] * 6,
        out_shape=[jax.ShapeDtypeStruct(weights[0].shape, jnp.float32)] * 6,
        cost_estimate=small_cost(),
        compiler_params=kernel_params(),
    )(group.reshape(1), *turned, *weights, *averages)


def adam_update(weight, grad, first, second):
    first_new = beta_one * first + (1.0 - beta_one) * grad
    second_new = beta_two * second + (1.0 - beta_two) * grad * grad
    first_hat = first_new / (1.0 - beta_one**STEP_NUMBER)
    second_hat = second_new / (1.0 - beta_two**STEP_NUMBER)
    weight_new = weight - adam_rate * (
        first_hat / (jnp.sqrt(second_hat) + adam_eps) + decay_rate * weight
    )
    return (weight_new, first_new, second_new)


def on_device(
    prior_states,
    target,
    noise_draw,
    level_index,
    g2m_edges,
    neighbours,
    m2g_edges,
    valid_mask,
    channel_weights,
    w_embed,
    w_cond,
    w_attn,
    w_up,
    w_down,
    w_dec,
    biases,
    mom_attn,
    mom_up,
    mom_down,
    m_embed,
    v_embed,
    m_cond,
    v_cond,
    m_dec,
    v_dec,
    m_bias,
    v_bias,
    ema_embed,
    ema_cond,
    ema_attn,
    ema_up,
    ema_down,
    ema_dec,
    ema_bias,
):
    narrow_pos = lax.axis_index("narrow")
    narrow_count = lax.axis_size("narrow")
    pixel_local = valid_mask.shape[1]
    node_local = neighbours.shape[1]
    pixel_total = pixel_local * narrow_count
    node_total = node_local * narrow_count
    embed_low = w_embed.astype(jnp.bfloat16)
    dec_low = w_dec.astype(jnp.bfloat16)
    bias_embed = biases[:LATENT_WIDTH].reshape(1, LATENT_WIDTH)
    bias_up = biases[LATENT_WIDTH : LATENT_WIDTH + FF]
    bias_out = biases[LATENT_WIDTH + FF :]
    noise_level, scale_in, skip_scale, out_scale, loss_scale = sigma_terms(level_index[0])
    target_rows = target[0].astype(jnp.float32)
    noisy = target_rows + noise_level * noise_draw[0].astype(jnp.float32)
    features = jnp.concatenate(
        [prior_states[0, 0], prior_states[0, 1], (scale_in * noisy).astype(jnp.bfloat16)], axis=0
    )
    lat_weight = lat_weights(narrow_pos * pixel_local, pixel_local, pixel_total)
    pixel_weight = lat_weight * valid_mask[0].astype(jnp.float32)
    near_ids = (neighbours[0] - narrow_pos * node_local) % node_total
    m2g_ids = (m2g_edges[0] - narrow_pos * node_local) % node_total
    near_bias = count_bias(near_ids, node_total)
    m2g_counts = count_matrix(m2g_ids, node_total)

    feature_slots, node_sums = [], []

    def use_slot(features_here, source):
        node_sums.append(
            gather_sum(
                source * pixel_local,
                g2m_cols,
                features_here,
                embed_low,
                bias_embed,
                node_sums[-1] if node_sums else None,
            )
        )
        feature_slots.append((features_here, source))
        return node_sums[-1], near_bias

    piece_rows = LATENT_WIDTH // lax.axis_size("wide")
    piece_first = lax.axis_index("wide") * piece_rows
    def own_pieces(one, two, three):
        pieces = [
            lax.dynamic_slice_in_dim(part, piece_first, piece_rows, 1).T for part in (one, two)
        ] + [lax.dynamic_slice_in_dim(three, piece_first, piece_rows, 0)]
        return jnp.concatenate(pieces, axis=0).astype(jnp.bfloat16)

    g2m_own = g2m_edges[0].T
    id_rows = g2m_own.size // LATENT_WIDTH
    packed = jnp.concatenate(
        [
            (g2m_own // 128).reshape(id_rows, LATENT_WIDTH).astype(jnp.bfloat16),
            (g2m_own % 128).reshape(id_rows, LATENT_WIDTH).astype(jnp.bfloat16),
            own_pieces(w_attn, w_up, w_down),
        ],
        axis=0,
    )
    padded = [
        pad_rows(values)
        for values in (
            target[0],
            noise_draw[0],
            channel_weights.reshape(-1, 1),
            bias_out.reshape(-1, 1),
        )
    ]
    packed_slots, near_bias, padded = lax.optimization_barrier(
        (ring_slots(packed), near_bias, padded)
    )
    id_slots = [
        (
            slot[:id_rows].astype(jnp.float32) * 128.0
            + slot[id_rows : 2 * id_rows].astype(jnp.float32)
        )
        .astype(jnp.int32)
        .reshape(g2m_own.shape)
        for slot in packed_slots
    ]
    g2m_rows = jnp.concatenate(id_slots, axis=1)
    g2m_cols = g2m_rows.T
    weight_near = in_order([slot[2 * id_rows :] for slot in packed_slots])
    weight_all = lax.all_gather(weight_near, "wide", axis=0)
    weight_full = [
        weight_all[:, :, place].transpose(1, 0, 2, 3).reshape(-1, LATENT_WIDTH)
        for place in range(3)
    ]
    later = [() for _ in range(narrow_count)]
    later[narrow_count - 2] = own_pieces(mom_attn, mom_up, mom_down)
    later[max(narrow_count - 3, 0)] = weight_full
    line_slots(features, use_slot, later)
    mom_near = in_order(ring_slots(later[narrow_count - 2]))
    weight_full = later[max(narrow_count - 3, 0)]
    attn_rows, up_rows, down_full = weight_full[0], weight_full[1], weight_full[2]
    conditioning = cond_features(noise_level)
    modulation = jnp.dot(conditioning, w_cond, precision=highest_precision)
    gain_two = 1.0 + modulation[2 * LATENT_WIDTH : 3 * LATENT_WIDTH]
    shifts = modulation.reshape(4, LATENT_WIDTH) + jnp.array([[1.0], [0.0], [1.0], [0.0]])
    node_sum = node_sums[-1]
    proj_map = attn_rows[3 * LATENT_WIDTH :]
    attn_in, query_rows, pair_rows = project(node_sum, shifts, attn_rows, node_local)
    pair_rows, mom_near = lax.optimization_barrier((pair_rows, mom_near))
    mom_all = lax.all_gather(mom_near, "wide", axis=0)
    attended, mass = attend(query_rows, pair_rows, near_bias)
    attended_rows = attended.astype(jnp.bfloat16)
    node_mid = node_sum[:node_local] / G2M_K + contract_last(attended_rows, proj_map)
    normed_two, inverse_two = norm_stats(node_mid)
    mlp_in = (normed_two * gain_two + modulation[3 * LATENT_WIDTH :]).astype(jnp.bfloat16)
    up_pre = contract_last(mlp_in, up_rows) + bias_up
    hidden = jax.nn.silu(up_pre).astype(jnp.bfloat16)
    node_out = node_mid + jnp.dot(hidden, down_full, preferred_element_type=jnp.float32)
    node_low = node_out.astype(jnp.bfloat16)
    node_raw = lax.dot_general(
        dec_low, node_low, (((0,), (1,)), ((), ())), preferred_element_type=jnp.float32
    ).astype(jnp.bfloat16)
    node_raw, mom_all = lax.optimization_barrier((node_raw, mom_all))
    all_raw = jnp.concatenate(ring_slots(node_raw), axis=1)
    raw_spread, out_bias_sum, loss_sum_local = decode(
        jnp.stack([noise_level, skip_scale, out_scale, loss_scale]),
        m2g_counts,
        pad_rows(all_raw),
        padded[0],
        padded[1],
        pixel_weight.reshape(1, pixel_local),
        padded[2],
        padded[3],
    )
    loss_local = loss_sum_local[0, 0]
    grad_out_bias = out_bias_sum[: bias_out.shape[0], 0]
    raw_spread = raw_spread[: bias_out.shape[0]]
    raw_spread, mom_all = lax.optimization_barrier((raw_spread, mom_all))
    mom_full = mom_all.transpose(2, 1, 0, 3, 4).reshape(3, -1, LATENT_WIDTH)
    grad_node_raw, mom_full = ring_sum(
        [
            raw_spread[:, slot * node_local : (slot + 1) * node_local]
            for slot in range(narrow_count)
        ],
        mom_full,
    )
    grad_node_raw = grad_node_raw / M2G_K
    grad_dec = lax.dot_general(
        node_low.astype(jnp.float32),
        grad_node_raw,
        (((0,), (1,)), ((), ())),
        precision=highest_precision,
    )
    grad_node_out = lax.dot_general(
        grad_node_raw,
        dec_low.astype(jnp.float32),
        (((0,), (1,)), ((), ())),
        precision=highest_precision,
    )
    grad_mlp = grad_node_out.astype(jnp.bfloat16)
    grad_down = contract_rows(hidden, grad_mlp)
    grad_hidden = contract_last(grad_mlp, down_full)
    grad_up_pre = (grad_hidden * silu_slope(up_pre)).astype(jnp.bfloat16)
    grad_up_bias = jnp.sum(grad_up_pre.astype(jnp.float32), axis=0)
    grad_up = contract_rows(grad_up_pre, mlp_in)
    grad_mlp_in = plain_dot(grad_up_pre, up_rows)
    grad_node_mid = grad_node_out + norm_back(grad_mlp_in * gain_two, normed_two, inverse_two)
    grad_proj_out = grad_node_mid.astype(jnp.bfloat16)
    grad_proj = contract_rows(grad_proj_out, attended_rows)
    early = jnp.concatenate([grad_up, grad_down, grad_proj], axis=0).astype(jnp.bfloat16)
    gradient_attended = plain_dot(grad_proj_out, proj_map).astype(jnp.bfloat16)
    early, gradient_attended = lax.optimization_barrier((early, gradient_attended))
    early = lax.psum(early, ("wide", "narrow"))
    grad_query_rows, grad_key_rows, grad_value_rows = attend_back(
        query_rows, pair_rows, near_bias, mass, attended, gradient_attended
    )
    node_grads, grad_qkv, column_sums = project_back(
        grad_query_rows,
        grad_key_rows,
        grad_value_rows,
        node_sum,
        attn_in,
        grad_node_mid,
        shifts,
        attn_rows,
    )
    grad_modulation = jnp.concatenate(
        [
            column_sums[0],
            column_sums[1],
            jnp.sum(grad_mlp_in * normed_two, axis=0),
            jnp.sum(grad_mlp_in, axis=0),
        ]
    )
    grad_cond = conditioning[:, None] * grad_modulation[None, :]
    grad_embed = None
    grad_embed_bias = None
    for features_here, source in feature_slots:
        embed_part, bias_part = scatter_sum(
            source * pixel_local, g2m_rows, node_grads, features_here, embed_low, bias_embed
        )
        grad_embed = embed_part if grad_embed is None else grad_embed + embed_part
        grad_embed_bias = bias_part if grad_embed_bias is None else grad_embed_bias + bias_part
    width = LATENT_WIDTH
    channels = w_dec.shape[1]
    late_rows = jnp.concatenate(
        [
            grad_embed,
            grad_embed_bias.reshape(1, width),
            grad_up_bias.reshape(FF // width, width),
            jnp.pad(grad_out_bias, (0, width - channels)).reshape(1, width),
            grad_dec.T,
        ]
        + [grad_cond[:, place * width : (place + 1) * width] for place in range(4)]
        + [
            jnp.pad(
                jnp.concatenate([loss_local.reshape(1), jnp.sum(pixel_weight).reshape(1)]),
                (0, width - 2),
            ).reshape(1, width),
        ],
        axis=0,
    )
    scalar_row = late_rows.shape[0] - 1
    late_rows = jnp.pad(late_rows, ((0, width - late_rows.shape[0]), (0, 0)))
    late_rows, grad_qkv, early = lax.optimization_barrier((late_rows, grad_qkv, early))
    early_square = jnp.sum(jnp.square(early.astype(jnp.float32)))
    joint, early_square = joint_sum(grad_qkv, late_rows, (early_square,))
    _, late_rows = joint_split(joint, 3 * LATENT_WIDTH)
    embed_rows = w_embed.shape[0]
    sum_embed = late_rows[:embed_rows]
    place = embed_rows
    bias_rows = late_rows[place : place + 2 + FF // width].reshape(-1)
    sum_bias = bias_rows[: biases.shape[0]]
    loss_sum = late_rows[scalar_row, 0]
    weight_total = late_rows[scalar_row, 1]
    place += 2 + FF // width
    sum_dec = late_rows[place : place + channels].T
    place += channels
    sum_cond = jnp.concatenate(
        [late_rows[place + COND * part : place + COND * (part + 1)] for part in range(4)], axis=1
    )
    group = lax.axis_index("wide") % 4
    turned, factor, grad_norm = turn_moment(
        jnp.minimum(group, 2),
        narrow_pos,
        early_square,
        scalar_row,
        mom_full,
        joint,
        early,
        w_down.shape[0],
    )
    factor, grad_norm = factor[0, 0], grad_norm[0, 0]
    moments = own_moments(
        narrow_pos, factor, joint, early, (mom_attn, mom_up, mom_down)
    )
    turned, moments = share_turned(turned, moments)
    moment_attn, moment_up, moment_down = moments
    new_attn, new_up, new_down, average_attn, average_up, average_down = take_step(
        group, turned, (w_attn, w_up, w_down), (ema_attn, ema_up, ema_down)
    )
    new_embed, first_embed, second_embed = adam_update(
        w_embed, factor * sum_embed, m_embed, v_embed
    )
    new_cond, first_cond, second_cond = adam_update(w_cond, factor * sum_cond, m_cond, v_cond)
    new_dec, first_dec, second_dec = adam_update(w_dec, factor * sum_dec, m_dec, v_dec)
    new_bias, first_bias, second_bias = adam_update(biases, factor * sum_bias, m_bias, v_bias)
    keep_rest = 1.0 - ema_keep
    return (
        new_attn,
        new_up,
        new_down,
        moment_attn,
        moment_up,
        moment_down,
        new_embed,
        new_cond,
        new_dec,
        new_bias,
        first_embed,
        second_embed,
        first_cond,
        second_cond,
        first_dec,
        second_dec,
        first_bias,
        second_bias,
        ema_keep * ema_embed + keep_rest * new_embed,
        ema_keep * ema_cond + keep_rest * new_cond,
        average_attn,
        average_up,
        average_down,
        ema_keep * ema_dec + keep_rest * new_dec,
        ema_keep * ema_bias + keep_rest * new_bias,
        loss_sum,
        weight_total,
        grad_norm,
    )


def solution(mesh):
    in_specs = (
        P("wide", None, None, "narrow"),
        P("wide", None, "narrow"),
        P("wide", None, "narrow"),
        P("wide"),
        P("wide", "narrow", None),
        P("wide", "narrow", None),
        P("wide", "narrow", None),
        P("wide", "narrow"),
        P(),
        P(),
        P(),
        P(None, "narrow"),
        P(None, "narrow"),
        P("narrow", None),
        P(),
        P(),
        P(None, "narrow"),
        P(None, "narrow"),
        P("narrow", None),
        P(),
        P(),
        P(),
        P(),
        P(),
        P(),
        P(),
        P(),
        P(),
        P(),
        P(None, "narrow"),
        P(None, "narrow"),
        P("narrow", None),
        P(),
        P(),
    )
    out_specs = (
        P(None, "narrow"),
        P(None, "narrow"),
        P("narrow", None),
        P(None, "narrow"),
        P(None, "narrow"),
        P("narrow", None),
        P(),
        P(),
        P(),
        P(),
        P(),
        P(),
        P(),
        P(),
        P(),
        P(),
        P(),
        P(),
        P(),
        P(),
        P(None, "narrow"),
        P(None, "narrow"),
        P("narrow", None),
        P(),
        P(),
        P(),
        P(),
        P(),
    )
    return jax.shard_map(
        on_device, mesh=mesh, in_specs=in_specs, out_specs=out_specs, check_vma=False
    )
```
